32 devices in a mesh: rep: 4 (over x, core), shard: 8 (over z, y).
Axes of the slice: x: 2, y: 2, z: 4, core: 2. Of those that a mesh axis runs over, the one named last changes fastest.
Arguments:
- latents: bfloat16 [128, 16, 256], P(('rep', 'shard')), may hold values from -6 to 6
- target_noise: bfloat16 [128, 16, 256], P(('rep', 'shard')), may hold values from -6 to 6
- labels: int32 [128], P(('rep', 'shard')), may hold values from 0 to 15
- timesteps: int32 [128], P(('rep', 'shard')), may hold values from 0 to 999
- loss_weight: int32 [128], P(('rep', 'shard')), may hold values from 0 to 6, as said below
- layer_mats: float32 [2, 512, 4096], P(None, 'shard'), may hold values from -0.53033009 to 0.53033009
- layer_mats_first: float32 [2, 512, 4096], P(None, 'shard'), may hold values from -0.0024414062 to 0.0024414062
- layer_mats_second: float32 [2, 512, 4096], P(None, 'shard'), may hold values from 5.2083333e-09 to 8.333333e-08
- down_mats: float32 [2, 2048, 512], P(None, 'shard'), may hold values from -0.125 to 0.125
- down_first: float32 [2, 2048, 512], P(None, 'shard'), may hold values from -0.0024414062 to 0.0024414062
- down_second: float32 [2, 2048, 512], P(None, 'shard'), may hold values from 5.2083333e-09 to 8.333333e-08
- skip_mat: float32 [1024, 512], P('shard'), may hold values from -0.1875 to 0.1875
- skip_first: float32 [1024, 512], P('shard'), may hold values from -0.0024414062 to 0.0024414062
- skip_second: float32 [1024, 512], P('shard'), may hold values from 5.2083333e-09 to 8.333333e-08
- tables: float32 [306, 512], P(None, 'shard'), may hold values from -2 to 2
- tables_first: float32 [306, 512], P(None, 'shard'), may hold values from -0.0024414062 to 0.0024414062
- tables_second: float32 [306, 512], P(None, 'shard'), may hold values from 5.2083333e-09 to 8.333333e-08
- vectors: float32 [24, 512], P(None, 'shard'), may hold values from -1.2 to 1.3
- vectors_first: float32 [24, 512], P(None, 'shard'), may hold values from -0.0024414062 to 0.0024414062
- vectors_second: float32 [24, 512], P(None, 'shard'), may hold values from 5.2083333e-09 to 8.333333e-08
Outputs:
- loss_sum: float32 [], replicated
- weight_total: float32 [], replicated
- new_layer_first: float32 [2, 512, 4096], P(None, 'shard')
- new_layer_second: float32 [2, 512, 4096], P(None, 'shard')
- new_layer_mats: float32 [2, 512, 4096], P(None, 'shard')
- low_layer_mats: bfloat16 [2, 512, 4096], P(None, 'shard')
- new_down_first: float32 [2, 2048, 512], P(None, 'shard')
- new_down_second: float32 [2, 2048, 512], P(None, 'shard')
- new_down_mats: float32 [2, 2048, 512], P(None, 'shard')
- low_down_mats: bfloat16 [2, 2048, 512], P(None, 'shard')
- new_skip_first: float32 [1024, 512], P('shard')
- new_skip_second: float32 [1024, 512], P('shard')
- new_skip_mat: float32 [1024, 512], P('shard')
- low_skip_mat: bfloat16 [1024, 512], P('shard')
- new_tables_first: float32 [306, 512], P(None, 'shard')
- new_tables_second: float32 [306, 512], P(None, 'shard')
- new_tables: float32 [306, 512], P(None, 'shard')
- low_tables: bfloat16 [306, 512], P(None, 'shard')
- new_vectors_first: float32 [24, 512], P(None, 'shard')
- new_vectors_second: float32 [24, 512], P(None, 'shard')
- new_vectors: float32 [24, 512], P(None, 'shard')
- low_vectors: bfloat16 [24, 512], P(None, 'shard')
The draws below stay inside these ranges and needn't reach their ends.
Inputs may be any that keep to these rules, and one draw needn't show every extreme that they name: `loss_weight`: zero marks a dummy sequence; some sequence has weight 6 in every draw.
All inputs are finite; a program needn't handle non-finite values.
Results may differ from the reference program's by a relative error of at most 0.018.
The reference program's roundings to bfloat16 on the way count: a program that leaves them out, or rounds other values in their place, can miss the bound.
Values may be sent and summed in bfloat16 or wider, within the bound.
No kernel may reach another device: no remote copies, remote signals or barrier semaphores. Data moves between devices by JAX's collectives and lax.ppermute only.
A program may use at most 256 MiB of HBM per device.

```python
import math
import jax
import jax.numpy as jnp
from jax import lax

D = 512
HEADS = 8
HD = 64
FF = 2048
CH = 16
NP = 256
CLASSES = 16
LAYERS = 2
STEP = 10
SEQ_DEV = 4
SEQS = 128
SEQ_LEN = 258
WIDE = 4096
NT = 306
NV = 24
N_REP = 4
N_SHARD = 8


def rough_values(draw_key, shape):
    values_raw = jax.random.normal(draw_key, shape, jnp.float32)
    return jnp.clip(values_raw, -4.0, 4.0)


def draw_layer_mats(key, part):
    key = jax.random.fold_in(key, 11)
    columns = jnp.arange(WIDE)
    column_scale = jnp.where((columns >= 3 * D) & (columns < 4 * D), 3.0, 1.0) * D ** (-0.5)
    return rough_values(key, (LAYERS, D, WIDE)) * column_scale[None, None, :]


def draw_tables(key, part):
    key = jax.random.fold_in(key, 13)
    row_ids = jnp.arange(NT)
    row_scale = jnp.where(row_ids < CH, 0.25, jnp.where(row_ids < NT - CH, 0.5, D ** (-0.5)))
    return rough_values(key, (NT, D)) * row_scale[:, None]


def draw_vectors(key, part):
    key = jax.random.fold_in(key, 15)
    key_gain, key_bias = jax.random.split(key)
    per_layer = 6 + FF // D
    row_ids = jnp.arange(NV)
    within = row_ids % per_layer
    is_gain = (row_ids < LAYERS * per_layer) & ((within == 0) | (within == 2)) | (row_ids == LAYERS * per_layer)
    gains = 1.0 + jax.random.uniform(key_gain, (NV, D), jnp.float32, -0.3, 0.3)
    biases = 0.3 * rough_values(key_bias, (NV, D))
    return jnp.where(is_gain[:, None], gains, biases)


def draw_loss_weight(key, part):
    key = jax.random.fold_in(key, 17)
    key_extra, key_drop = jax.random.split(key)
    seq_ids = jnp.arange(SEQS)
    device_id = seq_ids // SEQ_DEV
    rep_id = device_id // N_SHARD
    shard_id = device_id % N_SHARD
    base_rows = 1 + 2 * rep_id // max(N_REP - 1, 1) + 2 * shard_id // max(N_SHARD - 1, 1)
    extra_rows = jax.random.randint(key_extra, (SEQS,), 0, 2)
    dropped = jax.random.randint(key_drop, (SEQS,), 0, 16) == 0
    result = jnp.where(dropped, 0, base_rows + extra_rows)
    result = result.at[0].set(0).at[SEQS // 2].set(0).at[SEQS - 1].set(6)
    return result.astype(jnp.int32)


def set_ends(entries, key, low, largest):
    place = [jax.random.randint(jax.random.fold_in(key, axis), (), 0, length) for axis, length in enumerate(entries.shape)]
    main_axis = entries.shape.index(max(entries.shape))
    next_to = place[:main_axis] + [(place[main_axis] + 1) % entries.shape[main_axis]] + place[main_axis + 1:]
    return entries.at[tuple(place)].set(low).at[tuple(next_to)].set(largest)


def shard_levels(own_key, shape, cuts, low, high):
    def one(position, parts):
        steps = jax.random.uniform(jax.random.fold_in(jax.random.fold_in(own_key, 6), position), (parts,), jnp.float32, low / len(cuts), high / len(cuts))
        return jnp.repeat(jnp.exp(steps), shape[position] // parts).reshape((-1,) + (1,) * (len(shape) - position - 1))

    level = one(*cuts[0])
    for cut in cuts[1:]:
        level = level * one(*cut)
    return level


def gaussian(own_key, shape, scale, most, pieces=(), kind=jnp.bfloat16):
    factor_of = shard_levels(own_key, shape, pieces, -0.22, 0.18) if pieces else 1.0
    entries = jax.random.normal(own_key, shape, jnp.float32) * scale * factor_of
    return jnp.minimum(jnp.maximum(entries, -most), most).astype(kind)


def setup_inputs(seed: int = 0) -> dict:
    seeds = jax.random.split(jax.random.key(seed), 21)
    return {
        "latents": gaussian(seeds[0], (SEQS, CH, NP), 1.0, 6.0, ((0, 32),)),
        "target_noise": gaussian(seeds[1], (SEQS, CH, NP), 1.0, 6.0, ((0, 32),)),
        "labels": set_ends(jax.random.randint(seeds[2], (SEQS,), 0, CLASSES), jax.random.fold_in(seeds[2], 1), 0, CLASSES - 1).astype(jnp.int32),
        "timesteps": set_ends(jax.random.randint(seeds[3], (SEQS,), 0, 1000), jax.random.fold_in(seeds[3], 1), 0, 999).astype(jnp.int32),
        "loss_weight": draw_loss_weight(jax.random.fold_in(seeds[20], 71), 0),
        "layer_mats": draw_layer_mats(jax.random.fold_in(seeds[20], 71), 0),
        "layer_mats_first": gaussian(seeds[6], (LAYERS, D, WIDE), (0.002 * SEQS ** -0.5), 0.0024414062, ((1, 8),), jnp.float32),
        "layer_mats_second": jnp.clip(jnp.exp(math.log(8.333333312293689e-08) - 2.7725887 * jax.random.uniform(seeds[7], (LAYERS, D, WIDE), jnp.float32) ** shard_levels(seeds[7], (LAYERS, D, WIDE), ((1, 8),), -0.2, 0.2)), 5.208333320183556e-09, 8.333333312293689e-08),
        "down_mats": gaussian(seeds[8], (LAYERS, FF, D), FF ** -0.5, 0.125, ((1, 8),), jnp.float32),
        "down_first": gaussian(seeds[9], (LAYERS, FF, D), (0.002 * SEQS ** -0.5), 0.0024414062, ((1, 8),), jnp.float32),
        "down_second": jnp.clip(jnp.exp(math.log(8.333333312293689e-08) - 2.7725887 * jax.random.uniform(seeds[10], (LAYERS, FF, D), jnp.float32) ** shard_levels(seeds[10], (LAYERS, FF, D), ((1, 8),), -0.2, 0.2)), 5.208333320183556e-09, 8.333333312293689e-08),
        "skip_mat": gaussian(seeds[11], (2 * D, D), (2 * D) ** -0.5, 0.1875, ((0, 8),), jnp.float32),
        "skip_first": gaussian(seeds[12], (2 * D, D), (0.002 * SEQS ** -0.5), 0.0024414062, ((0, 8),), jnp.float32),
        "skip_second": jnp.clip(jnp.exp(math.log(8.333333312293689e-08) - 2.7725887 * jax.random.uniform(seeds[13], (2 * D, D), jnp.float32) ** shard_levels(seeds[13], (2 * D, D), ((0, 8),), -0.2, 0.2)), 5.208333320183556e-09, 8.333333312293689e-08),
        "tables": draw_tables(jax.random.fold_in(seeds[20], 71), 0),
        "tables_first": gaussian(seeds[15], (NT, D), (0.002 * SEQS ** -0.5), 0.0024414062, ((1, 8),), jnp.float32),
        "tables_second": jnp.clip(jnp.exp(math.log(8.333333312293689e-08) - 2.7725887 * jax.random.uniform(seeds[16], (NT, D), jnp.float32) ** shard_levels(seeds[16], (NT, D), ((1, 8),), -0.2, 0.2)), 5.208333320183556e-09, 8.333333312293689e-08),
        "vectors": draw_vectors(jax.random.fold_in(seeds[20], 71), 0),
        "vectors_first": gaussian(seeds[18], (NV, D), (0.002 * SEQS ** -0.5), 0.0024414062, ((1, 8),), jnp.float32),
        "vectors_second": jnp.clip(jnp.exp(math.log(8.333333312293689e-08) - 2.7725887 * jax.random.uniform(seeds[19], (NV, D), jnp.float32) ** shard_levels(seeds[19], (NV, D), ((1, 8),), -0.2, 0.2)), 5.208333320183556e-09, 8.333333312293689e-08),
    }


@jax.custom_vjp
def low(v):
    return lax.optimization_barrier(v.astype(jnp.bfloat16)).astype(jnp.float32)

@jax.custom_vjp
def low_back(v):
    return v

def low_keep(v):
    return (low(v), None)

def low_pass(kept, grad):
    return (grad,)

def back_keep(v):
    return (v, None)

def back_low(kept, grad):
    return (low(grad),)
low.defvjp(low_keep, low_pass)
low_back.defvjp(back_keep, back_low)
HIGHEST_PREC = lax.Precision.HIGHEST
beta_one = 0.5
beta_two = 0.75
epsilon = 1e-08
weight_decay = 0.05
step_rates = (0.05, 0.03, 0.03, 0.05, 0.3)

def matmul_high(left, right):
    return jnp.matmul(left, right, precision=HIGHEST_PREC)

def layer_norm(stream, gain, shift):
    center = lax.optimization_barrier(jnp.mean(stream, -1, keepdims=True))
    offset = stream - center
    spread = lax.optimization_barrier(jnp.mean(offset * offset, -1, keepdims=True))
    return offset * lax.rsqrt(spread + 1e-05) * gain + shift

def time_token(timesteps):
    half_width = D // 2
    freqs_row = jnp.exp(-math.log(10000.0) * jnp.arange(half_width, dtype=jnp.float32) / half_width)
    angles = timesteps.astype(jnp.float32)[:, None] * freqs_row[None, :]
    return jnp.concatenate([jnp.cos(angles), jnp.sin(angles)], -1)

def layer_vectors(vectors, layer_id):
    per_layer = 6 + FF // D
    start = layer_id * per_layer
    return (vectors[start:start + 6], vectors[start + 6:start + per_layer].reshape(FF))

def block_forward(stream, matrix, down_mat, layer_vec, fc1_bias):
    batch_seqs = stream.shape[0]
    normed = low(layer_norm(stream, layer_vec[0], layer_vec[1]))
    packed = low(low_back(matmul_high(normed, matrix[:, :3 * D])))
    packed = packed.reshape(batch_seqs, SEQ_LEN, 3, HEADS, HD)
    scores = jnp.einsum('bqhe,bkhe->bhqk', packed[:, :, 0], packed[:, :, 1], precision=HIGHEST_PREC)
    scores = low_back(scores * HD ** (-0.5))
    attend_w = low(jax.nn.softmax(scores, axis=-1))
    attended = jnp.einsum('bhqk,bkhe->bqhe', attend_w, packed[:, :, 2], precision=HIGHEST_PREC)
    attended = low(low_back(attended.reshape(batch_seqs, SEQ_LEN, D)))
    middle = stream + low_back(matmul_high(attended, matrix[:, 3 * D:4 * D])) + layer_vec[4]
    normed_two = low(layer_norm(middle, layer_vec[2], layer_vec[3]))
    hidden_act = low(jax.nn.gelu(low_back(matmul_high(normed_two, matrix[:, 4 * D:])) + fc1_bias))
    return middle + low_back(matmul_high(hidden_act, down_mat)) + layer_vec[5]

def group_loss(params, batch):
    layer_mats, down_mats, skip_mat, tables, vectors = params
    latents, target_noise, labels, timesteps, seq_weight = batch
    tail_rows = vectors[LAYERS * (6 + FF // D):]
    patch_rows = low_back(jnp.einsum('bcp,cd->bpd', latents, tables[:CH], precision=HIGHEST_PREC)) + tail_rows[3]
    class_rows = tables[CH:CH + CLASSES][labels]
    stream = jnp.concatenate([time_token(timesteps)[:, None], class_rows[:, None], patch_rows], 1)
    stream = stream + tables[CH + CLASSES:CH + CLASSES + SEQ_LEN]
    embedded = stream
    for layer_id in range(LAYERS):
        if layer_id == LAYERS // 2:
            joined = low(jnp.concatenate([stream, embedded], -1))
            stream = low_back(matmul_high(joined, skip_mat)) + tail_rows[2]
        layer_vec, fc1_bias = layer_vectors(vectors, layer_id)
        stream = block_forward(stream, layer_mats[layer_id], down_mats[layer_id], layer_vec, fc1_bias)
    final_norm = low(layer_norm(stream[:, 2:], tail_rows[0], tail_rows[1]))
    head_rows = tables[CH + CLASSES + SEQ_LEN:]
    prediction = low_back(jnp.einsum('cd,bpd->bcp', head_rows, final_norm, precision=HIGHEST_PREC))
    errors = prediction - target_noise
    per_seq = lax.optimization_barrier(jnp.mean(errors * errors, axis=(1, 2)))
    return jnp.sum(seq_weight * per_seq)

def adam_update(weight, grad, moment_one, moment_two, step_rate):
    moment_one = beta_one * moment_one + (1.0 - beta_one) * grad
    moment_two = beta_two * moment_two + (1.0 - beta_two) * grad * grad
    first_hat = moment_one / (1.0 - beta_one ** STEP)
    second_hat = moment_two / (1.0 - beta_two ** STEP)
    weight = weight - step_rate * (first_hat / (jnp.sqrt(second_hat) + epsilon) + weight_decay * weight)
    return (moment_one, moment_two, weight, weight.astype(jnp.bfloat16))

def reference(latents, target_noise, labels, timesteps, loss_weight, layer_mats, layer_mats_first, layer_mats_second, down_mats, down_first, down_second, skip_mat, skip_first, skip_second, tables, tables_first, tables_second, vectors, vectors_first, vectors_second):
    masters = (layer_mats, down_mats, skip_mat, tables, vectors)
    params = tuple((master.astype(jnp.bfloat16).astype(jnp.float32) for master in masters))
    group_size = math.gcd(SEQS, 16)
    group_count = SEQS // group_size
    seq_weight = loss_weight.astype(jnp.float32)
    batch = (latents.astype(jnp.float32).reshape(group_count, group_size, CH, NP), target_noise.astype(jnp.float32).reshape(group_count, group_size, CH, NP), labels.reshape(group_count, group_size), timesteps.reshape(group_count, group_size), seq_weight.reshape(group_count, group_size))
    checked = jax.checkpoint(group_loss)

    def total_loss(weights_in):

        def add_group(carry, item_batch):
            return (carry + checked(weights_in, item_batch), None)
        summed, _ = lax.scan(add_group, jnp.zeros((), jnp.float32), batch)
        return summed
    loss_sum, pull_back = jax.vjp(total_loss, params)
    weight_total = jnp.sum(seq_weight)
    inverse = 1.0 / weight_total
    grads = pull_back(inverse)[0]
    firsts = (layer_mats_first, down_first, skip_first, tables_first, vectors_first)
    seconds = (layer_mats_second, down_second, skip_second, tables_second, vectors_second)
    results = [adam_update(masters[index], grads[index], firsts[index], seconds[index], step_rates[index]) for index in range(5)]
    return (loss_sum, weight_total, results[0][0], results[0][1], results[0][2], results[0][3], results[1][0], results[1][1], results[1][2], results[1][3], results[2][0], results[2][1], results[2][2], results[2][3], results[3][0], results[3][1], results[3][2], results[3][3], results[4][0], results[4][1], results[4][2], results[4][3])
```

```python
import functools
import math

import jax
import jax.numpy as jnp
from jax import lax
from jax.experimental import pallas as pl
from jax.experimental.pallas import tpu as pltpu
from jax.sharding import PartitionSpec as P

D = 512
HEADS = 8
HD = 64
FF = 2048
CH = 16
NP = 256
CLASSES = 16
LAYERS = 2
STEP = 10
SEQ_LEN = 258

beta_one = 0.5
beta_two = 0.75
epsilon = 1e-08
weight_decay = 0.05
step_rates = (0.05, 0.03, 0.03, 0.05, 0.3)

TAIL = 16
T = NP + TAIL
ROW_PATCH = T
ROW_CLASS = ROW_PATCH + CH
ROW_HEAD = ROW_CLASS + CLASSES
ROW_VEC = ROW_HEAD + CH
N_VEC = LAYERS * (6 + FF // D) + 4
ROWS = D
ROW_WEIGHT = ROWS - 1
ROW_LOSS = 384
bf16 = jnp.bfloat16
f32 = jnp.float32
ALL = ("rep", "shard")
VMEM = pltpu.CompilerParams(vmem_limit_bytes=56 * 1024 * 1024)
ANY = pl.BlockSpec(memory_space=pl.ANY)
SMEM = pl.BlockSpec(memory_space=pltpu.SMEM)
WHOLE = pl.BlockSpec(memory_space=pltpu.VMEM)


class Part:
    def __init__(self, body, inputs, in_specs, outs, out_specs, scratch=()):
        self.body, self.inputs, self.in_specs = body, list(inputs), list(in_specs)
        self.outs, self.out_specs, self.scratch = list(outs), list(out_specs), list(scratch)


class Order:
    def __init__(self):
        self.last = None

    def __call__(self, kernel, inputs, in_specs, outs, out_specs, scratch=(), grid=(1,), name=None, aliases=None):
        part = Part(kernel, inputs, in_specs, outs, out_specs, scratch)
        return self.fuse([part], name, grid=grid, aliases=aliases)[0]

    def fuse(self, parts, name, after=(), grid=(1,), aliases=None):
        extra = list(after) + ([] if self.last is None else [self.last])
        inputs = [value for part in parts for value in part.inputs]
        counts = [(len(p.inputs), len(p.outs), len(p.scratch)) for p in parts]
        ends = [sum(c[i] for c in counts) for i in range(3)]
        skip = len(extra)

        def body(*refs):
            groups = (refs[: ends[0]], refs[ends[0] + skip : ends[0] + skip + ends[1]], refs[ends[0] + skip + ends[1] :])
            at = [0, 0, 0]
            rest = []
            for part, count in zip(parts, counts):
                own = [r for i in range(3) for r in groups[i][at[i] : at[i] + count[i]]]
                at = [i + n for i, n in zip(at, count)]
                more = part.body(*own)
                if more is not None:
                    next(more)
                    rest.append(more)
            for more in rest:
                next(more, None)

        result = pl.pallas_call(
            body,
            grid=grid,
            in_specs=[spec for part in parts for spec in part.in_specs] + [ANY] * skip,
            out_specs=[spec for part in parts for spec in part.out_specs],
            out_shape=[out for part in parts for out in part.outs],
            scratch_shapes=[item for part in parts for item in part.scratch],
            input_output_aliases=aliases or {},
            cost_estimate=pl.CostEstimate(flops=50_000_000_000, bytes_accessed=100_000_000, transcendentals=0),
            compiler_params=VMEM,
            name=name,
        )(*inputs, *extra)
        self.last = result[0]
        split, at = [], 0
        for part in parts:
            split.append(result[at : at + len(part.outs)])
            at += len(part.outs)
        return split


def dot(left, right):
    return jnp.dot(left, right, preferred_element_type=f32)


def dot_t(left, right):
    return lax.dot_general(left, right, (((1,), (1,)), ((), ())), preferred_element_type=f32)


def t_dot(left, right):
    return lax.dot_general(left, right, (((0,), (0,)), ((), ())), preferred_element_type=f32)


def norm_hat(stream):
    center = jnp.mean(stream, -1, keepdims=True)
    offset = stream - center
    spread = jnp.mean(offset * offset, -1, keepdims=True)
    inverse = lax.rsqrt(spread + 1e-05)
    return (offset * inverse, inverse)


def norm_back(hat, inverse, gain, grad):
    scaled = grad * gain
    first = jnp.mean(scaled, -1, keepdims=True)
    second = jnp.mean(scaled * hat, -1, keepdims=True)
    return inverse * (scaled - first - hat * second)


def rows_sum(values):
    return jnp.sum(values, 0, keepdims=True)


LSE = 16


def apart(rows, scale):
    lane = lax.broadcasted_iota(jnp.int32, (1, 2 * HD), 1)
    return jnp.concatenate([rows * jnp.where(lane // HD == e, scale, 0.0).astype(bf16) for e in range(2)], 0)


def block_mask():
    row = lax.broadcasted_iota(jnp.int32, (TAIL, D), 0)
    lane = lax.broadcasted_iota(jnp.int32, (TAIL, D), 1)
    return (row // 2 == lane // HD, row % 2 == 0)


def spread_tail(rows, scale):
    own, first = block_mask()
    wide = rows.astype(f32)
    both = jnp.where(first, wide[0:1], wide[1:2]) * scale
    return jnp.where(own, both, 0.0).astype(bf16)


def gather_tail(values):
    own, first = block_mask()
    kept = jnp.where(own, values, 0.0)
    zero = rows_sum(jnp.where(first, kept, 0.0))
    one = rows_sum(jnp.where(first, 0.0, kept))
    row = lax.broadcasted_iota(jnp.int32, (TAIL, D), 0)
    return jnp.where(row == 0, zero, jnp.where(row == 1, one, 0.0))


def mask_keys(scores):
    tail = scores[NP:]
    row = lax.broadcasted_iota(jnp.int32, tail.shape, 0)
    return jnp.concatenate([scores[:NP], jnp.where(row < SEQ_LEN - NP, tail, -1e30)], 0)


def softmax_rows(scores):
    top = jnp.max(scores, 0, keepdims=True)
    expon = jnp.exp(scores - top)
    total = jnp.sum(expon, 0, keepdims=True)
    return (expon * (1.0 / total)).astype(bf16), top + jnp.log(total)


def pipelined(count, *stages):
    held = {}
    for step in range(count + len(stages) - 1):
        for i, stage in enumerate(stages):
            if 0 <= step - i < count:
                held[step - i] = stage(step - i, held.get(step - i))


def attention_forward(stream, layer_id, vec_ref, wa_ref, h_ref, qkv_ref, lse_ref, o_ref, mid_ref):
    base = layer_id * (6 + FF // D)
    hat, _ = norm_hat(stream)
    normed = (hat * vec_ref[base : base + 1] + vec_ref[base + 1 : base + 2]).astype(bf16)
    h_ref[0] = normed
    qkv_ref[0] = dot(normed, wa_ref[:, : 3 * D]).astype(bf16)
    scale = HD**-0.5

    def cut(part, pair):
        return qkv_ref[0, :, part * D + 128 * pair : part * D + 128 * pair + 128]

    def score(pair, _):
        return dot_t(cut(1, pair), apart(cut(0, pair)[:NP], scale))

    def weigh(pair, scores):
        weights, log_total = softmax_rows(mask_keys(scores))
        lse_ref[0, 2 * pair : 2 * pair + 1] = log_total[:, :NP]
        lse_ref[0, 2 * pair + 1 : 2 * pair + 2] = log_total[:, NP:]
        return weights

    def mix(pair, weights):
        values = apart(cut(2, pair), 1.0)
        out = t_dot(weights[:, :NP], values[:T]) + t_dot(weights[:, NP:], values[T:])
        o_ref[0, :NP, 128 * pair : 128 * pair + 128] = out.astype(bf16)

    tails = spread_tail(qkv_ref[0, NP:, :D], scale)
    weights, log_total = softmax_rows(mask_keys(dot_t(qkv_ref[0, :, D : 2 * D], tails)))
    lse_ref[0, HEADS : HEADS + 1, :TAIL] = log_total
    o_ref[0, NP:] = gather_tail(t_dot(weights, qkv_ref[0, :, 2 * D :])).astype(bf16)
    pipelined(HEADS // 2, score, weigh, mix)
    mid_ref[0] = stream + dot(o_ref[0], wa_ref[:, 3 * D :]) + vec_ref[base + 4 : base + 5]


def embed_attention_kernel(
    label_ref, latent_ref, time_ref, tab_ref, vec_ref, wa_ref, x_ref, h_ref, qkv_ref, lse_ref, o_ref, mid_ref
):
    b = pl.program_id(0)
    patch_rows = t_dot(latent_ref[0], tab_ref[ROW_PATCH:ROW_CLASS]) + vec_ref[N_VEC - 1 : N_VEC]
    row = lax.broadcasted_iota(jnp.int32, (TAIL, CLASSES), 0)
    column = lax.broadcasted_iota(jnp.int32, (TAIL, CLASSES), 1)
    choose = jnp.where((row == 1) & (column == label_ref[b]), 1.0, 0.0).astype(bf16)
    tail_rows = time_ref[0] + dot(choose, tab_ref[ROW_CLASS:ROW_HEAD])
    stream = jnp.concatenate([patch_rows, tail_rows], 0) + tab_ref[:T].astype(f32)
    x_ref[0] = stream
    attention_forward(stream, 0, vec_ref, wa_ref, h_ref, qkv_ref, lse_ref, o_ref, mid_ref)


def skip_attention_kernel(x1_ref, x0_ref, ws_ref, vec_ref, wa_ref, x_ref, h_ref, qkv_ref, lse_ref, o_ref, mid_ref):
    one = x1_ref[0].astype(bf16)
    zero = x0_ref[0].astype(bf16)
    halves = [dot(one, ws_ref[i, :D]) + dot(zero, ws_ref[i, D:]) for i in range(2)]
    stream = jnp.concatenate(halves, 1) + vec_ref[N_VEC - 2 : N_VEC - 1]
    x_ref[0] = stream
    attention_forward(stream, 1, vec_ref, wa_ref, h_ref, qkv_ref, lse_ref, o_ref, mid_ref)


def mlp_forward(layer_id, mid_ref, vec_ref, w1_ref, w2_ref, h_ref, act_ref, slope_ref):
    base = layer_id * (6 + FF // D)
    hat, _ = norm_hat(mid_ref[...])
    normed = (hat * vec_ref[base + 2 : base + 3] + vec_ref[base + 3 : base + 4]).astype(bf16)
    h_ref[...] = normed
    const = math.sqrt(2.0 / math.pi)

    for j in range(FF // D):
        cols = slice(D * j, D * j + D)
        pre = dot(normed, w1_ref[:, cols]) + vec_ref[base + 6 + j : base + 7 + j]
        square = pre * pre
        half = 0.5 + 0.5 * jnp.tanh(pre * (const + (const * 0.044715) * square))
        act = pre * half
        act_ref[:, cols] = act.astype(bf16)
        slope = half + act * (1.0 - half) * (2.0 * const + (6.0 * const * 0.044715) * square)
        slope_ref[:, cols] = slope.astype(bf16)
    total = jnp.concatenate([dot(act_ref[...], w2_ref[i]) for i in range(2)], 1)
    return mid_ref[...] + total + vec_ref[base + 5 : base + 6]


def mlp_kernel(layer_id, mid_ref, vec_ref, w1_ref, w2_ref, h_ref, act_ref, slope_ref, out_ref):
    out_ref[...] = mlp_forward(layer_id, mid_ref, vec_ref, w1_ref, w2_ref, h_ref, act_ref, slope_ref)


def mlp_head_kernel(
    total_ref,
    weight_ref,
    mid_ref,
    vec_ref,
    w1_ref,
    w2_ref,
    noise_ref,
    tab_ref,
    h_ref,
    act_ref,
    slope_ref,
    dx_ref,
    dhead_ref,
    small_ref,
):
    b = pl.program_id(0)

    @pl.when(b == 0)
    def _():
        dhead_ref[...] = jnp.zeros_like(dhead_ref)
        small_ref[...] = jnp.zeros_like(small_ref)

    out = mlp_forward(1, mid_ref, vec_ref, w1_ref, w2_ref, h_ref, act_ref, slope_ref)
    hat, inverse = norm_hat(out[:NP])
    gain = vec_ref[N_VEC - 4 : N_VEC - 3]
    final = (hat * gain + vec_ref[N_VEC - 3 : N_VEC - 2]).astype(bf16)
    head = tab_ref[ROW_HEAD:ROW_VEC]
    errors = dot_t(head, final) - noise_ref[0].astype(f32)
    per_seq = jnp.sum(errors * errors) * (1.0 / (CH * NP))
    weight = weight_ref[b].astype(f32)
    scale = (jnp.ones((1, 1), f32) / total_ref[0, 0]) * weight * (2.0 / (CH * NP))
    grad_pred = (scale * errors).astype(bf16)
    dhead_ref[...] += dot(grad_pred, final)
    grad = t_dot(grad_pred, head)
    small_ref[0:1] += rows_sum(grad * hat)
    small_ref[1:2] += rows_sum(grad)
    small_ref[2:3] += jnp.full((1, D), weight * per_seq, f32)
    dx_ref[:NP] = norm_back(hat, inverse, gain, grad)
    dx_ref[NP:] = jnp.zeros((TAIL, D), f32)


def rows_of(b):
    return pl.ds(pl.multiple_of(T * b, TAIL), T)


def coords(c_ref):
    return tuple(c_ref[i] for i in range(4))


def place_of(c_ref, shard):
    _, _, z, y = coords(c_ref)
    return ((shard % 2) ^ y, (shard // 2 - z) & 3)


def sub_of(c_ref, h, t, g):
    x, c, _, _ = coords(c_ref)
    return 4 * (c ^ h) + 2 * t + (g ^ x)


def scatter_pieces(c_ref, keep_ref, send_ref, at, piece):
    for h, dest in ((0, keep_ref), (1, send_ref)):
        for t in range(2):
            for g in range(2):
                j = sub_of(c_ref, h, t, g)
                for s in range(8):
                    f, k = place_of(c_ref, s)
                    value = piece(j, s)
                    dest[t, g, f, k, at : at + value.shape[0]] = value


def by_columns(ref):
    return lambda j, s: ref[64 * s : 64 * s + 64, pl.ds(pl.multiple_of(256 * j, 256), 256)]


def by_rows(ref):
    return lambda j, s: ref[pl.ds(pl.multiple_of(64 * j, 64), 64), 256 * s : 256 * s + 256]


def mlp_backward_kernel(
    layer_id,
    c_ref,
    dout_ref,
    act_ref,
    slope_ref,
    h_ref,
    mid_ref,
    vec_ref,
    w1_ref,
    w2_ref,
    dmid_ref,
    keep_ref,
    send_ref,
    small_ref,
    dfc1b_ref,
    left_s,
    right_s,
    grads_s,
    acts_s,
    tile_s,
):
    b = pl.program_id(0)
    base = layer_id * (6 + FF // D)
    size = dout_ref.shape[0]

    @pl.when(b == 0)
    def _():
        small_ref[...] = jnp.zeros_like(small_ref)
        dfc1b_ref[...] = jnp.zeros_like(dfc1b_ref)

    dout = dout_ref[...]
    low = dout.astype(bf16)
    rows = pl.ds(pl.multiple_of(size * b, TAIL), size)
    left_s[rows] = h_ref[...]
    right_s[rows] = low
    acts_s[rows] = act_ref[...]

    def enter(j, _):
        block = slice(D * j, D * j + D)
        return dot_t(low[:, :256], w2_ref[0, block]) + dot_t(low[:, 256:], w2_ref[1, block])

    def bend(j, grad_act):
        cols = slice(D * j, D * j + D)
        grad_pre = grad_act * slope_ref[:, cols].astype(f32)
        dfc1b_ref[:, cols] += rows_sum(grad_pre)
        grad = grad_pre.astype(bf16)
        grads_s[rows, cols] = grad
        return grad

    total = []

    def leave(j, grad):
        part = dot_t(grad, w1_ref[:, D * j : D * j + D])
        total.append(part if not total else total[-1] + part)

    pipelined(FF // D, enter, bend, leave)
    grad_normed = total[-1]
    hat, inverse = norm_hat(mid_ref[...])
    small_ref[0:1] += rows_sum(grad_normed * hat)
    small_ref[1:2] += rows_sum(grad_normed)
    small_ref[2:3] += rows_sum(dout)
    dmid_ref[...] = dout + norm_back(hat, inverse, vec_ref[base + 2 : base + 3], grad_normed)

    @pl.when(b == pl.num_programs(0) - 1)
    def _():
        tile_s[...] = t_dot(left_s[...], grads_s[...]).astype(bf16)
        scatter_pieces(c_ref, keep_ref, send_ref, 0, by_columns(tile_s))
        tile_s[...] = t_dot(right_s[...], acts_s[...]).astype(bf16)
        scatter_pieces(c_ref, keep_ref, send_ref, 64, by_rows(tile_s))


def last_backward_kernel(
    layer_id,
    c_ref,
    dmid_ref,
    x_ref,
    h_ref,
    qkv_ref,
    lse_ref,
    o_ref,
    vec_ref,
    wa_ref,
    label_ref,
    d0_ref,
    latent_ref,
    dhead_ref,
    small_m0,
    small_m1,
    small_a1,
    small_head,
    dfc1b0,
    dfc1b1,
    keep_ref,
    send_ref,
    left_s,
    outs_s,
    grads_s,
    lows_s,
    dqkv_s,
    tile_s,
    small_ref,
    table_s,
):
    b = pl.program_id(0)

    @pl.when(b == 0)
    def _():
        table_s[...] = jnp.zeros_like(table_s)

    refs = (dmid_ref, x_ref, h_ref, qkv_ref, lse_ref, o_ref, vec_ref, wa_ref, small_ref, left_s, outs_s, grads_s, lows_s, dqkv_s)
    embed_grads(b, label_ref, attention_backward(layer_id, *refs) + d0_ref[0], latent_ref, table_s)

    @pl.when(b == pl.num_programs(0) - 1)
    def _():
        attention_weights(c_ref, keep_ref, send_ref, left_s, outs_s, grads_s, lows_s, tile_s)
        table_s[ROW_HEAD:ROW_VEC] = dhead_ref[...]
        row = ROW_VEC
        for own, mlp, fc1b in ((small_ref, small_m0, dfc1b0), (small_a1, small_m1, dfc1b1)):
            table_s[row : row + 2] = own[0:2]
            table_s[row + 2 : row + 4] = mlp[0:2]
            table_s[row + 4 : row + 5] = own[2:3]
            table_s[row + 5 : row + 6] = mlp[2:3]
            for i in range(FF // D):
                table_s[row + 6 + i : row + 7 + i] = fc1b[:, D * i : D * i + D]
            row += 6 + FF // D
        table_s[row : row + 2] = small_head[0:2]
        table_s[row + 2 : row + 3] = small_a1[3:4]
        table_pieces(c_ref, small_head[2:3, 0:1], table_s[...], keep_ref, send_ref, 64)


def attention_backward(
    layer_id, dmid_ref, x_ref, h_ref, qkv_ref, lse_ref, o_ref, vec_ref, wa_ref, small_ref, left_s, outs_s, grads_s, lows_s, dqkv_s
):
    b = pl.program_id(0)
    rows = rows_of(b)
    base = layer_id * (6 + FF // D)

    @pl.when(b == 0)
    def _():
        small_ref[...] = jnp.zeros_like(small_ref)

    dmid = dmid_ref[0]
    low = dmid.astype(bf16)
    left_s[rows] = h_ref[0]
    outs_s[rows] = o_ref[0]
    lows_s[rows] = low
    grad_att = dot_t(low, wa_ref[:, 3 * D :]).astype(bf16)
    scale = HD**-0.5

    def cut(part, pair):
        return qkv_ref[0, :, part * D + 128 * pair : part * D + 128 * pair + 128]

    def put(part, pair, value):
        dqkv_s[: value.shape[0], part * D + 128 * pair : part * D + 128 * pair + 128] = value.astype(bf16)

    tails, tail_douts = spread_tail(qkv_ref[0, NP:, :D], scale), spread_tail(grad_att[NP:], 1.0)
    weights = jnp.exp(mask_keys(dot_t(qkv_ref[0, :, D : 2 * D], tails)) - lse_ref[0, HEADS : HEADS + 1, :TAIL])
    grad_w = dot_t(qkv_ref[0, :, 2 * D :], tail_douts)
    grad_s = (weights * (grad_w - rows_sum(weights * grad_w))).astype(bf16)
    tail_dk = dot(grad_s, tails)
    tail_dv = dot(weights.astype(bf16), tail_douts)
    dqkv_s[NP:, :D] = (gather_tail(t_dot(grad_s, qkv_ref[0, :, D : 2 * D])) * scale).astype(bf16)

    def score(pair, _):
        queries = apart(cut(0, pair)[:NP], scale)
        douts = apart(grad_att[:NP, 128 * pair : 128 * pair + 128], 1.0)
        return dot_t(cut(1, pair), queries), dot_t(cut(2, pair), douts), queries, douts

    def weigh(pair, held):
        scores, grad_w, queries, douts = held
        log_total = jnp.concatenate([lse_ref[0, 2 * pair + e : 2 * pair + e + 1] for e in range(2)], 1)
        weights = jnp.exp(mask_keys(scores) - log_total)
        grad_s = weights * (grad_w - rows_sum(weights * grad_w))
        return weights.astype(bf16), grad_s.astype(bf16), queries, douts

    def mix(pair, held):
        weights, grad_s, queries, douts = held
        cols = slice(128 * pair, 128 * pair + 128)
        keys = apart(cut(1, pair), scale)
        put(0, pair, t_dot(grad_s[:, :NP], keys[:T]) + t_dot(grad_s[:, NP:], keys[T:]))
        put(1, pair, dot(grad_s, queries) + tail_dk[:, cols])
        put(2, pair, dot(weights, douts) + tail_dv[:, cols])

    pipelined(HEADS // 2, score, weigh, mix)
    grads_s[rows] = dqkv_s[...]
    grad_normed = dot_t(dqkv_s[...], wa_ref[:, : 3 * D])
    hat, inverse = norm_hat(x_ref[0])
    small_ref[0:1] += rows_sum(grad_normed * hat)
    small_ref[1:2] += rows_sum(grad_normed)
    small_ref[2:3] += rows_sum(dmid)
    return dmid + norm_back(hat, inverse, vec_ref[base : base + 1], grad_normed)


def attention_weights(c_ref, keep_ref, send_ref, left_s, outs_s, grads_s, lows_s, tile_s):
    tile_s[:, : 3 * D] = t_dot(left_s[...], grads_s[...]).astype(bf16)
    tile_s[:, 3 * D :] = t_dot(outs_s[...], lows_s[...]).astype(bf16)
    scatter_pieces(c_ref, keep_ref, send_ref, 0, by_columns(tile_s))


def middle_backward_kernel(
    layer_id,
    c_ref,
    dmid_ref,
    x_ref,
    h_ref,
    qkv_ref,
    lse_ref,
    o_ref,
    vec_ref,
    wa_ref,
    x1_ref,
    x0_ref,
    ws_ref,
    keep_ref,
    send_ref,
    d1_ref,
    d0_ref,
    small_ref,
    left_s,
    outs_s,
    grads_s,
    lows_s,
    dqkv_s,
    tile_s,
    both_s,
    skip_s,
    skip_tile_s,
):
    b = pl.program_id(0)
    refs = (dmid_ref, x_ref, h_ref, qkv_ref, lse_ref, o_ref, vec_ref, wa_ref, small_ref)
    grad = attention_backward(layer_id, *refs, left_s, outs_s, grads_s, lows_s, dqkv_s)
    low = grad.astype(bf16)
    small_ref[3:4] += rows_sum(grad)
    rows = rows_of(b)
    both_s[rows, :D] = x1_ref[0].astype(bf16)
    both_s[rows, D:] = x0_ref[0].astype(bf16)
    skip_s[rows] = low
    for u, dest in ((0, d1_ref), (1, d0_ref)):
        cols = slice(D * u, D * u + D)
        dest[0] = dot_t(low[:, :256], ws_ref[0, cols]) + dot_t(low[:, 256:], ws_ref[1, cols])

    @pl.when(b == pl.num_programs(0) - 1)
    def _():
        attention_weights(c_ref, keep_ref, send_ref, left_s, outs_s, grads_s, lows_s, tile_s)
        skip_tile_s[...] = t_dot(both_s[...], skip_s[...]).astype(bf16)
        for half in range(2):

            def piece(j, s, half=half):
                rows = pl.ds(pl.multiple_of(128 * s + 16 * j, 16), 16)
                return skip_tile_s[rows, 256 * half : 256 * half + 256]

            scatter_pieces(c_ref, keep_ref, send_ref, 64 + 16 * half, piece)


def embed_grads(b, label_ref, grad, latent_ref, table_s):
    table_s[:T] += grad
    patch = grad[:NP]
    last = ROW_VEC + N_VEC - 1
    table_s[last : last + 1] += rows_sum(patch)
    table_s[ROW_PATCH:ROW_CLASS] += dot(latent_ref[0], patch.astype(bf16))
    row = lax.broadcasted_iota(jnp.int32, (CLASSES, D), 0)
    table_s[ROW_CLASS:ROW_HEAD] += jnp.where(row == label_ref[b], grad[NP + 1 : NP + 2], 0.0)


def table_pieces(c_ref, loss, table, keep_ref, send_ref, at):
    x, c, z, y = coords(c_ref)
    me = (x * 2 + c) * 8 + z * 2 + y
    high = loss.astype(bf16).astype(f32)
    middle = (loss - high).astype(bf16).astype(f32)
    small = loss - high - middle
    row = lax.broadcasted_iota(jnp.int32, (ROWS, D), 0)
    kind = lax.broadcasted_iota(jnp.int32, (ROWS, D), 1) % 8
    slots = jnp.where(kind == 0, high, jnp.where(kind == 1, middle, jnp.where(kind == 2, small, 0.0)))
    turned = jnp.where(row == ROW_LOSS + me, slots, table).T
    for s in range(8):
        f, k = place_of(c_ref, s)
        for j in range(8):
            rows = slice(64 * s + 8 * j, 64 * s + 8 * j + 8)
            piece = jnp.concatenate([turned[rows, :256], turned[rows, 256:]], 0).astype(bf16)
            h, t, g = (j // 4) ^ c, j // 2 % 2, (j % 2) ^ x

            @pl.when(h == 0)
            def _(piece=piece, t=t, g=g, f=f, k=k):
                keep_ref[t, g, f, k, at : at + 16] = piece

            @pl.when(h == 1)
            def _(piece=piece, t=t, g=g, f=f, k=k):
                send_ref[t, g, f, k, at : at + 16] = piece


def per_seq(width, rows=T):
    return pl.BlockSpec((1, rows, width), lambda b: (b, 0, 0))


def fixed(shape):
    return pl.BlockSpec(shape, lambda b: (0,) * len(shape))


def shape_of(shape, dtype=f32):
    return jax.ShapeDtypeStruct(shape, dtype)


def pieces_shape(rows):
    return (2, 2, 2, 4, rows, 256)


def call_attention(order, first, n_seqs, inputs):
    shapes = [(T, D, f32), (T, D, bf16), (T, 3 * D, bf16), (LSE, NP, f32), (T, D, bf16), (T, D, f32)]
    vec_spec, wa_spec = fixed((N_VEC, D)), fixed((D, 4 * D))
    if first:
        in_specs = [SMEM, per_seq(NP, CH), per_seq(D, TAIL), fixed((ROWS, D)), vec_spec, wa_spec]
    else:
        in_specs = [per_seq(D), per_seq(D), fixed((2, 2 * D, D // 2)), vec_spec, wa_spec]
    return order(
        embed_attention_kernel if first else skip_attention_kernel,
        inputs,
        in_specs,
        [shape_of((n_seqs, r, w), d) for r, w, d in shapes],
        [per_seq(w, r) for r, w, _ in shapes],
        grid=(n_seqs,),
        name="attention_forward_%d" % (0 if first else 1),
    )


MLP_STEPS = 4


def flat(width, rows):
    return pl.BlockSpec((rows, width), lambda b: (b, 0))


def call_mlp(order, layer_id, n_seqs, mid, vec, w1, w2, head=None):
    shapes = [(D, bf16), (FF, bf16), (FF, bf16), (D, f32)]
    whole = n_seqs * T
    size = T if head else whole // MLP_STEPS
    inputs = [mid.reshape(whole, D), vec, w1, w2]
    specs = [flat(D, size), fixed((N_VEC, D)), fixed((D, FF)), fixed((2, FF, D // 2))]
    outs = [shape_of((whole, w), d) for w, d in shapes]
    out_specs = [flat(w, size) for w, _ in shapes]
    kernel = functools.partial(mlp_kernel, layer_id)
    if head:
        total, weights, noise, tab = head
        kernel = mlp_head_kernel
        inputs = [total, weights, *inputs, noise, tab]
        specs = [SMEM, SMEM, *specs, per_seq(NP, CH), fixed((ROWS, D))]
        outs += [shape_of((CH, D)), shape_of((8, D))]
        out_specs += [fixed((CH, D)), fixed((8, D))]
    out = order(kernel, inputs, specs, outs, out_specs, grid=(whole // size,), name="mlp_forward_%d" % layer_id)
    return [*out[:3], out[3].reshape(n_seqs, T, D), *out[4:]]


def call_mlp_backward(order, layer_id, n_seqs, place, dout, act, slope, normed, mid, vec, w1, w2):
    whole = n_seqs * T
    size = whole // MLP_STEPS
    pieces = pieces_shape(128)
    out = order(
        functools.partial(mlp_backward_kernel, layer_id),
        (place, dout.reshape(whole, D), act, slope, normed, mid.reshape(whole, D), vec, w1, w2),
        [SMEM, flat(D, size), flat(FF, size), flat(FF, size), flat(D, size), flat(D, size)]
        + [fixed((N_VEC, D)), fixed((D, FF)), fixed((2, FF, D // 2))],
        [shape_of((whole, D)), shape_of(pieces, bf16), shape_of(pieces, bf16), shape_of((8, D)), shape_of((1, FF))],
        [flat(D, size), fixed(pieces), fixed(pieces), fixed((8, D)), fixed((1, FF))],
        [
            pltpu.VMEM((whole, D), bf16),
            pltpu.VMEM((whole, D), bf16),
            pltpu.VMEM((whole, FF), bf16),
            pltpu.VMEM((whole, FF), bf16),
            pltpu.VMEM((D, FF), bf16),
        ],
        grid=(MLP_STEPS,),
        name="mlp_backward_%d" % layer_id,
    )
    return [out[0].reshape(n_seqs, T, D), *out[1:]]


def call_attention_backward(order, layer_id, n_seqs, place, dmid, x, normed, qkv, lse, att, vec, wa, more):
    whole = n_seqs * T
    pieces = pieces_shape(80 if layer_id == 0 else 96)
    specs = [SMEM, per_seq(D), per_seq(D), per_seq(D), per_seq(3 * D), per_seq(NP, LSE), per_seq(D)]
    specs += [fixed((N_VEC, D)), fixed((D, 4 * D))]
    scratch = [
        pltpu.VMEM((whole, D), bf16),
        pltpu.VMEM((whole, D), bf16),
        pltpu.VMEM((whole, 3 * D), bf16),
        pltpu.VMEM((whole, D), bf16),
        pltpu.VMEM((T, 3 * D), bf16),
        pltpu.VMEM((D, 4 * D), bf16),
    ]
    if layer_id == 1:
        kernel = middle_backward_kernel
        specs += [per_seq(D), per_seq(D), fixed((2, 2 * D, D // 2))]
        outs = [shape_of((n_seqs, T, D)), shape_of((n_seqs, T, D)), shape_of((8, D))]
        out_specs = [per_seq(D), per_seq(D), fixed((8, D))]
        scratch += [pltpu.VMEM((whole, 2 * D), bf16), pltpu.VMEM((whole, D), bf16), pltpu.VMEM((2 * D, D), bf16)]
    else:
        kernel = last_backward_kernel
        specs += [SMEM, per_seq(D), per_seq(NP, CH), fixed((CH, D))] + [fixed((8, D))] * 4 + [fixed((1, FF))] * 2
        scratch += [pltpu.VMEM((8, D), f32), pltpu.VMEM((ROWS, D), f32)]
        outs, out_specs = [], []
    return order(
        functools.partial(kernel, layer_id),
        [place, dmid, x, normed, qkv, lse, att, vec, wa, *more],
        specs,
        [shape_of(pieces, bf16), shape_of(pieces, bf16)] + outs,
        [fixed(pieces), fixed(pieces)] + out_specs,
        scratch,
        grid=(n_seqs,),
        name="attention_backward_%d" % layer_id,
    )


def device_id(x, c, z, y):
    return (x * 2 + c) * 8 + z * 2 + y


def pairs(move):
    every = [(x, c, z, y) for x in range(2) for c in range(2) for z in range(4) for y in range(2)]
    return [(device_id(*at), device_id(*move(*at))) for at in every]


TO_CORE = pairs(lambda x, c, z, y: (x, 1 - c, z, y))
TO_X = pairs(lambda x, c, z, y: (1 - x, c, z, y))
TO_Y = pairs(lambda x, c, z, y: (x, c, z, 1 - y))
TO_Z = [pairs(lambda x, c, z, y, k=k: (x, c, (z + k) % 4, y)) for k in range(4)]
PIECE_ROWS = {"a": 64, "m": 128, "s": 32, "t": 16}


def send(value, to):
    return lax.ppermute(value, ALL, to)


def rows_in(kinds):
    return sum(PIECE_ROWS[kind[0]] for kind in kinds)


def pack_kernel(kinds, c_ref, mats_ref, down_ref, skip_ref, tab_ref, vec_ref, weight_ref, u_ref, wide_s, narrow_s, sem):
    x, c, _, _ = coords(c_ref)
    copies, casts = [], []
    wide = narrow = row = 0
    for kind in kinds:
        l = int(kind[1:] or 0)
        if kind[0] in "am":
            for t in range(2):
                start = (2048 if kind[0] == "m" else 0) + 256 * (4 * c + 2 * t + x)
                copies.append((mats_ref.at[l, :, pl.ds(pl.multiple_of(start, 256), 256)], wide_s.at[wide]))
                casts.append((t, row, wide_s.at[wide], None))
                wide += 1
            row += 64
        if kind[0] in "ms":
            size = 32 if kind[0] == "m" else 16
            ref = down_ref.at[l] if kind[0] == "m" else skip_ref
            for t in range(2):
                start = pl.multiple_of(size * (4 * c + 2 * t + x), size)
                copies.append((ref.at[pl.ds(start, size)], narrow_s.at[narrow, :size]))
                for half in range(2):
                    cols = slice(256 * half, 256 * half + 256)
                    casts.append((t, row + size * half, narrow_s.at[narrow, :size], cols))
                narrow += 1
            row += 2 * size
        if kind[0] == "t":
            own_weight = weight_ref[0]
            for i in range(1, weight_ref.shape[0]):
                own_weight += weight_ref[i]
            turned = vec_ref[...].T
            first, last = CH + CLASSES, CH + CLASSES + SEQ_LEN
            corner = (lax.broadcasted_iota(jnp.int32, (16, 256), 0) == 8) & (
                lax.broadcasted_iota(jnp.int32, (16, 256), 1) == 255
            )
            for t in range(2):
                j = 4 * c + 2 * t + x
                table = tab_ref[pl.ds(pl.multiple_of(8 * j, 8), 8)]
                vecs = turned[0:8]
                for i in range(1, 8):
                    vecs = jnp.where(j == i, turned[8 * i : 8 * i + 8], vecs)
                rest = [
                    table[:, first : first + 2],
                    jnp.zeros((8, TAIL - 2), f32),
                    table[:, :first],
                    table[:, last:],
                    vecs,
                    jnp.zeros((8, ROWS - ROW_VEC - N_VEC), f32),
                ]
                piece = jnp.concatenate([table[:, first + 2 : last], jnp.concatenate(rest, 1)], 0)
                if t == 0:
                    piece = jnp.where(corner, own_weight.astype(f32), piece)
                u_ref[t, row : row + 16] = piece.astype(bf16)
            row += 16
    copies = [pltpu.make_async_copy(a, b, sem) for a, b in copies]
    for copy in copies:
        copy.start()
    yield
    for copy in copies:
        copy.wait()
    for t, at, ref, cols in casts:
        value = ref[...] if cols is None else ref[:, cols]
        u_ref[t, at : at + value.shape[0]] = value.astype(bf16)


def join_ring_kernel(u0, u1, u2, u3, b_ref, c_ref):
    for k, ref in enumerate((u0, u1, u2, u3)):
        b_ref[k] = ref[0]
        c_ref[k] = ref[1]


def join_pair_kernel(b0, b1, c0, c1, b_ref, c_ref):
    for i, (b, c) in enumerate(((b0, c0), (b1, c1))):
        b_ref[i] = b[...]
        c_ref[i] = c[...]


def join_own_kernel(b, c, both_ref):
    both_ref[0] = b[...]
    both_ref[1] = c[...]


def assemble_kernel(kinds, c_ref, *refs):
    x, c, z, y = coords(c_ref)
    sources, dests = refs[:7], refs[7:]
    for h in range(2):
        if h == 0:
            own_b, x_b, own_c, y_c = sources[:4]
        else:
            own_b, own_c, x_b, y_c = sources[4].at[0], sources[4].at[1], sources[5], sources[6]
        for t in range(2):
            for g in range(2):
                j = 4 * (c ^ h) + 2 * t + (g ^ x)
                cols = pl.ds(pl.multiple_of(256 * j, 256), 256)
                for f in range(2):
                    src = ((own_b, x_b)[g].at[f]) if t == 0 else ((own_c, y_c)[f].at[g])
                    for k in range(4):
                        s = 2 * ((z - k) & 3) + (y ^ f)
                        row = 0
                        at = 0
                        for kind in kinds:
                            if kind[0] in "am":
                                rows = pl.ds(pl.multiple_of(64 * s, 64), 64)
                                dests[at][rows, cols] = src[k, row : row + 64]
                                row, at = row + 64, at + 1
                            if kind[0] in "ms":
                                size = 32 if kind[0] == "m" else 16
                                rows = pl.ds(pl.multiple_of(size * (8 * s + j), size), size)
                                for half in range(2):
                                    dests[at][half, rows] = src[k, row : row + size]
                                    row += size
                                at += 1
                            if kind[0] == "t":
                                both = src[k, row : row + 16].astype(f32)
                                rows = pl.ds(pl.multiple_of(64 * s + 8 * j, 8), 8)
                                dests[-1][rows, :256] = both[:8]
                                dests[-1][rows, 256:] = both[8:]
    if "t" in kinds:
        table_ref, vec_ref, total_ref, turned_s = dests[-4:]
        table = turned_s[...].T
        table_ref[...] = table.astype(bf16)
        vec_ref[...] = table[ROW_VEC : ROW_VEC + N_VEC]
        total_ref[0, 0] = jnp.sum(table[ROW_WEIGHT : ROW_WEIGHT + 1])


class Gather:
    def __init__(self, place, kinds, sources):
        self.place, self.kinds, self.sources = place, kinds, sources
        self.rows = rows_in(kinds)

    def pack(self):
        return Part(
            functools.partial(pack_kernel, self.kinds),
            (self.place, *self.sources),
            [SMEM, ANY, ANY, ANY] + ([WHOLE, WHOLE, SMEM] if "t" in self.kinds else [ANY] * 3),
            [shape_of((2, self.rows, 256), bf16)],
            [WHOLE],
            [pltpu.VMEM((4, 64, 256), f32), pltpu.VMEM((4, 32, D), f32), pltpu.SemaphoreType.DMA],
        )

    def packed(self, results):
        (own,) = results
        self.ring = [own] + [send(own, TO_Z[k]) for k in range(1, 4)]

    def join_ring(self):
        half = shape_of((4, self.rows, 256), bf16)
        return Part(join_ring_kernel, self.ring, [WHOLE] * 4, [half] * 2, [WHOLE] * 2)

    def ring_joined(self, results):
        b, c = results
        self.halves = (b, send(b, TO_Y), c, send(c, TO_X))

    def join_pair(self):
        whole = shape_of((2, 4, self.rows, 256), bf16)
        return Part(join_pair_kernel, self.halves, [WHOLE] * 4, [whole, whole], [WHOLE] * 2)

    def pair_joined(self, results):
        b, c = results
        self.mine = [b, send(b, TO_X), c, send(c, TO_Y)]

    def join_own(self):
        both = shape_of((2, 2, 4, self.rows, 256), bf16)
        return Part(join_own_kernel, (self.mine[0], self.mine[2]), [WHOLE] * 2, [both], [WHOLE])

    def own_joined(self, results):
        self.other = [send(results[0], TO_CORE)]

    def rest_to_core(self):
        self.other += [send(self.mine[1], TO_CORE), send(self.mine[3], TO_CORE)]

    def assemble(self):
        shapes, scratch = [], []
        for kind in self.kinds:
            if kind[0] in "am":
                shapes.append(shape_of((D, 2048), bf16))
            if kind[0] == "m":
                shapes.append(shape_of((2, FF, 256), bf16))
            if kind[0] == "s":
                shapes.append(shape_of((2, 2 * D, 256), bf16))
            if kind[0] == "t":
                shapes += [shape_of((ROWS, D), bf16), shape_of((N_VEC, D)), shape_of((1, 1))]
                scratch = [pltpu.VMEM((D, ROWS), f32)]
        return Part(
            functools.partial(assemble_kernel, self.kinds),
            (self.place, *self.mine, *self.other),
            [SMEM] + [WHOLE] * 7,
            shapes,
            [SMEM if shape.shape == (1, 1) else WHOLE for shape in shapes],
            scratch,
        )


def added(*values):
    total = values[0].astype(f32)
    for value in values[1:]:
        total += value.astype(f32)
    return total.astype(bf16)


def add_core_kernel(n, *refs):
    keeps, gots, (b0_ref, b1_ref, c0_ref, c1_ref) = refs[:n], refs[n : 2 * n], refs[2 * n :]
    row = 0
    for keep, got in zip(keeps, gots):
        rows = slice(row, row + keep.shape[4])
        row = rows.stop
        for i in range(2):
            for dest, at in ((b0_ref, (0, 0, i)), (b1_ref, (0, 1, i)), (c0_ref, (1, i, 0)), (c1_ref, (1, i, 1))):
                dest[i, :, rows] = added(keep[at], got[at])


def add_both_kernel(b0_ref, gb_ref, c0_ref, gc_ref, b_ref, sb_ref, c_ref, sc_ref):
    for keep, got, dests in ((b0_ref, gb_ref, (b_ref, sb_ref)), (c0_ref, gc_ref, (c_ref, sc_ref))):
        for i, dest in enumerate(dests):
            dest[...] = added(keep[i], got[i])


def add_ring_kernel(b_ref, gb_ref, c_ref, gc_ref, *dests):
    for t, (keep, got) in enumerate(((b_ref, gb_ref), (c_ref, gc_ref))):
        for k, dest in enumerate(dests):
            dest[t] = added(keep[k], got[k])


def add_last_kernel(*refs):
    row = 0
    for i in range(0, len(refs) - 1, 4):
        rows = slice(row, row + refs[i].shape[1])
        row = rows.stop
        refs[-1][:, rows] = added(*(ref[...] for ref in refs[i : i + 4]))


class Reduce:
    def __init__(self, kinds):
        self.kinds = kinds
        self.rows = rows_in(kinds)
        self.keep, self.got = [], []

    def start(self, keep, give):
        self.keep.append(keep)
        self.got.append(send(give, TO_CORE))

    def core(self):
        def six(rows):
            return pl.BlockSpec((2, 2, 2, 1, rows, 256), lambda k: (0, 0, 0, k, 0, 0))

        four = pl.BlockSpec((2, 1, self.rows, 256), lambda k: (0, k, 0, 0))
        parts = self.keep + self.got
        return Part(
            functools.partial(add_core_kernel, len(self.keep)),
            parts,
            [six(part.shape[4]) for part in parts],
            [shape_of((2, 4, self.rows, 256), bf16)] * 4,
            [four] * 4,
        )

    def core_added(self, results):
        b0, b1, c0, c1 = results
        self.parts = (b0, send(b1, TO_X), c0, send(c1, TO_Y))

    def both(self):
        four = pl.BlockSpec((2, 1, self.rows, 256), lambda k: (0, k, 0, 0))
        three = pl.BlockSpec((1, self.rows, 256), lambda k: (k, 0, 0))
        return Part(
            add_both_kernel, self.parts, [four] * 4, [shape_of((4, self.rows, 256), bf16)] * 4, [three] * 4
        )

    def both_added(self, results):
        b, sb, c, sc = results
        self.parts = (b, send(sb, TO_Y), c, send(sc, TO_X))

    def ring(self):
        small = shape_of((2, self.rows, 256), bf16)
        return Part(add_ring_kernel, self.parts, [WHOLE] * 4, [small] * 4, [WHOLE] * 4)

    def ring_added(self, results):
        self.parts = [results[0]] + [send(results[k], TO_Z[k]) for k in range(1, 4)]


class Owned:
    def __init__(self, *chunks):
        self.chunks = chunks
        self.kinds = [kind for chunk in chunks for kind in chunk.kinds]

    def last(self):
        parts = [part for chunk in self.chunks for part in chunk.parts]
        out = shape_of((2, rows_in(self.kinds), 256), bf16)
        return Part(add_last_kernel, parts, [WHOLE] * len(parts), [out], [WHOLE])

    def last_added(self, results):
        (mine,) = results
        near = send(mine, TO_X)
        self.parts = (mine, near, send(mine, TO_CORE), send(near, TO_CORE))

    def adam(self, order, place, states, bufs, name):
        inputs, in_specs, outs, out_specs, aliases = [place, *self.parts], [SMEM] + [WHOLE] * 4, [], [], {}
        targets = []
        for kind in self.kinds:
            l = int(kind[1:] or 0)
            if kind[0] == "a":
                targets.append(("mats", "a", pl.BlockSpec((1, 64, 4096), lambda i, l=l: (l, 0, 0))))
            if kind[0] == "m":
                targets.append(("down", "d", pl.BlockSpec((1, 256, D), lambda i, l=l: (l, 0, 0))))
            if kind[0] == "s":
                targets.append(("skip", "s", fixed((128, D))))
            if kind[0] == "t":
                targets.append(("tables", "t", fixed((64, SEQ_LEN + 3 * CH))))
                targets.append(("vectors", "v", fixed((N_VEC, 64))))
        held = []
        for name, _, spec in targets:
            inputs += list(states[name])
            in_specs += [spec] * 3
            weight = states[name][0]
            if bufs.get(name) is not None:
                held += [(len(outs) + i, buf) for i, buf in enumerate(bufs[name])]
            outs += [shape_of(weight.shape)] * 3 + [shape_of(weight.shape, bf16)]
            out_specs += [spec] * 4
        n_read = len(inputs)
        for at, buf in held:
            aliases[len(inputs)] = at
            inputs.append(buf)
            in_specs.append(ANY)
        scratch = []
        if any(t[1] == "d" for t in targets):
            scratch.append(pltpu.VMEM((D, 256), f32))
        if any(t[1] == "t" for t in targets):
            scratch.append(pltpu.VMEM((64, ROWS), f32))
            outs.append(shape_of((1, 1)))
            out_specs.append(SMEM)
        result = order(
            functools.partial(adam_kernel, self.kinds, [t[1] for t in targets], n_read, len(inputs)),
            inputs,
            in_specs,
            outs,
            out_specs,
            scratch,
            name=name,
            aliases=aliases,
        )
        for i, (name, _, _) in enumerate(targets):
            bufs[name] = result[4 * i : 4 * i + 4]
        return result[4 * len(targets) :]


def adam_kernel(kinds, targets, n_read, n_in, c_ref, *refs):
    x, c, _, _ = coords(c_ref)
    parts, ins, outs = refs[:4], refs[4 : n_read - 1], refs[n_in - 1 :]
    scratch = list(outs[4 * len(targets) :])
    loss_ref = scratch.pop(0) if "t" in targets else None
    offsets, row = {}, 0
    for kind in kinds:
        offsets[kind[0]] = row
        row += PIECE_ROWS[kind[0]]
    pieces = []
    for h in range(2):
        for g in range(2):
            for t in range(2):
                pieces.append((4 * (c ^ h) + 2 * t + (g ^ x), parts[2 * h + g].at[t]))
    for i, kind in enumerate(targets):
        state, dests = ins[3 * i : 3 * i + 3], outs[4 * i : 4 * i + 4]
        row = offsets[{"d": "m", "v": "t"}.get(kind, kind)]

        def update(at, grad, rate, state=state, dests=dests):
            weight, first, second = (ref[at] for ref in state)
            values = adam_update(weight, grad, first, second, rate)
            for dest, value in zip(dests, values):
                dest[at] = value

        if kind == "a":
            for at_row, start in ((row, 0), (offsets["m"], 2048)):
                for j, piece in pieces:
                    at = (0, slice(None), pl.ds(pl.multiple_of(start + 256 * j, 256), 256))
                    update(at, piece[at_row : at_row + 64], step_rates[0])
        if kind == "d":
            held = scratch[0]
            for j, piece in pieces:
                held[pl.ds(pl.multiple_of(64 * j, 64), 64)] = piece[row + 64 : row + 128].astype(f32)
            update((0,), held[...].T, step_rates[1])
        if kind == "s":
            for j, piece in pieces:
                for half in range(2):
                    at = (pl.ds(pl.multiple_of(16 * j, 16), 16), slice(256 * half, 256 * half + 256))
                    update(at, piece[row + 16 * half : row + 16 * half + 16], step_rates[2])
        if kind == "t":
            held = scratch[-1]
            for j, piece in pieces:
                both = piece[row : row + 16].astype(f32)
                rows = pl.ds(pl.multiple_of(8 * j, 8), 8)
                held[rows, :256] = both[:8]
                held[rows, 256:] = both[8:]
            grad = held[...]
            parts_of = [grad[:, ROW_PATCH:ROW_HEAD], grad[:, NP : NP + 2], grad[:, :NP], grad[:, ROW_HEAD:ROW_VEC]]
            update(slice(None), jnp.concatenate(parts_of, 1), step_rates[3])
            loss_ref[0, 0] = jnp.sum(grad[0:3, ROW_LOSS : ROW_LOSS + 32])
        if kind == "v":
            grad = scratch[-1][:, ROW_VEC : ROW_VEC + N_VEC].T
            update(slice(None), grad, step_rates[4])


def gather_any(mats, down, skip, tables, vectors):
    first, last = CH + CLASSES, CH + CLASSES + SEQ_LEN
    width = tables.shape[1]
    tab = jnp.concatenate(
        [
            tables[first + 2 : last],
            tables[first : first + 2],
            jnp.zeros((TAIL - 2, width), f32),
            tables[:first],
            tables[last:],
            vectors,
            jnp.zeros((ROWS - ROW_VEC - N_VEC, width), f32),
        ]
    )
    every = lax.all_gather(mats.astype(bf16), "shard", axis=1, tiled=True)
    downs = lax.all_gather(down.astype(bf16), "shard", axis=1, tiled=True)
    skips = lax.all_gather(skip.astype(bf16), "shard", axis=0, tiled=True)
    table = lax.all_gather(tab.astype(bf16), "shard", axis=1, tiled=True)

    def halves(m):
        return jnp.stack([m[:, : D // 2], m[:, D // 2 :]])

    mats_of = [(every[l, :, :2048], every[l, :, 2048:]) for l in range(LAYERS)]
    return (mats_of, [halves(downs[l]) for l in range(LAYERS)], halves(skips), table)


def reduce_any(grads):
    def ordered(kind):
        both = jnp.stack(grads[kind])
        return both.transpose(0, 1, 2, 4, 3, 5, 6).reshape((8, 8) + both.shape[5:])

    def shard_sum(value, axis):
        owned = lax.psum_scatter(value.astype(f32), "shard", scatter_dimension=axis, tiled=True)
        return lax.psum(owned.astype(bf16), "rep")

    mats, down = [], []
    for l in range(LAYERS):
        attn, mlp = ordered("a%d" % l), ordered("m%d" % l)
        both = [part[:, :, :64].transpose(1, 2, 0, 3).reshape(D, 2048) for part in (attn, mlp)]
        mats.append(jnp.concatenate(both, 1))
        down.append(mlp[:, :, 64:].transpose(0, 2, 1, 3).reshape(D, FF).T)
    skip = ordered("a1")[:, :, 64:].reshape(8, 8, 2, 16, 256).transpose(1, 0, 3, 2, 4).reshape(2 * D, D)
    turned = ordered("a0")[:, :, 64:].reshape(8, 8, 2, 8, 256).transpose(1, 0, 3, 2, 4).reshape(D, ROWS)
    return (shard_sum(jnp.stack(mats), 1), shard_sum(jnp.stack(down), 1), shard_sum(skip, 0), shard_sum(turned, 0))


def time_token(timesteps):
    half_width = D // 2
    freqs_row = jnp.exp(-math.log(10000.0) * jnp.arange(half_width, dtype=f32) / half_width)
    angles = timesteps.astype(f32)[:, None] * freqs_row[None, :]
    return jnp.concatenate([jnp.cos(angles), jnp.sin(angles)], -1)


def adam_update(weight, grad, moment_one, moment_two, step_rate):
    grad = grad.astype(f32)
    moment_one = beta_one * moment_one + (1.0 - beta_one) * grad
    moment_two = beta_two * moment_two + (1.0 - beta_two) * grad * grad
    first_hat = moment_one / (1.0 - beta_one**STEP)
    second_hat = moment_two / (1.0 - beta_two**STEP)
    weight = weight - step_rate * (first_hat / (jnp.sqrt(second_hat) + epsilon) + weight_decay * weight)
    return (moment_one, moment_two, weight, weight.astype(bf16))


def local(
    fast,
    latents,
    target_noise,
    labels,
    timesteps,
    loss_weight,
    layer_mats,
    layer_mats_first,
    layer_mats_second,
    down_mats,
    down_first,
    down_second,
    skip_mat,
    skip_first,
    skip_second,
    tables,
    tables_first,
    tables_second,
    vectors,
    vectors_first,
    vectors_second,
):
    n_seqs = latents.shape[0]
    if fast:
        rep, shard = lax.axis_index("rep"), lax.axis_index("shard")
        place = jnp.stack([rep // 2, rep % 2, shard // 2, shard % 2]).astype(jnp.int32)
    else:
        place = jnp.zeros((4,), jnp.int32)
    order = Order()
    time_rows = jnp.pad(time_token(timesteps)[:, None], ((0, 0), (0, TAIL - 1), (0, 0)))
    mats, downs = [None, None], [None, None]
    forward = {}

    def attention(l):
        if l == 0:
            inputs = (labels, latents, time_rows, table, vec, mats[0][0])
        else:
            inputs = (forward["x1"], forward["x0"], ws, vec, mats[1][0])
        forward["a%d" % l] = call_attention(order, l == 0, n_seqs, inputs)
        if l == 0:
            forward["x0"] = forward["a0"][0]

    def mlp(l):
        head = (weight_total, loss_weight, target_noise, table) if l == 1 else None
        out = call_mlp(order, l, n_seqs, forward["a%d" % l][5], vec, mats[l][1], downs[l], head)
        forward["m%d" % l] = out
        forward["x%d" % (l + 1)] = out[3]

    if fast:
        args = (layer_mats, down_mats, skip_mat, tables.T, vectors, loss_weight)
        one, two, three, four = (Gather(place, kinds, args) for kinds in GATHER_CHUNKS)
        one.packed(*order.fuse([one.pack()], "pack_0"))
        joined, packed = order.fuse([one.join_ring(), two.pack()], "join_ring_0")
        one.ring_joined(joined)
        two.packed(packed)
        one.pair_joined(*order.fuse([one.join_pair()], "join_pair_0"))
        joined, own = order.fuse([two.join_ring(), one.join_own()], "join_ring_1")
        two.ring_joined(joined)
        one.own_joined(own)
        one.rest_to_core()
        (wa0, table, vec, weight_total), packed = order.fuse([one.assemble(), three.pack()], "assemble_0")
        mats[0] = (wa0, None)
        three.packed(packed)
        two.pair_joined(*order.fuse([two.join_pair()], "join_pair_1"))
        attention(0)
        joined, own = order.fuse([three.join_ring(), two.join_own()], "join_ring_2")
        three.ring_joined(joined)
        two.own_joined(own)
        two.rest_to_core()
        (w10, downs[0]), packed = order.fuse([two.assemble(), four.pack()], "assemble_1")
        mats[0] = (wa0, w10)
        four.packed(packed)
        three.pair_joined(*order.fuse([three.join_pair()], "join_pair_2"))
        mlp(0)
        joined, own = order.fuse([four.join_ring(), three.join_own()], "join_ring_3")
        four.ring_joined(joined)
        three.own_joined(own)
        three.rest_to_core()
        ((wa1, ws),) = order.fuse([three.assemble()], "assemble_2")
        mats[1] = (wa1, None)
        four.pair_joined(*order.fuse([four.join_pair()], "join_pair_3"))
        four.own_joined(*order.fuse([four.join_own()], "join_own_3"))
        attention(1)
        four.rest_to_core()
        ((w11, downs[1]),) = order.fuse([four.assemble()], "assemble_3")
        mats[1] = (wa1, w11)
        mlp(1)
    else:
        mats, downs, ws, table = gather_any(layer_mats, down_mats, skip_mat, tables, vectors)
        vec = table[ROW_VEC : ROW_VEC + N_VEC].astype(f32)
        weight_total = lax.psum(jnp.sum(loss_weight.astype(f32)), ALL).reshape(1, 1)
        attention(0)
        mlp(0)
        attention(1)
        mlp(1)

    dx, dhead, small_head = forward["m1"][3:]
    grads, small = {}, {}

    def mlp_back(l, dout):
        normed, act, slope = forward["m%d" % l][:3]
        out = call_mlp_backward(
            order, l, n_seqs, place, dout, act, slope, normed, forward["a%d" % l][5], vec, mats[l][1], downs[l]
        )
        grads["m%d" % l], small["m%d" % l], small["f%d" % l] = out[1:3], out[3], out[4]
        return out[0]

    def attention_back(l, dmid, more):
        x, normed, qkv, lse, att, _ = forward["a%d" % l]
        out = call_attention_backward(order, l, n_seqs, place, dmid, x, normed, qkv, lse, att, vec, mats[l][0], more)
        grads["a%d" % l] = out[:2]
        return out[2:]

    bufs = {}
    if fast:
        first, second, third = (Reduce(kinds) for kinds in REDUCE_CHUNKS)
        states = {
            "mats": (layer_mats, layer_mats_first, layer_mats_second),
            "down": (down_mats, down_first, down_second),
            "skip": (skip_mat, skip_first, skip_second),
            "tables": (tables.T, tables_first.T, tables_second.T),
            "vectors": (vectors, vectors_first, vectors_second),
        }
    dmid = mlp_back(1, dx)
    if fast:
        first.start(*grads["m1"])
    dx, d0, small["a1"] = attention_back(1, dmid, (forward["x1"], forward["x0"], ws))
    if fast:
        first.start(*grads["a1"])
        first.core_added(*order.fuse([first.core()], "add_core_1", grid=(4,)))
    dmid = mlp_back(0, dx)
    if fast:
        second.start(*grads["m0"])
        first.both_added(*order.fuse([first.both()], "add_both_1", grid=(4,)))
        second.core_added(*order.fuse([second.core()], "add_core_2", grid=(4,)))
    last = (labels, d0, latents, dhead, small["m0"], small["m1"], small["a1"], small_head, small["f0"], small["f1"])
    attention_back(0, dmid, last)
    if fast:
        third.start(*grads["a0"])
        second.both_added(*order.fuse([second.both()], "add_both_2", grid=(4,)))
        first.ring_added(*order.fuse([first.ring()], "add_ring_1"))
        third.core_added(*order.fuse([third.core()], "add_core_3", grid=(4,)))
        second.ring_added(*order.fuse([second.ring()], "add_ring_2"))
        third.both_added(*order.fuse([third.both()], "add_both_3", grid=(4,)))
        upper, lower = Owned(first), Owned(second, third)
        upper.last_added(*order.fuse([upper.last()], "add_last_1"))
        third.ring_added(*order.fuse([third.ring()], "add_ring_3"))
        upper.adam(order, place, states, bufs, "adam_1")
        lower.last_added(*order.fuse([lower.last()], "add_last_0"))
        (loss,) = lower.adam(order, place, states, bufs, "adam_0")
        loss_sum = loss[0, 0]
        results = [bufs[name] for name in ("mats", "down", "skip", "tables", "vectors")]
        results[3] = [part.T for part in results[3]]
    else:
        loss_sum = lax.psum(small_head[2, 0], ALL)
        g_mats, g_down, g_skip, g_turned = reduce_any(grads)
        g_rows = g_turned.T
        g_tables = jnp.concatenate(
            [g_rows[ROW_PATCH:ROW_HEAD], g_rows[NP : NP + 2], g_rows[:NP], g_rows[ROW_HEAD:ROW_VEC]]
        )
        g_vectors = g_rows[ROW_VEC : ROW_VEC + N_VEC]
        results = [
            adam_update(layer_mats, g_mats, layer_mats_first, layer_mats_second, step_rates[0]),
            adam_update(down_mats, g_down, down_first, down_second, step_rates[1]),
            adam_update(skip_mat, g_skip, skip_first, skip_second, step_rates[2]),
            adam_update(tables, g_tables, tables_first, tables_second, step_rates[3]),
            adam_update(vectors, g_vectors, vectors_first, vectors_second, step_rates[4]),
        ]
    return (loss_sum, weight_total[0, 0], *(part for result in results for part in result))


GATHER_CHUNKS = (("a0", "t"), ("m0",), ("a1", "s"), ("m1",))
REDUCE_CHUNKS = (("m1", "a1", "s"), ("m0",), ("a0", "t"))


def solution(mesh):
    one, two, rows = P(None, "shard", None), P("shard", None), P(None, "shard")
    every = P(ALL, None, None)
    placed = (every, every, P(ALL), P(ALL), P(ALL), *[one] * 6, *[two] * 3, *[rows] * 6)
    fast = mesh.shape["rep"] == 4 and mesh.shape["shard"] == 8
    return jax.shard_map(
        functools.partial(local, fast),
        mesh=mesh,
        in_specs=placed,
        out_specs=(P(), P(), *[one] * 8, *[two] * 4, *[rows] * 8),
        check_vma=False,
    )
```

```python
import functools
import math

import jax
import jax.numpy as jnp
from jax import lax
from jax.experimental import pallas as pl
from jax.experimental.pallas import tpu as pltpu
from jax.sharding import PartitionSpec as P

D = 512
HEADS = 8
HD = 64
FF = 2048
CH = 16
NP = 256
CLASSES = 16
LAYERS = 2
STEP = 10
SEQ_LEN = 258

beta_one = 0.5
beta_two = 0.75
epsilon = 1e-08
weight_decay = 0.05
step_rates = (0.05, 0.03, 0.03, 0.05, 0.3)

TAIL = 16
T = NP + TAIL
ROW_PATCH = T
ROW_CLASS = ROW_PATCH + CH
ROW_HEAD = ROW_CLASS + CLASSES
ROW_VEC = ROW_HEAD + CH
N_VEC = LAYERS * (6 + FF // D) + 4
ROWS = D
ROW_WEIGHT = ROWS - 1
ROW_LOSS = 384
bf16 = jnp.bfloat16
f32 = jnp.float32
ALL = ("rep", "shard")
MIB = 1024 * 1024
MARGIN = 6 * MIB
WIDE = ("pack_0", "join_ring_0")
ANY = pl.BlockSpec(memory_space=pl.ANY)
SMEM = pl.BlockSpec(memory_space=pltpu.SMEM)
WHOLE = pl.BlockSpec(memory_space=pltpu.VMEM)


def room(shape, dtype):
    size = jnp.dtype(dtype).itemsize
    rows, columns = ((1,) + tuple(shape))[-2:]
    rows, columns = -(-rows * size // 32) * 32 // size, -(-columns // 128) * 128
    return math.prod(shape[:-2]) * rows * columns * size


class Part:
    def __init__(self, body, inputs, in_specs, outs, out_specs, scratch=()):
        self.body, self.inputs, self.in_specs = body, list(inputs), list(in_specs)
        self.outs, self.out_specs, self.scratch = list(outs), list(out_specs), list(scratch)


class Order:
    def __init__(self):
        self.last = None

    def __call__(self, kernel, inputs, in_specs, outs, out_specs, scratch=(), grid=(1,), name=None, aliases=None):
        part = Part(kernel, inputs, in_specs, outs, out_specs, scratch)
        return self.fuse([part], name, grid=grid, aliases=aliases)[0]

    def fuse(self, parts, name, after=(), grid=(1,), aliases=None):
        extra = list(after) + ([] if self.last is None else [self.last])
        inputs = [value for part in parts for value in part.inputs]
        counts = [(len(p.inputs), len(p.outs), len(p.scratch)) for p in parts]
        ends = [sum(c[i] for c in counts) for i in range(3)]
        skip = len(extra)

        def body(*refs):
            groups = (refs[: ends[0]], refs[ends[0] + skip : ends[0] + skip + ends[1]], refs[ends[0] + skip + ends[1] :])
            at = [0, 0, 0]
            rest = []
            for part, count in zip(parts, counts):
                own = [r for i in range(3) for r in groups[i][at[i] : at[i] + count[i]]]
                at = [i + n for i, n in zip(at, count)]
                more = part.body(*own)
                if more is not None:
                    next(more)
                    rest.append(more)
            for more in rest:
                next(more, None)

        need = 0
        for part in parts:
            for spec, value in (*zip(part.in_specs, part.inputs), *zip(part.out_specs, part.outs)):
                if spec is not ANY and spec is not SMEM:
                    need += 2 * room(spec.block_shape or value.shape, value.dtype)
            need += sum(room(item.shape, item.dtype) for item in part.scratch if hasattr(item, "inner_aval") or hasattr(item, "shape"))
        result = pl.pallas_call(
            body,
            grid=grid,
            in_specs=[spec for part in parts for spec in part.in_specs] + [ANY] * skip,
            out_specs=[spec for part in parts for spec in part.out_specs],
            out_shape=[out for part in parts for out in part.outs],
            scratch_shapes=[item for part in parts for item in part.scratch],
            input_output_aliases=aliases or {},
            cost_estimate=pl.CostEstimate(flops=50_000_000_000, bytes_accessed=100_000_000, transcendentals=0),
            compiler_params=pltpu.CompilerParams(vmem_limit_bytes=56 * MIB if name in WIDE else min(need + MARGIN, 56 * MIB)),
            name=name,
        )(*inputs, *extra)
        self.last = result[0]
        split, at = [], 0
        for part in parts:
            split.append(result[at : at + len(part.outs)])
            at += len(part.outs)
        return split


def dot(left, right):
    return jnp.dot(left, right, preferred_element_type=f32)


def dot_t(left, right):
    return lax.dot_general(left, right, (((1,), (1,)), ((), ())), preferred_element_type=f32)


def t_dot(left, right):
    return lax.dot_general(left, right, (((0,), (0,)), ((), ())), preferred_element_type=f32)


def norm_hat(stream):
    center = jnp.mean(stream, -1, keepdims=True)
    offset = stream - center
    spread = jnp.mean(offset * offset, -1, keepdims=True)
    inverse = lax.rsqrt(spread + 1e-05)
    return (offset * inverse, inverse)


def norm_back(hat, inverse, gain, grad):
    scaled = grad * gain
    first = jnp.mean(scaled, -1, keepdims=True)
    second = jnp.mean(scaled * hat, -1, keepdims=True)
    return inverse * (scaled - first - hat * second)


def rows_sum(values):
    return jnp.sum(values, 0, keepdims=True)


LSE = 16


def apart(rows, scale):
    lane = lax.broadcasted_iota(jnp.int32, (1, 2 * HD), 1)
    return jnp.concatenate([rows * jnp.where(lane // HD == e, scale, 0.0).astype(bf16) for e in range(2)], 0)


def block_mask():
    row = lax.broadcasted_iota(jnp.int32, (TAIL, D), 0)
    lane = lax.broadcasted_iota(jnp.int32, (TAIL, D), 1)
    return (row // 2 == lane // HD, row % 2 == 0)


def spread_tail(rows, scale):
    own, first = block_mask()
    wide = rows.astype(f32)
    both = jnp.where(first, wide[0:1], wide[1:2]) * scale
    return jnp.where(own, both, 0.0).astype(bf16)


def gather_tail(values):
    own, first = block_mask()
    kept = jnp.where(own, values, 0.0)
    zero = rows_sum(jnp.where(first, kept, 0.0))
    one = rows_sum(jnp.where(first, 0.0, kept))
    row = lax.broadcasted_iota(jnp.int32, (TAIL, D), 0)
    return jnp.where(row == 0, zero, jnp.where(row == 1, one, 0.0))


def mask_keys(scores):
    tail = scores[NP:]
    row = lax.broadcasted_iota(jnp.int32, tail.shape, 0)
    return jnp.concatenate([scores[:NP], jnp.where(row < SEQ_LEN - NP, tail, -1e30)], 0)


def softmax_rows(scores):
    top = jnp.max(scores, 0, keepdims=True)
    expon = jnp.exp(scores - top)
    total = jnp.sum(expon, 0, keepdims=True)
    return (expon * (1.0 / total)).astype(bf16), top + jnp.log(total)


def pipelined(count, *stages):
    held = {}
    for step in range(count + len(stages) - 1):
        for i, stage in enumerate(stages):
            if 0 <= step - i < count:
                held[step - i] = stage(step - i, held.get(step - i))


def attention_forward(stream, layer_id, vec_ref, wa_ref, h_ref, qkv_ref, lse_ref, o_ref, mid_ref):
    base = layer_id * (6 + FF // D)
    hat, _ = norm_hat(stream)
    normed = (hat * vec_ref[base : base + 1] + vec_ref[base + 1 : base + 2]).astype(bf16)
    h_ref[0] = normed
    qkv_ref[0] = dot(normed, wa_ref[:, : 3 * D]).astype(bf16)
    scale = HD**-0.5

    def cut(part, pair):
        return qkv_ref[0, :, part * D + 128 * pair : part * D + 128 * pair + 128]

    def score(pair, _):
        return dot_t(cut(1, pair), apart(cut(0, pair)[:NP], scale))

    def weigh(pair, scores):
        weights, log_total = softmax_rows(mask_keys(scores))
        lse_ref[0, 2 * pair : 2 * pair + 1] = log_total[:, :NP]
        lse_ref[0, 2 * pair + 1 : 2 * pair + 2] = log_total[:, NP:]
        return weights

    def mix(pair, weights):
        values = apart(cut(2, pair), 1.0)
        out = t_dot(weights[:, :NP], values[:T]) + t_dot(weights[:, NP:], values[T:])
        o_ref[0, :NP, 128 * pair : 128 * pair + 128] = out.astype(bf16)

    tails = spread_tail(qkv_ref[0, NP:, :D], scale)
    weights, log_total = softmax_rows(mask_keys(dot_t(qkv_ref[0, :, D : 2 * D], tails)))
    lse_ref[0, HEADS : HEADS + 1, :TAIL] = log_total
    o_ref[0, NP:] = gather_tail(t_dot(weights, qkv_ref[0, :, 2 * D :])).astype(bf16)
    pipelined(HEADS // 2, score, weigh, mix)
    mid_ref[0] = stream + dot(o_ref[0], wa_ref[:, 3 * D :]) + vec_ref[base + 4 : base + 5]


def embed_attention_kernel(
    label_ref, latent_ref, time_ref, tab_ref, vec_ref, wa_ref, x_ref, h_ref, qkv_ref, lse_ref, o_ref, mid_ref
):
    b = pl.program_id(0)
    patch_rows = t_dot(latent_ref[0], tab_ref[ROW_PATCH:ROW_CLASS]) + vec_ref[N_VEC - 1 : N_VEC]
    row = lax.broadcasted_iota(jnp.int32, (TAIL, CLASSES), 0)
    column = lax.broadcasted_iota(jnp.int32, (TAIL, CLASSES), 1)
    choose = jnp.where((row == 1) & (column == label_ref[b]), 1.0, 0.0).astype(bf16)
    tail_rows = time_ref[0] + dot(choose, tab_ref[ROW_CLASS:ROW_HEAD])
    stream = jnp.concatenate([patch_rows, tail_rows], 0) + tab_ref[:T].astype(f32)
    x_ref[0] = stream
    attention_forward(stream, 0, vec_ref, wa_ref, h_ref, qkv_ref, lse_ref, o_ref, mid_ref)


def skip_attention_kernel(x1_ref, x0_ref, ws_ref, vec_ref, wa_ref, x_ref, h_ref, qkv_ref, lse_ref, o_ref, mid_ref):
    one = x1_ref[0].astype(bf16)
    zero = x0_ref[0].astype(bf16)
    halves = [dot(one, ws_ref[i, :D]) + dot(zero, ws_ref[i, D:]) for i in range(2)]
    stream = jnp.concatenate(halves, 1) + vec_ref[N_VEC - 2 : N_VEC - 1]
    x_ref[0] = stream
    attention_forward(stream, 1, vec_ref, wa_ref, h_ref, qkv_ref, lse_ref, o_ref, mid_ref)


def mlp_forward(layer_id, mid_ref, vec_ref, w1_ref, w2_ref, h_ref, act_ref, slope_ref):
    base = layer_id * (6 + FF // D)
    hat, _ = norm_hat(mid_ref[...])
    normed = (hat * vec_ref[base + 2 : base + 3] + vec_ref[base + 3 : base + 4]).astype(bf16)
    h_ref[...] = normed
    const = math.sqrt(2.0 / math.pi)

    for j in range(FF // D):
        cols = slice(D * j, D * j + D)
        pre = dot(normed, w1_ref[:, cols]) + vec_ref[base + 6 + j : base + 7 + j]
        square = pre * pre
        half = 0.5 + 0.5 * jnp.tanh(pre * (const + (const * 0.044715) * square))
        act = pre * half
        act_ref[:, cols] = act.astype(bf16)
        slope = half + act * (1.0 - half) * (2.0 * const + (6.0 * const * 0.044715) * square)
        slope_ref[:, cols] = slope.astype(bf16)
    total = jnp.concatenate([dot(act_ref[...], w2_ref[i]) for i in range(2)], 1)
    return mid_ref[...] + total + vec_ref[base + 5 : base + 6]


def mlp_kernel(layer_id, mid_ref, vec_ref, w1_ref, w2_ref, h_ref, act_ref, slope_ref, out_ref):
    out_ref[...] = mlp_forward(layer_id, mid_ref, vec_ref, w1_ref, w2_ref, h_ref, act_ref, slope_ref)


def mlp_head_kernel(
    total_ref,
    weight_ref,
    mid_ref,
    vec_ref,
    w1_ref,
    w2_ref,
    noise_ref,
    tab_ref,
    h_ref,
    act_ref,
    slope_ref,
    dx_ref,
    dhead_ref,
    small_ref,
):
    b = pl.program_id(0)

    @pl.when(b == 0)
    def _():
        dhead_ref[...] = jnp.zeros_like(dhead_ref)
        small_ref[...] = jnp.zeros_like(small_ref)

    out = mlp_forward(1, mid_ref, vec_ref, w1_ref, w2_ref, h_ref, act_ref, slope_ref)
    hat, inverse = norm_hat(out[:NP])
    gain = vec_ref[N_VEC - 4 : N_VEC - 3]
    final = (hat * gain + vec_ref[N_VEC - 3 : N_VEC - 2]).astype(bf16)
    head = tab_ref[ROW_HEAD:ROW_VEC]
    errors = dot_t(head, final) - noise_ref[0].astype(f32)
    per_seq = jnp.sum(errors * errors) * (1.0 / (CH * NP))
    weight = weight_ref[b].astype(f32)
    scale = (jnp.ones((1, 1), f32) / total_ref[0, 0]) * weight * (2.0 / (CH * NP))
    grad_pred = (scale * errors).astype(bf16)
    dhead_ref[...] += dot(grad_pred, final)
    grad = t_dot(grad_pred, head)
    small_ref[0:1] += rows_sum(grad * hat)
    small_ref[1:2] += rows_sum(grad)
    small_ref[2:3] += jnp.full((1, D), weight * per_seq, f32)
    dx_ref[:NP] = norm_back(hat, inverse, gain, grad)
    dx_ref[NP:] = jnp.zeros((TAIL, D), f32)


def rows_of(b):
    return pl.ds(pl.multiple_of(T * b, TAIL), T)


def coords(c_ref):
    return tuple(c_ref[i] for i in range(4))


def place_of(c_ref, shard):
    _, _, z, y = coords(c_ref)
    return ((shard % 2) ^ y, (shard // 2 - z) & 3)


def sub_of(c_ref, h, t, g):
    x, c, _, _ = coords(c_ref)
    return 4 * (c ^ h) + 2 * t + (g ^ x)


def scatter_pieces(c_ref, keep_ref, send_ref, at, piece):
    for h, dest in ((0, keep_ref), (1, send_ref)):
        for t in range(2):
            for g in range(2):
                j = sub_of(c_ref, h, t, g)
                for s in range(8):
                    f, k = place_of(c_ref, s)
                    value = piece(j, s)
                    dest[t, g, f, k, at : at + value.shape[0]] = value


def by_columns(ref):
    return lambda j, s: ref[64 * s : 64 * s + 64, pl.ds(pl.multiple_of(256 * j, 256), 256)]


def by_rows(ref):
    return lambda j, s: ref[pl.ds(pl.multiple_of(64 * j, 64), 64), 256 * s : 256 * s + 256]


def mlp_backward_kernel(
    layer_id,
    c_ref,
    dout_ref,
    act_ref,
    slope_ref,
    h_ref,
    mid_ref,
    vec_ref,
    w1_ref,
    w2_ref,
    dmid_ref,
    keep_ref,
    send_ref,
    small_ref,
    dfc1b_ref,
    left_s,
    right_s,
    grads_s,
    acts_s,
    tile_s,
):
    b = pl.program_id(0)
    base = layer_id * (6 + FF // D)
    size = dout_ref.shape[0]

    @pl.when(b == 0)
    def _():
        small_ref[...] = jnp.zeros_like(small_ref)
        dfc1b_ref[...] = jnp.zeros_like(dfc1b_ref)

    dout = dout_ref[...]
    low = dout.astype(bf16)
    rows = pl.ds(pl.multiple_of(size * b, TAIL), size)
    left_s[rows] = h_ref[...]
    right_s[rows] = low
    acts_s[rows] = act_ref[...]

    def enter(j, _):
        block = slice(D * j, D * j + D)
        return dot_t(low[:, :256], w2_ref[0, block]) + dot_t(low[:, 256:], w2_ref[1, block])

    def bend(j, grad_act):
        cols = slice(D * j, D * j + D)
        grad_pre = grad_act * slope_ref[:, cols].astype(f32)
        dfc1b_ref[:, cols] += rows_sum(grad_pre)
        grad = grad_pre.astype(bf16)
        grads_s[rows, cols] = grad
        return grad

    total = []

    def leave(j, grad):
        part = dot_t(grad, w1_ref[:, D * j : D * j + D])
        total.append(part if not total else total[-1] + part)

    pipelined(FF // D, enter, bend, leave)
    grad_normed = total[-1]
    hat, inverse = norm_hat(mid_ref[...])
    small_ref[0:1] += rows_sum(grad_normed * hat)
    small_ref[1:2] += rows_sum(grad_normed)
    small_ref[2:3] += rows_sum(dout)
    dmid_ref[...] = dout + norm_back(hat, inverse, vec_ref[base + 2 : base + 3], grad_normed)

    @pl.when(b == pl.num_programs(0) - 1)
    def _():
        tile_s[...] = t_dot(left_s[...], grads_s[...]).astype(bf16)
        scatter_pieces(c_ref, keep_ref, send_ref, 0, by_columns(tile_s))
        tile_s[...] = t_dot(right_s[...], acts_s[...]).astype(bf16)
        scatter_pieces(c_ref, keep_ref, send_ref, 64, by_rows(tile_s))


def last_backward_kernel(
    layer_id,
    c_ref,
    dmid_ref,
    x_ref,
    h_ref,
    qkv_ref,
    lse_ref,
    o_ref,
    vec_ref,
    wa_ref,
    label_ref,
    d0_ref,
    latent_ref,
    dhead_ref,
    small_m0,
    small_m1,
    small_a1,
    small_head,
    dfc1b0,
    dfc1b1,
    keep_ref,
    send_ref,
    left_s,
    outs_s,
    grads_s,
    lows_s,
    dqkv_s,
    tile_s,
    small_ref,
    table_s,
):
    b = pl.program_id(0)

    @pl.when(b == 0)
    def _():
        table_s[...] = jnp.zeros_like(table_s)

    refs = (dmid_ref, x_ref, h_ref, qkv_ref, lse_ref, o_ref, vec_ref, wa_ref, small_ref, left_s, outs_s, grads_s, lows_s, dqkv_s)
    embed_grads(b, label_ref, attention_backward(layer_id, *refs) + d0_ref[0], latent_ref, table_s)

    @pl.when(b == pl.num_programs(0) - 1)
    def _():
        attention_weights(c_ref, keep_ref, send_ref, left_s, outs_s, grads_s, lows_s, tile_s)
        table_s[ROW_HEAD:ROW_VEC] = dhead_ref[...]
        row = ROW_VEC
        for own, mlp, fc1b in ((small_ref, small_m0, dfc1b0), (small_a1, small_m1, dfc1b1)):
            table_s[row : row + 2] = own[0:2]
            table_s[row + 2 : row + 4] = mlp[0:2]
            table_s[row + 4 : row + 5] = own[2:3]
            table_s[row + 5 : row + 6] = mlp[2:3]
            for i in range(FF // D):
                table_s[row + 6 + i : row + 7 + i] = fc1b[:, D * i : D * i + D]
            row += 6 + FF // D
        table_s[row : row + 2] = small_head[0:2]
        table_s[row + 2 : row + 3] = small_a1[3:4]
        table_pieces(c_ref, small_head[2:3, 0:1], table_s[...], keep_ref, send_ref, 64)


def attention_backward(
    layer_id, dmid_ref, x_ref, h_ref, qkv_ref, lse_ref, o_ref, vec_ref, wa_ref, small_ref, left_s, outs_s, grads_s, lows_s, dqkv_s
):
    b = pl.program_id(0)
    rows = rows_of(b)
    base = layer_id * (6 + FF // D)

    @pl.when(b == 0)
    def _():
        small_ref[...] = jnp.zeros_like(small_ref)

    dmid = dmid_ref[0]
    low = dmid.astype(bf16)
    left_s[rows] = h_ref[0]
    outs_s[rows] = o_ref[0]
    lows_s[rows] = low
    grad_att = dot_t(low, wa_ref[:, 3 * D :]).astype(bf16)
    scale = HD**-0.5

    def cut(part, pair):
        return qkv_ref[0, :, part * D + 128 * pair : part * D + 128 * pair + 128]

    def put(part, pair, value):
        dqkv_s[: value.shape[0], part * D + 128 * pair : part * D + 128 * pair + 128] = value.astype(bf16)

    tails, tail_douts = spread_tail(qkv_ref[0, NP:, :D], scale), spread_tail(grad_att[NP:], 1.0)
    weights = jnp.exp(mask_keys(dot_t(qkv_ref[0, :, D : 2 * D], tails)) - lse_ref[0, HEADS : HEADS + 1, :TAIL])
    grad_w = dot_t(qkv_ref[0, :, 2 * D :], tail_douts)
    grad_s = (weights * (grad_w - rows_sum(weights * grad_w))).astype(bf16)
    tail_dk = dot(grad_s, tails)
    tail_dv = dot(weights.astype(bf16), tail_douts)
    dqkv_s[NP:, :D] = (gather_tail(t_dot(grad_s, qkv_ref[0, :, D : 2 * D])) * scale).astype(bf16)

    def score(pair, _):
        queries = apart(cut(0, pair)[:NP], scale)
        douts = apart(grad_att[:NP, 128 * pair : 128 * pair + 128], 1.0)
        return dot_t(cut(1, pair), queries), dot_t(cut(2, pair), douts), queries, douts

    def weigh(pair, held):
        scores, grad_w, queries, douts = held
        log_total = jnp.concatenate([lse_ref[0, 2 * pair + e : 2 * pair + e + 1] for e in range(2)], 1)
        weights = jnp.exp(mask_keys(scores) - log_total)
        grad_s = weights * (grad_w - rows_sum(weights * grad_w))
        return weights.astype(bf16), grad_s.astype(bf16), queries, douts

    def mix(pair, held):
        weights, grad_s, queries, douts = held
        cols = slice(128 * pair, 128 * pair + 128)
        keys = apart(cut(1, pair), scale)
        put(0, pair, t_dot(grad_s[:, :NP], keys[:T]) + t_dot(grad_s[:, NP:], keys[T:]))
        put(1, pair, dot(grad_s, queries) + tail_dk[:, cols])
        put(2, pair, dot(weights, douts) + tail_dv[:, cols])

    pipelined(HEADS // 2, score, weigh, mix)
    grads_s[rows] = dqkv_s[...]
    grad_normed = dot_t(dqkv_s[...], wa_ref[:, : 3 * D])
    hat, inverse = norm_hat(x_ref[0])
    small_ref[0:1] += rows_sum(grad_normed * hat)
    small_ref[1:2] += rows_sum(grad_normed)
    small_ref[2:3] += rows_sum(dmid)
    return dmid + norm_back(hat, inverse, vec_ref[base : base + 1], grad_normed)


def attention_weights(c_ref, keep_ref, send_ref, left_s, outs_s, grads_s, lows_s, tile_s):
    tile_s[:, : 3 * D] = t_dot(left_s[...], grads_s[...]).astype(bf16)
    tile_s[:, 3 * D :] = t_dot(outs_s[...], lows_s[...]).astype(bf16)
    scatter_pieces(c_ref, keep_ref, send_ref, 0, by_columns(tile_s))


def middle_backward_kernel(
    layer_id,
    c_ref,
    dmid_ref,
    x_ref,
    h_ref,
    qkv_ref,
    lse_ref,
    o_ref,
    vec_ref,
    wa_ref,
    x1_ref,
    x0_ref,
    ws_ref,
    keep_ref,
    send_ref,
    d1_ref,
    d0_ref,
    small_ref,
    left_s,
    outs_s,
    grads_s,
    lows_s,
    dqkv_s,
    tile_s,
    both_s,
    skip_s,
    skip_tile_s,
):
    b = pl.program_id(0)
    refs = (dmid_ref, x_ref, h_ref, qkv_ref, lse_ref, o_ref, vec_ref, wa_ref, small_ref)
    grad = attention_backward(layer_id, *refs, left_s, outs_s, grads_s, lows_s, dqkv_s)
    low = grad.astype(bf16)
    small_ref[3:4] += rows_sum(grad)
    rows = rows_of(b)
    both_s[rows, :D] = x1_ref[0].astype(bf16)
    both_s[rows, D:] = x0_ref[0].astype(bf16)
    skip_s[rows] = low
    for u, dest in ((0, d1_ref), (1, d0_ref)):
        cols = slice(D * u, D * u + D)
        dest[0] = dot_t(low[:, :256], ws_ref[0, cols]) + dot_t(low[:, 256:], ws_ref[1, cols])

    @pl.when(b == pl.num_programs(0) - 1)
    def _():
        attention_weights(c_ref, keep_ref, send_ref, left_s, outs_s, grads_s, lows_s, tile_s)
        skip_tile_s[...] = t_dot(both_s[...], skip_s[...]).astype(bf16)
        for half in range(2):

            def piece(j, s, half=half):
                rows = pl.ds(pl.multiple_of(128 * s + 16 * j, 16), 16)
                return skip_tile_s[rows, 256 * half : 256 * half + 256]

            scatter_pieces(c_ref, keep_ref, send_ref, 64 + 16 * half, piece)


def embed_grads(b, label_ref, grad, latent_ref, table_s):
    table_s[:T] += grad
    patch = grad[:NP]
    last = ROW_VEC + N_VEC - 1
    table_s[last : last + 1] += rows_sum(patch)
    table_s[ROW_PATCH:ROW_CLASS] += dot(latent_ref[0], patch.astype(bf16))
    row = lax.broadcasted_iota(jnp.int32, (CLASSES, D), 0)
    table_s[ROW_CLASS:ROW_HEAD] += jnp.where(row == label_ref[b], grad[NP + 1 : NP + 2], 0.0)


def table_pieces(c_ref, loss, table, keep_ref, send_ref, at):
    x, c, z, y = coords(c_ref)
    me = (x * 2 + c) * 8 + z * 2 + y
    high = loss.astype(bf16).astype(f32)
    middle = (loss - high).astype(bf16).astype(f32)
    small = loss - high - middle
    row = lax.broadcasted_iota(jnp.int32, (ROWS, D), 0)
    kind = lax.broadcasted_iota(jnp.int32, (ROWS, D), 1) % 8
    slots = jnp.where(kind == 0, high, jnp.where(kind == 1, middle, jnp.where(kind == 2, small, 0.0)))
    turned = jnp.where(row == ROW_LOSS + me, slots, table).T
    for s in range(8):
        f, k = place_of(c_ref, s)
        for j in range(8):
            rows = slice(64 * s + 8 * j, 64 * s + 8 * j + 8)
            piece = jnp.concatenate([turned[rows, :256], turned[rows, 256:]], 0).astype(bf16)
            h, t, g = (j // 4) ^ c, j // 2 % 2, (j % 2) ^ x

            @pl.when(h == 0)
            def _(piece=piece, t=t, g=g, f=f, k=k):
                keep_ref[t, g, f, k, at : at + 16] = piece

            @pl.when(h == 1)
            def _(piece=piece, t=t, g=g, f=f, k=k):
                send_ref[t, g, f, k, at : at + 16] = piece


def per_seq(width, rows=T):
    return pl.BlockSpec((1, rows, width), lambda b: (b, 0, 0))


def fixed(shape):
    return pl.BlockSpec(shape, lambda b: (0,) * len(shape))


def shape_of(shape, dtype=f32):
    return jax.ShapeDtypeStruct(shape, dtype)


def pieces_shape(rows):
    return (2, 2, 2, 4, rows, 256)


def call_attention(order, first, n_seqs, inputs):
    shapes = [(T, D, f32), (T, D, bf16), (T, 3 * D, bf16), (LSE, NP, f32), (T, D, bf16), (T, D, f32)]
    vec_spec, wa_spec = fixed((N_VEC, D)), fixed((D, 4 * D))
    if first:
        in_specs = [SMEM, per_seq(NP, CH), per_seq(D, TAIL), fixed((ROWS, D)), vec_spec, wa_spec]
    else:
        in_specs = [per_seq(D), per_seq(D), fixed((2, 2 * D, D // 2)), vec_spec, wa_spec]
    return order(
        embed_attention_kernel if first else skip_attention_kernel,
        inputs,
        in_specs,
        [shape_of((n_seqs, r, w), d) for r, w, d in shapes],
        [per_seq(w, r) for r, w, _ in shapes],
        grid=(n_seqs,),
        name="attention_forward_%d" % (0 if first else 1),
    )


MLP_STEPS = 4


def flat(width, rows):
    return pl.BlockSpec((rows, width), lambda b: (b, 0))


def call_mlp(order, layer_id, n_seqs, mid, vec, w1, w2, head=None):
    shapes = [(D, bf16), (FF, bf16), (FF, bf16), (D, f32)]
    whole = n_seqs * T
    size = T if head else whole // MLP_STEPS
    inputs = [mid.reshape(whole, D), vec, w1, w2]
    specs = [flat(D, size), fixed((N_VEC, D)), fixed((D, FF)), fixed((2, FF, D // 2))]
    outs = [shape_of((whole, w), d) for w, d in shapes]
    out_specs = [flat(w, size) for w, _ in shapes]
    kernel = functools.partial(mlp_kernel, layer_id)
    if head:
        total, weights, noise, tab = head
        kernel = mlp_head_kernel
        inputs = [total, weights, *inputs, noise, tab]
        specs = [SMEM, SMEM, *specs, per_seq(NP, CH), fixed((ROWS, D))]
        outs += [shape_of((CH, D)), shape_of((8, D))]
        out_specs += [fixed((CH, D)), fixed((8, D))]
    out = order(kernel, inputs, specs, outs, out_specs, grid=(whole // size,), name="mlp_forward_%d" % layer_id)
    return [*out[:3], out[3].reshape(n_seqs, T, D), *out[4:]]


def call_mlp_backward(order, layer_id, n_seqs, place, dout, act, slope, normed, mid, vec, w1, w2):
    whole = n_seqs * T
    size = whole // MLP_STEPS
    pieces = pieces_shape(128)
    out = order(
        functools.partial(mlp_backward_kernel, layer_id),
        (place, dout.reshape(whole, D), act, slope, normed, mid.reshape(whole, D), vec, w1, w2),
        [SMEM, flat(D, size), flat(FF, size), flat(FF, size), flat(D, size), flat(D, size)]
        + [fixed((N_VEC, D)), fixed((D, FF)), fixed((2, FF, D // 2))],
        [shape_of((whole, D)), shape_of(pieces, bf16), shape_of(pieces, bf16), shape_of((8, D)), shape_of((1, FF))],
        [flat(D, size), fixed(pieces), fixed(pieces), fixed((8, D)), fixed((1, FF))],
        [
            pltpu.VMEM((whole, D), bf16),
            pltpu.VMEM((whole, D), bf16),
            pltpu.VMEM((whole, FF), bf16),
            pltpu.VMEM((whole, FF), bf16),
            pltpu.VMEM((D, FF), bf16),
        ],
        grid=(MLP_STEPS,),
        name="mlp_backward_%d" % layer_id,
    )
    return [out[0].reshape(n_seqs, T, D), *out[1:]]


def call_attention_backward(order, layer_id, n_seqs, place, dmid, x, normed, qkv, lse, att, vec, wa, more):
    whole = n_seqs * T
    pieces = pieces_shape(80 if layer_id == 0 else 96)
    specs = [SMEM, per_seq(D), per_seq(D), per_seq(D), per_seq(3 * D), per_seq(NP, LSE), per_seq(D)]
    specs += [fixed((N_VEC, D)), fixed((D, 4 * D))]
    scratch = [
        pltpu.VMEM((whole, D), bf16),
        pltpu.VMEM((whole, D), bf16),
        pltpu.VMEM((whole, 3 * D), bf16),
        pltpu.VMEM((whole, D), bf16),
        pltpu.VMEM((T, 3 * D), bf16),
        pltpu.VMEM((D, 4 * D), bf16),
    ]
    if layer_id == 1:
        kernel = middle_backward_kernel
        specs += [per_seq(D), per_seq(D), fixed((2, 2 * D, D // 2))]
        outs = [shape_of((n_seqs, T, D)), shape_of((n_seqs, T, D)), shape_of((8, D))]
        out_specs = [per_seq(D), per_seq(D), fixed((8, D))]
        scratch += [pltpu.VMEM((whole, 2 * D), bf16), pltpu.VMEM((whole, D), bf16), pltpu.VMEM((2 * D, D), bf16)]
    else:
        kernel = last_backward_kernel
        specs += [SMEM, per_seq(D), per_seq(NP, CH), fixed((CH, D))] + [fixed((8, D))] * 4 + [fixed((1, FF))] * 2
        scratch += [pltpu.VMEM((8, D), f32), pltpu.VMEM((ROWS, D), f32)]
        outs, out_specs = [], []
    return order(
        functools.partial(kernel, layer_id),
        [place, dmid, x, normed, qkv, lse, att, vec, wa, *more],
        specs,
        [shape_of(pieces, bf16), shape_of(pieces, bf16)] + outs,
        [fixed(pieces), fixed(pieces)] + out_specs,
        scratch,
        grid=(n_seqs,),
        name="attention_backward_%d" % layer_id,
    )


def device_id(x, c, z, y):
    return (x * 2 + c) * 8 + z * 2 + y


def pairs(move):
    every = [(x, c, z, y) for x in range(2) for c in range(2) for z in range(4) for y in range(2)]
    return [(device_id(*at), device_id(*move(*at))) for at in every]


TO_CORE = pairs(lambda x, c, z, y: (x, 1 - c, z, y))
TO_X = pairs(lambda x, c, z, y: (1 - x, c, z, y))
TO_Y = pairs(lambda x, c, z, y: (x, c, z, 1 - y))
TO_Z = [pairs(lambda x, c, z, y, k=k: (x, c, (z + k) % 4, y)) for k in range(4)]
PIECE_ROWS = {"a": 64, "m": 128, "s": 32, "t": 16}


def send(value, to):
    return lax.ppermute(value, ALL, to)


def rows_in(kinds):
    return sum(PIECE_ROWS[kind[0]] for kind in kinds)


def pack_kernel(kinds, c_ref, mats_ref, down_ref, skip_ref, tab_ref, vec_ref, weight_ref, u_ref, wide_s, narrow_s, sem):
    x, c, _, _ = coords(c_ref)
    copies, casts = [], []
    wide = narrow = row = 0
    for kind in kinds:
        l = int(kind[1:] or 0)
        if kind[0] in "am":
            for t in range(2):
                start = (2048 if kind[0] == "m" else 0) + 256 * (4 * c + 2 * t + x)
                copies.append((mats_ref.at[l, :, pl.ds(pl.multiple_of(start, 256), 256)], wide_s.at[wide]))
                casts.append((t, row, wide_s.at[wide], None))
                wide += 1
            row += 64
        if kind[0] in "ms":
            size = 32 if kind[0] == "m" else 16
            ref = down_ref.at[l] if kind[0] == "m" else skip_ref
            for t in range(2):
                start = pl.multiple_of(size * (4 * c + 2 * t + x), size)
                copies.append((ref.at[pl.ds(start, size)], narrow_s.at[narrow, :size]))
                for half in range(2):
                    cols = slice(256 * half, 256 * half + 256)
                    casts.append((t, row + size * half, narrow_s.at[narrow, :size], cols))
                narrow += 1
            row += 2 * size
        if kind[0] == "t":
            own_weight = weight_ref[0]
            for i in range(1, weight_ref.shape[0]):
                own_weight += weight_ref[i]
            turned = vec_ref[...].T
            first, last = CH + CLASSES, CH + CLASSES + SEQ_LEN
            corner = (lax.broadcasted_iota(jnp.int32, (16, 256), 0) == 8) & (
                lax.broadcasted_iota(jnp.int32, (16, 256), 1) == 255
            )
            for t in range(2):
                j = 4 * c + 2 * t + x
                table = tab_ref[pl.ds(pl.multiple_of(8 * j, 8), 8)]
                vecs = turned[0:8]
                for i in range(1, 8):
                    vecs = jnp.where(j == i, turned[8 * i : 8 * i + 8], vecs)
                rest = [
                    table[:, first : first + 2],
                    jnp.zeros((8, TAIL - 2), f32),
                    table[:, :first],
                    table[:, last:],
                    vecs,
                    jnp.zeros((8, ROWS - ROW_VEC - N_VEC), f32),
                ]
                piece = jnp.concatenate([table[:, first + 2 : last], jnp.concatenate(rest, 1)], 0)
                if t == 0:
                    piece = jnp.where(corner, own_weight.astype(f32), piece)
                u_ref[t, row : row + 16] = piece.astype(bf16)
            row += 16
    copies = [pltpu.make_async_copy(a, b, sem) for a, b in copies]
    for copy in copies:
        copy.start()
    yield
    for copy in copies:
        copy.wait()
    for t, at, ref, cols in casts:
        value = ref[...] if cols is None else ref[:, cols]
        u_ref[t, at : at + value.shape[0]] = value.astype(bf16)


def join_ring_kernel(u0, u1, u2, u3, b_ref, c_ref):
    for k, ref in enumerate((u0, u1, u2, u3)):
        b_ref[k] = ref[0]
        c_ref[k] = ref[1]


def join_pair_kernel(b0, b1, c0, c1, b_ref, c_ref):
    for i, (b, c) in enumerate(((b0, c0), (b1, c1))):
        b_ref[i] = b[...]
        c_ref[i] = c[...]


def join_own_kernel(b, c, both_ref):
    both_ref[0] = b[...]
    both_ref[1] = c[...]


def assemble_kernel(kinds, c_ref, *refs):
    x, c, z, y = coords(c_ref)
    sources, dests = refs[:6], refs[6:]
    for h in range(2):
        if h == 0:
            own_b, x_b, own_c, y_c = sources[:4]
        else:
            own_b, own_c, x_b, y_c = (sources[4 + i].at[k] for i in range(2) for k in range(2))
        for t in range(2):
            for g in range(2):
                j = 4 * (c ^ h) + 2 * t + (g ^ x)
                cols = pl.ds(pl.multiple_of(256 * j, 256), 256)
                for f in range(2):
                    src = ((own_b, x_b)[g].at[f]) if t == 0 else ((own_c, y_c)[f].at[g])
                    for k in range(4):
                        s = 2 * ((z - k) & 3) + (y ^ f)
                        row = 0
                        at = 0
                        for kind in kinds:
                            if kind[0] in "am":
                                rows = pl.ds(pl.multiple_of(64 * s, 64), 64)
                                dests[at][rows, cols] = src[k, row : row + 64]
                                row, at = row + 64, at + 1
                            if kind[0] in "ms":
                                size = 32 if kind[0] == "m" else 16
                                rows = pl.ds(pl.multiple_of(size * (8 * s + j), size), size)
                                for half in range(2):
                                    dests[at][half, rows] = src[k, row : row + size]
                                    row += size
                                at += 1
                            if kind[0] == "t":
                                both = src[k, row : row + 16].astype(f32)
                                rows = pl.ds(pl.multiple_of(64 * s + 8 * j, 8), 8)
                                dests[-1][rows, :256] = both[:8]
                                dests[-1][rows, 256:] = both[8:]
    if "t" in kinds:
        table_ref, vec_ref, total_ref, turned_s = dests[-4:]
        table = turned_s[...].T
        table_ref[...] = table.astype(bf16)
        vec_ref[...] = table[ROW_VEC : ROW_VEC + N_VEC]
        total_ref[0, 0] = jnp.sum(table[ROW_WEIGHT : ROW_WEIGHT + 1])


def assemble_all_kernel(kinds, source, *dests):
    for x in range(2):
        for c in range(2):
            for s in range(8):
                for t in range(2):
                    j = 4 * c + 2 * t + x
                    src = source.at[8 * (2 * x + c) + s, t]
                    row = at = 0
                    for kind in kinds:
                        if kind[0] in "am":
                            dests[at][64 * s : 64 * s + 64, 256 * j : 256 * j + 256] = src[row : row + 64]
                            row, at = row + 64, at + 1
                        if kind[0] in "ms":
                            size = 32 if kind[0] == "m" else 16
                            for half in range(2):
                                start = size * (8 * s + j)
                                dests[at][half, start : start + size] = src[row : row + size]
                                row += size
                            at += 1


class Gather:
    def __init__(self, place, kinds, sources):
        self.place, self.kinds, self.sources = place, kinds, sources
        self.rows = rows_in(kinds)

    def pack(self):
        return Part(
            functools.partial(pack_kernel, self.kinds),
            (self.place, *self.sources),
            [SMEM, ANY, ANY, ANY] + ([WHOLE, WHOLE, SMEM] if "t" in self.kinds else [ANY] * 3),
            [shape_of((2, self.rows, 256), bf16)],
            [WHOLE],
            [pltpu.VMEM((4, 64, 256), f32), pltpu.VMEM((4, 32, D), f32), pltpu.SemaphoreType.DMA],
        )

    def packed_for_all(self, results):
        self.every = lax.all_gather(results[0], ALL)

    def assemble_all(self):
        shapes = self.shapes()
        return Part(
            functools.partial(assemble_all_kernel, self.kinds), [self.every], [WHOLE], shapes, [WHOLE] * len(shapes)
        )

    def packed(self, results):
        (own,) = results
        self.ring = [own] + [send(own, TO_Z[k]) for k in range(1, 4)]

    def join_ring(self):
        half = shape_of((4, self.rows, 256), bf16)
        return Part(join_ring_kernel, self.ring, [WHOLE] * 4, [half] * 2, [WHOLE] * 2)

    def ring_joined(self, results):
        b, c = results
        self.halves = (b, send(b, TO_Y), c, send(c, TO_X))

    def join_pair(self):
        whole = shape_of((2, 4, self.rows, 256), bf16)
        return Part(join_pair_kernel, self.halves, [WHOLE] * 4, [whole, whole], [WHOLE] * 2)

    def pair_joined(self, results):
        b, c = results
        self.mine = [b, send(b, TO_X), c, send(c, TO_Y)]

    def join_own(self):
        both = shape_of((2, 2, 4, self.rows, 256), bf16)
        return Part(join_own_kernel, (self.mine[0], self.mine[2]), [WHOLE] * 2, [both], [WHOLE])

    def own_joined(self, results):
        self.other = [send(results[0], TO_CORE)]

    def join_rest(self):
        both = shape_of((2, 2, 4, self.rows, 256), bf16)
        return Part(join_own_kernel, (self.mine[1], self.mine[3]), [WHOLE] * 2, [both], [WHOLE])

    def rest_joined(self, results):
        self.other.append(send(results[0], TO_CORE))

    def shapes(self):
        shapes = []
        for kind in self.kinds:
            if kind[0] in "am":
                shapes.append(shape_of((D, 2048), bf16))
            if kind[0] == "m":
                shapes.append(shape_of((2, FF, 256), bf16))
            if kind[0] == "s":
                shapes.append(shape_of((2, 2 * D, 256), bf16))
            if kind[0] == "t":
                shapes += [shape_of((ROWS, D), bf16), shape_of((N_VEC, D)), shape_of((1, 1))]
        return shapes

    def assemble(self):
        shapes = self.shapes()
        scratch = [pltpu.VMEM((D, ROWS), f32)] if "t" in self.kinds else []
        return Part(
            functools.partial(assemble_kernel, self.kinds),
            (self.place, *self.mine, *self.other),
            [SMEM] + [WHOLE] * 6,
            shapes,
            [SMEM if shape.shape == (1, 1) else WHOLE for shape in shapes],
            scratch,
        )


def added(*values):
    total = values[0].astype(f32)
    for value in values[1:]:
        total += value.astype(f32)
    return total.astype(bf16)


def add_core_kernel(n, *refs):
    keeps, gots, (b0_ref, b1_ref, c0_ref, c1_ref) = refs[:n], refs[n : 2 * n], refs[2 * n :]
    row = 0
    for keep, got in zip(keeps, gots):
        rows = slice(row, row + keep.shape[4])
        row = rows.stop
        for i in range(2):
            for dest, at in ((b0_ref, (0, 0, i)), (b1_ref, (0, 1, i)), (c0_ref, (1, i, 0)), (c1_ref, (1, i, 1))):
                dest[i, :, rows] = added(keep[at], got[at])


def add_both_kernel(b0_ref, gb_ref, c0_ref, gc_ref, b_ref, sb_ref, c_ref, sc_ref):
    for keep, got, dests in ((b0_ref, gb_ref, (b_ref, sb_ref)), (c0_ref, gc_ref, (c_ref, sc_ref))):
        for i, dest in enumerate(dests):
            dest[...] = added(keep[i], got[i])


def add_ring_kernel(b_ref, gb_ref, c_ref, gc_ref, *dests):
    for t, (keep, got) in enumerate(((b_ref, gb_ref), (c_ref, gc_ref))):
        for k, dest in enumerate(dests):
            dest[t] = added(keep[k], got[k])


def add_last_kernel(*refs):
    row = 0
    for i in range(0, len(refs) - 1, 4):
        rows = slice(row, row + refs[i].shape[1])
        row = rows.stop
        refs[-1][:, rows] = added(*(ref[...] for ref in refs[i : i + 4]))


class Reduce:
    def __init__(self, kinds):
        self.kinds = kinds
        self.rows = rows_in(kinds)
        self.keep, self.got = [], []

    def start(self, keep, give):
        self.keep.append(keep)
        self.got.append(send(give, TO_CORE))

    def core(self):
        def six(rows):
            return pl.BlockSpec((2, 2, 2, 1, rows, 256), lambda k: (0, 0, 0, k, 0, 0))

        four = pl.BlockSpec((2, 1, self.rows, 256), lambda k: (0, k, 0, 0))
        parts = self.keep + self.got
        return Part(
            functools.partial(add_core_kernel, len(self.keep)),
            parts,
            [six(part.shape[4]) for part in parts],
            [shape_of((2, 4, self.rows, 256), bf16)] * 4,
            [four] * 4,
        )

    def core_added(self, results):
        b0, b1, c0, c1 = results
        self.parts = (b0, send(b1, TO_X), c0, send(c1, TO_Y))

    def both(self):
        four = pl.BlockSpec((2, 1, self.rows, 256), lambda k: (0, k, 0, 0))
        three = pl.BlockSpec((1, self.rows, 256), lambda k: (k, 0, 0))
        return Part(
            add_both_kernel, self.parts, [four] * 4, [shape_of((4, self.rows, 256), bf16)] * 4, [three] * 4
        )

    def both_added(self, results):
        b, sb, c, sc = results
        self.parts = (b, send(sb, TO_Y), c, send(sc, TO_X))

    def ring(self):
        small = shape_of((2, self.rows, 256), bf16)
        return Part(add_ring_kernel, self.parts, [WHOLE] * 4, [small] * 4, [WHOLE] * 4)

    def ring_added(self, results):
        self.parts = [results[0]] + [send(results[k], TO_Z[k]) for k in range(1, 4)]


class Owned:
    def __init__(self, *chunks):
        self.chunks = chunks
        self.kinds = [kind for chunk in chunks for kind in chunk.kinds]

    def last(self):
        parts = [part for chunk in self.chunks for part in chunk.parts]
        out = shape_of((2, rows_in(self.kinds), 256), bf16)
        return Part(add_last_kernel, parts, [WHOLE] * len(parts), [out], [WHOLE])

    def last_added(self, results):
        (mine,) = results
        near = send(mine, TO_X)
        self.parts = (mine, near, send(mine, TO_CORE), send(near, TO_CORE))

    def adam(self, order, place, states, bufs, name):
        inputs, in_specs, outs, out_specs, aliases = [place, *self.parts], [SMEM] + [WHOLE] * 4, [], [], {}
        targets = []
        for kind in self.kinds:
            l = int(kind[1:] or 0)
            if kind[0] == "a":
                targets.append(("mats", "a", pl.BlockSpec((1, 64, 4096), lambda i, l=l: (l, 0, 0))))
            if kind[0] == "m":
                targets.append(("down", "d", pl.BlockSpec((1, 256, D), lambda i, l=l: (l, 0, 0))))
            if kind[0] == "s":
                targets.append(("skip", "s", fixed((128, D))))
            if kind[0] == "t":
                targets.append(("tables", "t", fixed((64, SEQ_LEN + 3 * CH))))
                targets.append(("vectors", "v", fixed((N_VEC, 64))))
        held = []
        for name, _, spec in targets:
            inputs += list(states[name])
            in_specs += [spec] * 3
            weight = states[name][0]
            if bufs.get(name) is not None:
                held += [(len(outs) + i, buf) for i, buf in enumerate(bufs[name])]
            outs += [shape_of(weight.shape)] * 3 + [shape_of(weight.shape, bf16)]
            out_specs += [spec] * 4
        n_read = len(inputs)
        for at, buf in held:
            aliases[len(inputs)] = at
            inputs.append(buf)
            in_specs.append(ANY)
        scratch = []
        if any(t[1] == "d" for t in targets):
            scratch.append(pltpu.VMEM((D, 256), f32))
        if any(t[1] == "t" for t in targets):
            scratch.append(pltpu.VMEM((64, ROWS), f32))
            outs.append(shape_of((1, 1)))
            out_specs.append(SMEM)
        result = order(
            functools.partial(adam_kernel, self.kinds, [t[1] for t in targets], n_read, len(inputs)),
            inputs,
            in_specs,
            outs,
            out_specs,
            scratch,
            name=name,
            aliases=aliases,
        )
        for i, (name, _, _) in enumerate(targets):
            bufs[name] = result[4 * i : 4 * i + 4]
        return result[4 * len(targets) :]


def adam_kernel(kinds, targets, n_read, n_in, c_ref, *refs):
    x, c, _, _ = coords(c_ref)
    parts, ins, outs = refs[:4], refs[4 : n_read - 1], refs[n_in - 1 :]
    scratch = list(outs[4 * len(targets) :])
    loss_ref = scratch.pop(0) if "t" in targets else None
    offsets, row = {}, 0
    for kind in kinds:
        offsets[kind[0]] = row
        row += PIECE_ROWS[kind[0]]
    pieces = []
    for h in range(2):
        for g in range(2):
            for t in range(2):
                pieces.append((4 * (c ^ h) + 2 * t + (g ^ x), parts[2 * h + g].at[t]))
    for i, kind in enumerate(targets):
        state, dests = ins[3 * i : 3 * i + 3], outs[4 * i : 4 * i + 4]
        row = offsets[{"d": "m", "v": "t"}.get(kind, kind)]

        def update(at, grad, rate, state=state, dests=dests):
            weight, first, second = (ref[at] for ref in state)
            values = adam_update(weight, grad, first, second, rate)
            for dest, value in zip(dests, values):
                dest[at] = value

        if kind == "a":
            for at_row, start in ((row, 0), (offsets["m"], 2048)):
                for j, piece in pieces:
                    at = (0, slice(None), pl.ds(pl.multiple_of(start + 256 * j, 256), 256))
                    update(at, piece[at_row : at_row + 64], step_rates[0])
        if kind == "d":
            held = scratch[0]
            for j, piece in pieces:
                held[pl.ds(pl.multiple_of(64 * j, 64), 64)] = piece[row + 64 : row + 128].astype(f32)
            update((0,), held[...].T, step_rates[1])
        if kind == "s":
            for j, piece in pieces:
                for half in range(2):
                    at = (pl.ds(pl.multiple_of(16 * j, 16), 16), slice(256 * half, 256 * half + 256))
                    update(at, piece[row + 16 * half : row + 16 * half + 16], step_rates[2])
        if kind == "t":
            held = scratch[-1]
            for j, piece in pieces:
                both = piece[row : row + 16].astype(f32)
                rows = pl.ds(pl.multiple_of(8 * j, 8), 8)
                held[rows, :256] = both[:8]
                held[rows, 256:] = both[8:]
            grad = held[...]
            parts_of = [grad[:, ROW_PATCH:ROW_HEAD], grad[:, NP : NP + 2], grad[:, :NP], grad[:, ROW_HEAD:ROW_VEC]]
            update(slice(None), jnp.concatenate(parts_of, 1), step_rates[3])
            loss_ref[0, 0] = jnp.sum(grad[0:3, ROW_LOSS : ROW_LOSS + 32])
        if kind == "v":
            grad = scratch[-1][:, ROW_VEC : ROW_VEC + N_VEC].T
            update(slice(None), grad, step_rates[4])


def gather_any(mats, down, skip, tables, vectors):
    first, last = CH + CLASSES, CH + CLASSES + SEQ_LEN
    width = tables.shape[1]
    tab = jnp.concatenate(
        [
            tables[first + 2 : last],
            tables[first : first + 2],
            jnp.zeros((TAIL - 2, width), f32),
            tables[:first],
            tables[last:],
            vectors,
            jnp.zeros((ROWS - ROW_VEC - N_VEC, width), f32),
        ]
    )
    every = lax.all_gather(mats.astype(bf16), "shard", axis=1, tiled=True)
    downs = lax.all_gather(down.astype(bf16), "shard", axis=1, tiled=True)
    skips = lax.all_gather(skip.astype(bf16), "shard", axis=0, tiled=True)
    table = lax.all_gather(tab.astype(bf16), "shard", axis=1, tiled=True)

    def halves(m):
        return jnp.stack([m[:, : D // 2], m[:, D // 2 :]])

    mats_of = [(every[l, :, :2048], every[l, :, 2048:]) for l in range(LAYERS)]
    return (mats_of, [halves(downs[l]) for l in range(LAYERS)], halves(skips), table)


def reduce_any(grads):
    def ordered(kind):
        both = jnp.stack(grads[kind])
        return both.transpose(0, 1, 2, 4, 3, 5, 6).reshape((8, 8) + both.shape[5:])

    def shard_sum(value, axis):
        owned = lax.psum_scatter(value.astype(f32), "shard", scatter_dimension=axis, tiled=True)
        return lax.psum(owned.astype(bf16), "rep")

    mats, down = [], []
    for l in range(LAYERS):
        attn, mlp = ordered("a%d" % l), ordered("m%d" % l)
        both = [part[:, :, :64].transpose(1, 2, 0, 3).reshape(D, 2048) for part in (attn, mlp)]
        mats.append(jnp.concatenate(both, 1))
        down.append(mlp[:, :, 64:].transpose(0, 2, 1, 3).reshape(D, FF).T)
    skip = ordered("a1")[:, :, 64:].reshape(8, 8, 2, 16, 256).transpose(1, 0, 3, 2, 4).reshape(2 * D, D)
    turned = ordered("a0")[:, :, 64:].reshape(8, 8, 2, 8, 256).transpose(1, 0, 3, 2, 4).reshape(D, ROWS)
    return (shard_sum(jnp.stack(mats), 1), shard_sum(jnp.stack(down), 1), shard_sum(skip, 0), shard_sum(turned, 0))


def time_token(timesteps):
    half_width = D // 2
    freqs_row = jnp.exp(-math.log(10000.0) * jnp.arange(half_width, dtype=f32) / half_width)
    angles = timesteps.astype(f32)[:, None] * freqs_row[None, :]
    return jnp.concatenate([jnp.cos(angles), jnp.sin(angles)], -1)


def adam_update(weight, grad, moment_one, moment_two, step_rate):
    grad = grad.astype(f32)
    moment_one = beta_one * moment_one + (1.0 - beta_one) * grad
    moment_two = beta_two * moment_two + (1.0 - beta_two) * grad * grad
    first_hat = moment_one / (1.0 - beta_one**STEP)
    second_hat = moment_two / (1.0 - beta_two**STEP)
    weight = weight - step_rate * (first_hat / (jnp.sqrt(second_hat) + epsilon) + weight_decay * weight)
    return (moment_one, moment_two, weight, weight.astype(bf16))


def local(
    fast,
    latents,
    target_noise,
    labels,
    timesteps,
    loss_weight,
    layer_mats,
    layer_mats_first,
    layer_mats_second,
    down_mats,
    down_first,
    down_second,
    skip_mat,
    skip_first,
    skip_second,
    tables,
    tables_first,
    tables_second,
    vectors,
    vectors_first,
    vectors_second,
):
    n_seqs = latents.shape[0]
    if fast:
        rep, shard = lax.axis_index("rep"), lax.axis_index("shard")
        place = jnp.stack([rep // 2, rep % 2, shard // 2, shard % 2]).astype(jnp.int32)
    else:
        place = jnp.zeros((4,), jnp.int32)
    order = Order()
    time_rows = jnp.pad(time_token(timesteps)[:, None], ((0, 0), (0, TAIL - 1), (0, 0)))
    mats, downs = [None, None], [None, None]
    forward = {}

    def attention(l):
        if l == 0:
            inputs = (labels, latents, time_rows, table, vec, mats[0][0])
        else:
            inputs = (forward["x1"], forward["x0"], ws, vec, mats[1][0])
        forward["a%d" % l] = call_attention(order, l == 0, n_seqs, inputs)
        if l == 0:
            forward["x0"] = forward["a0"][0]

    def mlp(l):
        head = (weight_total, loss_weight, target_noise, table) if l == 1 else None
        out = call_mlp(order, l, n_seqs, forward["a%d" % l][5], vec, mats[l][1], downs[l], head)
        forward["m%d" % l] = out
        forward["x%d" % (l + 1)] = out[3]

    if fast:
        args = (layer_mats, down_mats, skip_mat, tables.T, vectors, loss_weight)
        one, two, three = (Gather(place, kinds, args) for kinds in GATHER_CHUNKS)
        one.packed(*order.fuse([one.pack()], "pack_0"))
        joined, packed = order.fuse([one.join_ring(), two.pack()], "join_ring_0")
        one.ring_joined(joined)
        two.packed(packed)
        one.pair_joined(*order.fuse([one.join_pair()], "join_pair_0"))
        joined, own = order.fuse([two.join_ring(), one.join_own()], "join_ring_1")
        two.ring_joined(joined)
        one.own_joined(own)
        one.rest_joined(*order.fuse([one.join_rest()], "join_rest_0"))
        (wa0, table, vec, weight_total), packed = order.fuse([one.assemble(), three.pack()], "assemble_0")
        mats[0] = (wa0, None)
        three.packed(packed)
        two.pair_joined(*order.fuse([two.join_pair()], "join_pair_1"))
        attention(0)
        joined, own = order.fuse([three.join_ring(), two.join_own()], "join_ring_2")
        three.ring_joined(joined)
        two.own_joined(own)
        two.rest_joined(*order.fuse([two.join_rest()], "join_rest_1"))
        ((w10, downs[0]),) = order.fuse([two.assemble()], "assemble_1")
        mats[0] = (wa0, w10)
        three.pair_joined(*order.fuse([three.join_pair()], "join_pair_2"))
        mlp(0)
        three.own_joined(*order.fuse([three.join_own()], "join_own_2"))
        three.rest_joined(*order.fuse([three.join_rest()], "join_rest_2"))
        ((wa1, ws, w11, downs[1]),) = order.fuse([three.assemble()], "assemble_2")
        mats[1] = (wa1, w11)
        attention(1)
        mlp(1)
    else:
        mats, downs, ws, table = gather_any(layer_mats, down_mats, skip_mat, tables, vectors)
        vec = table[ROW_VEC : ROW_VEC + N_VEC].astype(f32)
        weight_total = lax.psum(jnp.sum(loss_weight.astype(f32)), ALL).reshape(1, 1)
        attention(0)
        mlp(0)
        attention(1)
        mlp(1)

    dx, dhead, small_head = forward["m1"][3:]
    grads, small = {}, {}

    def mlp_back(l, dout):
        normed, act, slope = forward["m%d" % l][:3]
        out = call_mlp_backward(
            order, l, n_seqs, place, dout, act, slope, normed, forward["a%d" % l][5], vec, mats[l][1], downs[l]
        )
        grads["m%d" % l], small["m%d" % l], small["f%d" % l] = out[1:3], out[3], out[4]
        return out[0]

    def attention_back(l, dmid, more):
        x, normed, qkv, lse, att, _ = forward["a%d" % l]
        out = call_attention_backward(order, l, n_seqs, place, dmid, x, normed, qkv, lse, att, vec, mats[l][0], more)
        grads["a%d" % l] = out[:2]
        return out[2:]

    bufs = {}
    if fast:
        first, second, third = (Reduce(kinds) for kinds in REDUCE_CHUNKS)
        states = {
            "mats": (layer_mats, layer_mats_first, layer_mats_second),
            "down": (down_mats, down_first, down_second),
            "skip": (skip_mat, skip_first, skip_second),
            "tables": (tables.T, tables_first.T, tables_second.T),
            "vectors": (vectors, vectors_first, vectors_second),
        }
    dmid = mlp_back(1, dx)
    if fast:
        first.start(*grads["m1"])
    dx, d0, small["a1"] = attention_back(1, dmid, (forward["x1"], forward["x0"], ws))
    if fast:
        first.start(*grads["a1"])
        first.core_added(*order.fuse([first.core()], "add_core_1", grid=(4,)))
    dmid = mlp_back(0, dx)
    if fast:
        second.start(*grads["m0"])
        first.both_added(*order.fuse([first.both()], "add_both_1", grid=(4,)))
        second.core_added(*order.fuse([second.core()], "add_core_2", grid=(4,)))
    last = (labels, d0, latents, dhead, small["m0"], small["m1"], small["a1"], small_head, small["f0"], small["f1"])
    attention_back(0, dmid, last)
    if fast:
        upper, lower = Owned(first), Owned(second, third)
        third.start(*grads["a0"])
        first.ring_added(*order.fuse([first.ring()], "add_ring_1"))
        second.both_added(*order.fuse([second.both()], "add_both_2", grid=(4,)))
        third.core_added(*order.fuse([third.core()], "add_core_3", grid=(4,)))
        second.ring_added(*order.fuse([second.ring()], "add_ring_2"))
        upper.last_added(*order.fuse([upper.last()], "add_last_1"))
        third.both_added(*order.fuse([third.both()], "add_both_3", grid=(4,)))
        third.ring_added(*order.fuse([third.ring()], "add_ring_3"))
        upper.adam(order, place, states, bufs, "adam_1")
        lower.last_added(*order.fuse([lower.last()], "add_last_0"))
        (loss,) = lower.adam(order, place, states, bufs, "adam_0")
        loss_sum = loss[0, 0]
        results = [bufs[name] for name in ("mats", "down", "skip", "tables", "vectors")]
        results[3] = [part.T for part in results[3]]
    else:
        loss_sum = lax.psum(small_head[2, 0], ALL)
        g_mats, g_down, g_skip, g_turned = reduce_any(grads)
        g_rows = g_turned.T
        g_tables = jnp.concatenate(
            [g_rows[ROW_PATCH:ROW_HEAD], g_rows[NP : NP + 2], g_rows[:NP], g_rows[ROW_HEAD:ROW_VEC]]
        )
        g_vectors = g_rows[ROW_VEC : ROW_VEC + N_VEC]
        results = [
            adam_update(layer_mats, g_mats, layer_mats_first, layer_mats_second, step_rates[0]),
            adam_update(down_mats, g_down, down_first, down_second, step_rates[1]),
            adam_update(skip_mat, g_skip, skip_first, skip_second, step_rates[2]),
            adam_update(tables, g_tables, tables_first, tables_second, step_rates[3]),
            adam_update(vectors, g_vectors, vectors_first, vectors_second, step_rates[4]),
        ]
    return (loss_sum, weight_total[0, 0], *(part for result in results for part in result))


GATHER_CHUNKS = (("a0", "t"), ("m0",), ("a1", "s", "m1"))
REDUCE_CHUNKS = (("m1", "a1", "s"), ("m0",), ("a0", "t"))


def solution(mesh):
    one, two, rows = P(None, "shard", None), P("shard", None), P(None, "shard")
    every = P(ALL, None, None)
    placed = (every, every, P(ALL), P(ALL), P(ALL), *[one] * 6, *[two] * 3, *[rows] * 6)
    fast = mesh.shape["rep"] == 4 and mesh.shape["shard"] == 8
    return jax.shard_map(
        functools.partial(local, fast),
        mesh=mesh,
        in_specs=placed,
        out_specs=(P(), P(), *[one] * 8, *[two] * 4, *[rows] * 8),
        check_vma=False,
    )
```

```python
import functools
import math

import jax
import jax.numpy as jnp
from jax import lax
from jax.experimental import pallas as pl
from jax.experimental.pallas import tpu as pltpu
from jax.sharding import PartitionSpec as P

D = 512
HEADS = 8
HD = 64
FF = 2048
CH = 16
NP = 256
CLASSES = 16
LAYERS = 2
STEP = 10
SEQ_LEN = 258

beta_one = 0.5
beta_two = 0.75
epsilon = 1e-08
weight_decay = 0.05
step_rates = (0.05, 0.03, 0.03, 0.05, 0.3)

TAIL = 16
T = NP + TAIL
ROW_PATCH = T
ROW_CLASS = ROW_PATCH + CH
ROW_HEAD = ROW_CLASS + CLASSES
ROW_VEC = ROW_HEAD + CH
N_VEC = LAYERS * (6 + FF // D) + 4
ROWS = D
ROW_WEIGHT = ROWS - 1
ROW_LOSS = 384
bf16 = jnp.bfloat16
f32 = jnp.float32
ALL = ("rep", "shard")
MIB = 1024 * 1024
MARGIN = 6 * MIB
WIDE = ("pack_0",)
ANY = pl.BlockSpec(memory_space=pl.ANY)
SMEM = pl.BlockSpec(memory_space=pltpu.SMEM)
WHOLE = pl.BlockSpec(memory_space=pltpu.VMEM)


def room(shape, dtype):
    size = jnp.dtype(dtype).itemsize
    rows, columns = ((1,) + tuple(shape))[-2:]
    rows, columns = -(-rows * size // 32) * 32 // size, -(-columns // 128) * 128
    return math.prod(shape[:-2]) * rows * columns * size


class Part:
    def __init__(self, body, inputs, in_specs, outs, out_specs, scratch=()):
        self.body, self.inputs, self.in_specs = body, list(inputs), list(in_specs)
        self.outs, self.out_specs, self.scratch = list(outs), list(out_specs), list(scratch)


class Order:
    def __init__(self):
        self.last = None

    def __call__(self, kernel, inputs, in_specs, outs, out_specs, scratch=(), grid=(1,), name=None, aliases=None):
        part = Part(kernel, inputs, in_specs, outs, out_specs, scratch)
        return self.fuse([part], name, grid=grid, aliases=aliases)[0]

    def fuse(self, parts, name, after=(), grid=(1,), aliases=None):
        extra = list(after) + ([] if self.last is None else [self.last])
        inputs = [value for part in parts for value in part.inputs]
        counts = [(len(p.inputs), len(p.outs), len(p.scratch)) for p in parts]
        ends = [sum(c[i] for c in counts) for i in range(3)]
        skip = len(extra)

        def body(*refs):
            groups = (refs[: ends[0]], refs[ends[0] + skip : ends[0] + skip + ends[1]], refs[ends[0] + skip + ends[1] :])
            at = [0, 0, 0]
            rest = []
            for part, count in zip(parts, counts):
                own = [r for i in range(3) for r in groups[i][at[i] : at[i] + count[i]]]
                at = [i + n for i, n in zip(at, count)]
                more = part.body(*own)
                if more is not None:
                    next(more)
                    rest.append(more)
            for more in rest:
                next(more, None)

        need = 0
        for part in parts:
            for spec, value in (*zip(part.in_specs, part.inputs), *zip(part.out_specs, part.outs)):
                if spec is not ANY and spec is not SMEM:
                    need += 2 * room(spec.block_shape or value.shape, value.dtype)
            need += sum(room(item.shape, item.dtype) for item in part.scratch if hasattr(item, "inner_aval") or hasattr(item, "shape"))
        result = pl.pallas_call(
            body,
            grid=grid,
            in_specs=[spec for part in parts for spec in part.in_specs] + [ANY] * skip,
            out_specs=[spec for part in parts for spec in part.out_specs],
            out_shape=[out for part in parts for out in part.outs],
            scratch_shapes=[item for part in parts for item in part.scratch],
            input_output_aliases=aliases or {},
            cost_estimate=pl.CostEstimate(flops=50_000_000_000, bytes_accessed=100_000_000, transcendentals=0),
            compiler_params=pltpu.CompilerParams(vmem_limit_bytes=56 * MIB if name in WIDE else min(need + MARGIN, 56 * MIB)),
            name=name,
        )(*inputs, *extra)
        self.last = result[0]
        split, at = [], 0
        for part in parts:
            split.append(result[at : at + len(part.outs)])
            at += len(part.outs)
        return split


def dot(left, right):
    return jnp.dot(left, right, preferred_element_type=f32)


def dot_t(left, right):
    return lax.dot_general(left, right, (((1,), (1,)), ((), ())), preferred_element_type=f32)


def t_dot(left, right):
    return lax.dot_general(left, right, (((0,), (0,)), ((), ())), preferred_element_type=f32)


def norm_hat(stream):
    center = jnp.mean(stream, -1, keepdims=True)
    offset = stream - center
    spread = jnp.mean(offset * offset, -1, keepdims=True)
    inverse = lax.rsqrt(spread + 1e-05)
    return (offset * inverse, inverse)


def norm_back(hat, inverse, gain, grad):
    scaled = grad * gain
    first = jnp.mean(scaled, -1, keepdims=True)
    second = jnp.mean(scaled * hat, -1, keepdims=True)
    return inverse * (scaled - first - hat * second)


def rows_sum(values):
    return jnp.sum(values, 0, keepdims=True)


LSE = 16


def apart(rows, scale):
    lane = lax.broadcasted_iota(jnp.int32, (1, 2 * HD), 1)
    return jnp.concatenate([rows * jnp.where(lane // HD == e, scale, 0.0).astype(bf16) for e in range(2)], 0)


def block_mask():
    row = lax.broadcasted_iota(jnp.int32, (TAIL, D), 0)
    lane = lax.broadcasted_iota(jnp.int32, (TAIL, D), 1)
    return (row // 2 == lane // HD, row % 2 == 0)


def spread_tail(rows, scale):
    own, first = block_mask()
    wide = rows.astype(f32)
    both = jnp.where(first, wide[0:1], wide[1:2]) * scale
    return jnp.where(own, both, 0.0).astype(bf16)


def gather_tail(values):
    own, first = block_mask()
    kept = jnp.where(own, values, 0.0)
    zero = rows_sum(jnp.where(first, kept, 0.0))
    one = rows_sum(jnp.where(first, 0.0, kept))
    row = lax.broadcasted_iota(jnp.int32, (TAIL, D), 0)
    return jnp.where(row == 0, zero, jnp.where(row == 1, one, 0.0))


def mask_keys(scores):
    tail = scores[NP:]
    row = lax.broadcasted_iota(jnp.int32, tail.shape, 0)
    return jnp.concatenate([scores[:NP], jnp.where(row < SEQ_LEN - NP, tail, -1e30)], 0)


def softmax_rows(scores):
    top = jnp.max(scores, 0, keepdims=True)
    expon = jnp.exp(scores - top)
    total = jnp.sum(expon, 0, keepdims=True)
    return (expon * (1.0 / total)).astype(bf16), top + jnp.log(total)


def pipelined(count, *stages):
    held = {}
    for step in range(count + len(stages) - 1):
        for i, stage in enumerate(stages):
            if 0 <= step - i < count:
                held[step - i] = stage(step - i, held.get(step - i))


def attention_forward(stream, layer_id, vec_ref, wa_ref, h_ref, qkv_ref, lse_ref, o_ref, mid_ref):
    base = layer_id * (6 + FF // D)
    hat, _ = norm_hat(stream)
    normed = (hat * vec_ref[base : base + 1] + vec_ref[base + 1 : base + 2]).astype(bf16)
    h_ref[0] = normed
    qkv_ref[0] = dot(normed, wa_ref[:, : 3 * D]).astype(bf16)
    scale = HD**-0.5

    def cut(part, pair):
        return qkv_ref[0, :, part * D + 128 * pair : part * D + 128 * pair + 128]

    def score(pair, _):
        return dot_t(cut(1, pair), apart(cut(0, pair)[:NP], scale))

    def weigh(pair, scores):
        weights, log_total = softmax_rows(mask_keys(scores))
        lse_ref[0, 2 * pair : 2 * pair + 1] = log_total[:, :NP]
        lse_ref[0, 2 * pair + 1 : 2 * pair + 2] = log_total[:, NP:]
        return weights

    def mix(pair, weights):
        values = apart(cut(2, pair), 1.0)
        out = t_dot(weights[:, :NP], values[:T]) + t_dot(weights[:, NP:], values[T:])
        o_ref[0, :NP, 128 * pair : 128 * pair + 128] = out.astype(bf16)

    tails = spread_tail(qkv_ref[0, NP:, :D], scale)
    weights, log_total = softmax_rows(mask_keys(dot_t(qkv_ref[0, :, D : 2 * D], tails)))
    lse_ref[0, HEADS : HEADS + 1, :TAIL] = log_total
    o_ref[0, NP:] = gather_tail(t_dot(weights, qkv_ref[0, :, 2 * D :])).astype(bf16)
    pipelined(HEADS // 2, score, weigh, mix)
    mid_ref[0] = stream + dot(o_ref[0], wa_ref[:, 3 * D :]) + vec_ref[base + 4 : base + 5]


def embed_attention_kernel(
    label_ref, latent_ref, time_ref, tab_ref, vec_ref, wa_ref, x_ref, h_ref, qkv_ref, lse_ref, o_ref, mid_ref
):
    b = pl.program_id(0)
    patch_rows = t_dot(latent_ref[0], tab_ref[ROW_PATCH:ROW_CLASS]) + vec_ref[N_VEC - 1 : N_VEC]
    row = lax.broadcasted_iota(jnp.int32, (TAIL, CLASSES), 0)
    column = lax.broadcasted_iota(jnp.int32, (TAIL, CLASSES), 1)
    choose = jnp.where((row == 1) & (column == label_ref[b]), 1.0, 0.0).astype(bf16)
    tail_rows = time_ref[0] + dot(choose, tab_ref[ROW_CLASS:ROW_HEAD])
    stream = jnp.concatenate([patch_rows, tail_rows], 0) + tab_ref[:T].astype(f32)
    x_ref[0] = stream
    attention_forward(stream, 0, vec_ref, wa_ref, h_ref, qkv_ref, lse_ref, o_ref, mid_ref)


def skip_attention_kernel(x1_ref, x0_ref, ws_ref, vec_ref, wa_ref, x_ref, h_ref, qkv_ref, lse_ref, o_ref, mid_ref):
    one = x1_ref[0].astype(bf16)
    zero = x0_ref[0].astype(bf16)
    halves = [dot(one, ws_ref[i, :D]) + dot(zero, ws_ref[i, D:]) for i in range(2)]
    stream = jnp.concatenate(halves, 1) + vec_ref[N_VEC - 2 : N_VEC - 1]
    x_ref[0] = stream
    attention_forward(stream, 1, vec_ref, wa_ref, h_ref, qkv_ref, lse_ref, o_ref, mid_ref)


def mlp_forward(layer_id, mid_ref, vec_ref, w1_ref, w2_ref, h_ref, act_ref, slope_ref):
    base = layer_id * (6 + FF // D)
    hat, _ = norm_hat(mid_ref[...])
    normed = (hat * vec_ref[base + 2 : base + 3] + vec_ref[base + 3 : base + 4]).astype(bf16)
    h_ref[...] = normed
    const = math.sqrt(2.0 / math.pi)

    for j in range(FF // D):
        cols = slice(D * j, D * j + D)
        pre = dot(normed, w1_ref[:, cols]) + vec_ref[base + 6 + j : base + 7 + j]
        square = pre * pre
        half = 0.5 + 0.5 * jnp.tanh(pre * (const + (const * 0.044715) * square))
        act = pre * half
        act_ref[:, cols] = act.astype(bf16)
        slope = half + act * (1.0 - half) * (2.0 * const + (6.0 * const * 0.044715) * square)
        slope_ref[:, cols] = slope.astype(bf16)
    total = jnp.concatenate([dot(act_ref[...], w2_ref[i]) for i in range(2)], 1)
    return mid_ref[...] + total + vec_ref[base + 5 : base + 6]


def mlp_kernel(layer_id, mid_ref, vec_ref, w1_ref, w2_ref, h_ref, act_ref, slope_ref, out_ref):
    out_ref[...] = mlp_forward(layer_id, mid_ref, vec_ref, w1_ref, w2_ref, h_ref, act_ref, slope_ref)


def head_backward(b, total_ref, weight_ref, out, noise_ref, tab_ref, vec_ref, dhead_ref, small_ref):
    hat, inverse = norm_hat(out[:NP])
    gain = vec_ref[N_VEC - 4 : N_VEC - 3]
    final = (hat * gain + vec_ref[N_VEC - 3 : N_VEC - 2]).astype(bf16)
    head = tab_ref[ROW_HEAD:ROW_VEC]
    errors = dot_t(head, final) - noise_ref[0].astype(f32)
    per_seq = jnp.sum(errors * errors) * (1.0 / (CH * NP))
    weight = weight_ref[b].astype(f32)
    scale = (jnp.ones((1, 1), f32) / total_ref[0, 0]) * weight * (2.0 / (CH * NP))
    grad_pred = (scale * errors).astype(bf16)
    dhead_ref[...] += dot(grad_pred, final)
    grad = t_dot(grad_pred, head)
    small_ref[0:1] += rows_sum(grad * hat)
    small_ref[1:2] += rows_sum(grad)
    small_ref[2:3] += jnp.full((1, D), weight * per_seq, f32)
    return jnp.concatenate([norm_back(hat, inverse, gain, grad), jnp.zeros((TAIL, D), f32)], 0)


def rows_of(b):
    return pl.ds(pl.multiple_of(T * b, TAIL), T)


def coords(c_ref):
    return tuple(c_ref[i] for i in range(4))


def place_of(c_ref, shard):
    _, _, z, y = coords(c_ref)
    return ((shard % 2) ^ y, (shard // 2 - z) & 3)


def sub_of(c_ref, h, t, g):
    x, c, _, _ = coords(c_ref)
    return 4 * (c ^ h) + 2 * t + (g ^ x)


def scatter_pieces(c_ref, keep_ref, send_ref, at, piece):
    for h, dest in ((0, keep_ref), (1, send_ref)):
        for t in range(2):
            for g in range(2):
                j = sub_of(c_ref, h, t, g)
                for s in range(8):
                    f, k = place_of(c_ref, s)
                    value = piece(j, s)
                    dest[t, g, f, k, at : at + value.shape[0]] = value


def by_columns(ref):
    return lambda j, s: ref[64 * s : 64 * s + 64, pl.ds(pl.multiple_of(256 * j, 256), 256)]


def by_rows(ref):
    return lambda j, s: ref[pl.ds(pl.multiple_of(64 * j, 64), 64), 256 * s : 256 * s + 256]


def mlp_backward(
    layer_id, rows, dout, slope_ref, mid_ref, vec_ref, w1_ref, w2_ref, dmid_ref, small_ref, dfc1b_ref, right_s, grads_s
):
    base = layer_id * (6 + FF // D)
    low = dout.astype(bf16)
    right_s[rows] = low

    def enter(j, _):
        block = slice(D * j, D * j + D)
        return dot_t(low[:, :256], w2_ref[0, block]) + dot_t(low[:, 256:], w2_ref[1, block])

    def bend(j, grad_act):
        cols = slice(D * j, D * j + D)
        grad_pre = grad_act * slope_ref[:, cols].astype(f32)
        dfc1b_ref[:, cols] += rows_sum(grad_pre)
        grad = grad_pre.astype(bf16)
        grads_s[rows, cols] = grad
        return grad

    total = []

    def leave(j, grad):
        part = dot_t(grad, w1_ref[:, D * j : D * j + D])
        total.append(part if not total else total[-1] + part)

    pipelined(FF // D, enter, bend, leave)
    grad_normed = total[-1]
    hat, inverse = norm_hat(mid_ref[...])
    small_ref[0:1] += rows_sum(grad_normed * hat)
    small_ref[1:2] += rows_sum(grad_normed)
    small_ref[2:3] += rows_sum(dout)
    dmid_ref[...] = dout + norm_back(hat, inverse, vec_ref[base + 2 : base + 3], grad_normed)


def mlp_weights(c_ref, keep_ref, send_ref, left_s, right_s, grads_s, acts_s, tile_s):
    tile_s[...] = t_dot(left_s[...], grads_s[...]).astype(bf16)
    scatter_pieces(c_ref, keep_ref, send_ref, 0, by_columns(tile_s))
    tile_s[...] = t_dot(right_s[...], acts_s[...]).astype(bf16)
    scatter_pieces(c_ref, keep_ref, send_ref, 64, by_rows(tile_s))


def mlp_backward_kernel(
    layer_id,
    c_ref,
    dout_ref,
    act_ref,
    slope_ref,
    h_ref,
    mid_ref,
    vec_ref,
    w1_ref,
    w2_ref,
    dmid_ref,
    keep_ref,
    send_ref,
    small_ref,
    dfc1b_ref,
    left_s,
    right_s,
    grads_s,
    acts_s,
    tile_s,
):
    b = pl.program_id(0)

    @pl.when(b == 0)
    def _():
        small_ref[...] = jnp.zeros_like(small_ref)
        dfc1b_ref[...] = jnp.zeros_like(dfc1b_ref)

    rows = rows_of(b)
    left_s[rows] = h_ref[...]
    acts_s[rows] = act_ref[...]
    weights = (mid_ref, vec_ref, w1_ref, w2_ref)
    mlp_backward(layer_id, rows, dout_ref[...], slope_ref, *weights, dmid_ref, small_ref, dfc1b_ref, right_s, grads_s)

    @pl.when(b == pl.num_programs(0) - 1)
    def _():
        mlp_weights(c_ref, keep_ref, send_ref, left_s, right_s, grads_s, acts_s, tile_s)


def mlp_turn_kernel(
    total_ref,
    weight_ref,
    c_ref,
    mid_ref,
    vec_ref,
    w1_ref,
    w2_ref,
    noise_ref,
    tab_ref,
    dmid_ref,
    keep_ref,
    send_ref,
    small_ref,
    dfc1b_ref,
    dhead_ref,
    small_head_ref,
    left_s,
    right_s,
    grads_s,
    acts_s,
    tile_s,
    slope_s,
):
    b = pl.program_id(0)

    @pl.when(b == 0)
    def _():
        for ref in (small_ref, dfc1b_ref, dhead_ref, small_head_ref):
            ref[...] = jnp.zeros_like(ref)

    rows = rows_of(b)
    weights = (mid_ref, vec_ref, w1_ref, w2_ref)
    out = mlp_forward(1, *weights, left_s.at[rows], acts_s.at[rows], slope_s)
    dout = head_backward(b, total_ref, weight_ref, out, noise_ref, tab_ref, vec_ref, dhead_ref, small_head_ref)
    mlp_backward(1, rows, dout, slope_s, *weights, dmid_ref, small_ref, dfc1b_ref, right_s, grads_s)

    @pl.when(b == pl.num_programs(0) - 1)
    def _():
        mlp_weights(c_ref, keep_ref, send_ref, left_s, right_s, grads_s, acts_s, tile_s)


def last_backward_kernel(
    layer_id,
    c_ref,
    dmid_ref,
    x_ref,
    h_ref,
    qkv_ref,
    lse_ref,
    o_ref,
    vec_ref,
    wa_ref,
    label_ref,
    d0_ref,
    latent_ref,
    dhead_ref,
    small_m0,
    small_m1,
    small_a1,
    small_head,
    dfc1b0,
    dfc1b1,
    keep_ref,
    send_ref,
    left_s,
    outs_s,
    grads_s,
    lows_s,
    dqkv_s,
    tile_s,
    small_ref,
    table_s,
):
    b = pl.program_id(0)

    @pl.when(b == 0)
    def _():
        table_s[...] = jnp.zeros_like(table_s)

    refs = (dmid_ref, x_ref, h_ref, qkv_ref, lse_ref, o_ref, vec_ref, wa_ref, small_ref, left_s, outs_s, grads_s, lows_s, dqkv_s)
    embed_grads(b, label_ref, attention_backward(layer_id, *refs) + d0_ref[0], latent_ref, table_s)

    @pl.when(b == pl.num_programs(0) - 1)
    def _():
        attention_weights(c_ref, keep_ref, send_ref, left_s, outs_s, grads_s, lows_s, tile_s)
        table_s[ROW_HEAD:ROW_VEC] = dhead_ref[...]
        row = ROW_VEC
        for own, mlp, fc1b in ((small_ref, small_m0, dfc1b0), (small_a1, small_m1, dfc1b1)):
            table_s[row : row + 2] = own[0:2]
            table_s[row + 2 : row + 4] = mlp[0:2]
            table_s[row + 4 : row + 5] = own[2:3]
            table_s[row + 5 : row + 6] = mlp[2:3]
            for i in range(FF // D):
                table_s[row + 6 + i : row + 7 + i] = fc1b[:, D * i : D * i + D]
            row += 6 + FF // D
        table_s[row : row + 2] = small_head[0:2]
        table_s[row + 2 : row + 3] = small_a1[3:4]
        table_pieces(c_ref, small_head[2:3, 0:1], table_s[...], keep_ref, send_ref, 64)


def attention_backward(
    layer_id, dmid_ref, x_ref, h_ref, qkv_ref, lse_ref, o_ref, vec_ref, wa_ref, small_ref, left_s, outs_s, grads_s, lows_s, dqkv_s
):
    b = pl.program_id(0)
    rows = rows_of(b)
    base = layer_id * (6 + FF // D)

    @pl.when(b == 0)
    def _():
        small_ref[...] = jnp.zeros_like(small_ref)

    dmid = dmid_ref[0]
    low = dmid.astype(bf16)
    left_s[rows] = h_ref[0]
    outs_s[rows] = o_ref[0]
    lows_s[rows] = low
    grad_att = dot_t(low, wa_ref[:, 3 * D :]).astype(bf16)
    scale = HD**-0.5

    def cut(part, pair):
        return qkv_ref[0, :, part * D + 128 * pair : part * D + 128 * pair + 128]

    def put(part, pair, value):
        dqkv_s[: value.shape[0], part * D + 128 * pair : part * D + 128 * pair + 128] = value.astype(bf16)

    tails, tail_douts = spread_tail(qkv_ref[0, NP:, :D], scale), spread_tail(grad_att[NP:], 1.0)
    weights = jnp.exp(mask_keys(dot_t(qkv_ref[0, :, D : 2 * D], tails)) - lse_ref[0, HEADS : HEADS + 1, :TAIL])
    grad_w = dot_t(qkv_ref[0, :, 2 * D :], tail_douts)
    grad_s = (weights * (grad_w - rows_sum(weights * grad_w))).astype(bf16)
    tail_dk = dot(grad_s, tails)
    tail_dv = dot(weights.astype(bf16), tail_douts)
    dqkv_s[NP:, :D] = (gather_tail(t_dot(grad_s, qkv_ref[0, :, D : 2 * D])) * scale).astype(bf16)

    def score(pair, _):
        queries = apart(cut(0, pair)[:NP], scale)
        douts = apart(grad_att[:NP, 128 * pair : 128 * pair + 128], 1.0)
        return dot_t(cut(1, pair), queries), dot_t(cut(2, pair), douts), queries, douts

    def weigh(pair, held):
        scores, grad_w, queries, douts = held
        log_total = jnp.concatenate([lse_ref[0, 2 * pair + e : 2 * pair + e + 1] for e in range(2)], 1)
        weights = jnp.exp(mask_keys(scores) - log_total)
        grad_s = weights * (grad_w - rows_sum(weights * grad_w))
        return weights.astype(bf16), grad_s.astype(bf16), queries, douts

    def mix(pair, held):
        weights, grad_s, queries, douts = held
        cols = slice(128 * pair, 128 * pair + 128)
        keys = apart(cut(1, pair), scale)
        put(0, pair, t_dot(grad_s[:, :NP], keys[:T]) + t_dot(grad_s[:, NP:], keys[T:]))
        put(1, pair, dot(grad_s, queries) + tail_dk[:, cols])
        put(2, pair, dot(weights, douts) + tail_dv[:, cols])

    pipelined(HEADS // 2, score, weigh, mix)
    grads_s[rows] = dqkv_s[...]
    grad_normed = dot_t(dqkv_s[...], wa_ref[:, : 3 * D])
    hat, inverse = norm_hat(x_ref[0])
    small_ref[0:1] += rows_sum(grad_normed * hat)
    small_ref[1:2] += rows_sum(grad_normed)
    small_ref[2:3] += rows_sum(dmid)
    return dmid + norm_back(hat, inverse, vec_ref[base : base + 1], grad_normed)


def attention_weights(c_ref, keep_ref, send_ref, left_s, outs_s, grads_s, lows_s, tile_s):
    tile_s[:, : 3 * D] = t_dot(left_s[...], grads_s[...]).astype(bf16)
    tile_s[:, 3 * D :] = t_dot(outs_s[...], lows_s[...]).astype(bf16)
    scatter_pieces(c_ref, keep_ref, send_ref, 0, by_columns(tile_s))


def middle_backward_kernel(
    layer_id,
    c_ref,
    dmid_ref,
    x_ref,
    h_ref,
    qkv_ref,
    lse_ref,
    o_ref,
    vec_ref,
    wa_ref,
    x1_ref,
    x0_ref,
    ws_ref,
    keep_ref,
    send_ref,
    d1_ref,
    d0_ref,
    small_ref,
    left_s,
    outs_s,
    grads_s,
    lows_s,
    dqkv_s,
    tile_s,
    both_s,
    skip_s,
    skip_tile_s,
):
    b = pl.program_id(0)
    refs = (dmid_ref, x_ref, h_ref, qkv_ref, lse_ref, o_ref, vec_ref, wa_ref, small_ref)
    grad = attention_backward(layer_id, *refs, left_s, outs_s, grads_s, lows_s, dqkv_s)
    low = grad.astype(bf16)
    small_ref[3:4] += rows_sum(grad)
    rows = rows_of(b)
    both_s[rows, :D] = x1_ref[0].astype(bf16)
    both_s[rows, D:] = x0_ref[0].astype(bf16)
    skip_s[rows] = low
    for u, dest in ((0, d1_ref), (1, d0_ref)):
        cols = slice(D * u, D * u + D)
        dest[0] = dot_t(low[:, :256], ws_ref[0, cols]) + dot_t(low[:, 256:], ws_ref[1, cols])

    @pl.when(b == pl.num_programs(0) - 1)
    def _():
        attention_weights(c_ref, keep_ref, send_ref, left_s, outs_s, grads_s, lows_s, tile_s)
        skip_tile_s[...] = t_dot(both_s[...], skip_s[...]).astype(bf16)
        for half in range(2):

            def piece(j, s, half=half):
                rows = pl.ds(pl.multiple_of(128 * s + 16 * j, 16), 16)
                return skip_tile_s[rows, 256 * half : 256 * half + 256]

            scatter_pieces(c_ref, keep_ref, send_ref, 64 + 16 * half, piece)


def embed_grads(b, label_ref, grad, latent_ref, table_s):
    table_s[:T] += grad
    patch = grad[:NP]
    last = ROW_VEC + N_VEC - 1
    table_s[last : last + 1] += rows_sum(patch)
    table_s[ROW_PATCH:ROW_CLASS] += dot(latent_ref[0], patch.astype(bf16))
    row = lax.broadcasted_iota(jnp.int32, (CLASSES, D), 0)
    table_s[ROW_CLASS:ROW_HEAD] += jnp.where(row == label_ref[b], grad[NP + 1 : NP + 2], 0.0)


def table_pieces(c_ref, loss, table, keep_ref, send_ref, at):
    x, c, z, y = coords(c_ref)
    me = (x * 2 + c) * 8 + z * 2 + y
    high = loss.astype(bf16).astype(f32)
    middle = (loss - high).astype(bf16).astype(f32)
    small = loss - high - middle
    row = lax.broadcasted_iota(jnp.int32, (ROWS, D), 0)
    kind = lax.broadcasted_iota(jnp.int32, (ROWS, D), 1) % 8
    slots = jnp.where(kind == 0, high, jnp.where(kind == 1, middle, jnp.where(kind == 2, small, 0.0)))
    turned = jnp.where(row == ROW_LOSS + me, slots, table).T
    for s in range(8):
        f, k = place_of(c_ref, s)
        for j in range(8):
            rows = slice(64 * s + 8 * j, 64 * s + 8 * j + 8)
            piece = jnp.concatenate([turned[rows, :256], turned[rows, 256:]], 0).astype(bf16)
            h, t, g = (j // 4) ^ c, j // 2 % 2, (j % 2) ^ x

            @pl.when(h == 0)
            def _(piece=piece, t=t, g=g, f=f, k=k):
                keep_ref[t, g, f, k, at : at + 16] = piece

            @pl.when(h == 1)
            def _(piece=piece, t=t, g=g, f=f, k=k):
                send_ref[t, g, f, k, at : at + 16] = piece


def per_seq(width, rows=T):
    return pl.BlockSpec((1, rows, width), lambda b: (b, 0, 0))


def fixed(shape):
    return pl.BlockSpec(shape, lambda b: (0,) * len(shape))


def shape_of(shape, dtype=f32):
    return jax.ShapeDtypeStruct(shape, dtype)


def pieces_shape(rows):
    return (2, 2, 2, 4, rows, 256)


def call_attention(order, first, n_seqs, inputs):
    shapes = [(T, D, f32), (T, D, bf16), (T, 3 * D, bf16), (LSE, NP, f32), (T, D, bf16), (T, D, f32)]
    vec_spec, wa_spec = fixed((N_VEC, D)), fixed((D, 4 * D))
    if first:
        in_specs = [SMEM, per_seq(NP, CH), per_seq(D, TAIL), fixed((ROWS, D)), vec_spec, wa_spec]
    else:
        in_specs = [per_seq(D), per_seq(D), fixed((2, 2 * D, D // 2)), vec_spec, wa_spec]
    return order(
        embed_attention_kernel if first else skip_attention_kernel,
        inputs,
        in_specs,
        [shape_of((n_seqs, r, w), d) for r, w, d in shapes],
        [per_seq(w, r) for r, w, _ in shapes],
        grid=(n_seqs,),
        name="attention_forward_%d" % (0 if first else 1),
    )


def flat(width):
    return pl.BlockSpec((T, width), lambda b: (b, 0))


def call_mlp(order, layer_id, n_seqs, mid, vec, w1, w2):
    shapes = [(D, bf16), (FF, bf16), (FF, bf16), (D, f32)]
    whole = n_seqs * T
    out = order(
        functools.partial(mlp_kernel, layer_id),
        [mid.reshape(whole, D), vec, w1, w2],
        [flat(D), fixed((N_VEC, D)), fixed((D, FF)), fixed((2, FF, D // 2))],
        [shape_of((whole, w), d) for w, d in shapes],
        [flat(w) for w, _ in shapes],
        grid=(n_seqs,),
        name="mlp_forward_%d" % layer_id,
    )
    return [*out[:3], out[3].reshape(n_seqs, T, D)]


def mlp_backward_outs(n_seqs):
    whole = n_seqs * T
    pieces = pieces_shape(128)
    outs = [shape_of((whole, D)), shape_of(pieces, bf16), shape_of(pieces, bf16), shape_of((8, D)), shape_of((1, FF))]
    out_specs = [flat(D), fixed(pieces), fixed(pieces), fixed((8, D)), fixed((1, FF))]
    scratch = [
        pltpu.VMEM((whole, D), bf16),
        pltpu.VMEM((whole, D), bf16),
        pltpu.VMEM((whole, FF), bf16),
        pltpu.VMEM((whole, FF), bf16),
        pltpu.VMEM((D, FF), bf16),
    ]
    return outs, out_specs, scratch


def call_mlp_backward(order, layer_id, n_seqs, place, dout, act, slope, normed, mid, vec, w1, w2):
    whole = n_seqs * T
    outs, out_specs, scratch = mlp_backward_outs(n_seqs)
    out = order(
        functools.partial(mlp_backward_kernel, layer_id),
        (place, dout.reshape(whole, D), act, slope, normed, mid.reshape(whole, D), vec, w1, w2),
        [SMEM, flat(D), flat(FF), flat(FF), flat(D), flat(D)]
        + [fixed((N_VEC, D)), fixed((D, FF)), fixed((2, FF, D // 2))],
        outs,
        out_specs,
        scratch,
        grid=(n_seqs,),
        name="mlp_backward_%d" % layer_id,
    )
    return [out[0].reshape(n_seqs, T, D), *out[1:]]


def call_mlp_turn(order, n_seqs, total, weights, place, mid, vec, w1, w2, noise, tab):
    whole = n_seqs * T
    outs, out_specs, scratch = mlp_backward_outs(n_seqs)
    out = order(
        mlp_turn_kernel,
        (total, weights, place, mid.reshape(whole, D), vec, w1, w2, noise, tab),
        [SMEM, SMEM, SMEM, flat(D), fixed((N_VEC, D)), fixed((D, FF)), fixed((2, FF, D // 2))]
        + [per_seq(NP, CH), fixed((ROWS, D))],
        outs + [shape_of((CH, D)), shape_of((8, D))],
        out_specs + [fixed((CH, D)), fixed((8, D))],
        scratch + [pltpu.VMEM((T, FF), bf16)],
        grid=(n_seqs,),
        name="mlp_turn",
    )
    return [out[0].reshape(n_seqs, T, D), *out[1:]]


def call_attention_backward(order, layer_id, n_seqs, place, dmid, x, normed, qkv, lse, att, vec, wa, more):
    whole = n_seqs * T
    pieces = pieces_shape(80 if layer_id == 0 else 96)
    specs = [SMEM, per_seq(D), per_seq(D), per_seq(D), per_seq(3 * D), per_seq(NP, LSE), per_seq(D)]
    specs += [fixed((N_VEC, D)), fixed((D, 4 * D))]
    scratch = [
        pltpu.VMEM((whole, D), bf16),
        pltpu.VMEM((whole, D), bf16),
        pltpu.VMEM((whole, 3 * D), bf16),
        pltpu.VMEM((whole, D), bf16),
        pltpu.VMEM((T, 3 * D), bf16),
        pltpu.VMEM((D, 4 * D), bf16),
    ]
    if layer_id == 1:
        kernel = middle_backward_kernel
        specs += [per_seq(D), per_seq(D), fixed((2, 2 * D, D // 2))]
        outs = [shape_of((n_seqs, T, D)), shape_of((n_seqs, T, D)), shape_of((8, D))]
        out_specs = [per_seq(D), per_seq(D), fixed((8, D))]
        scratch += [pltpu.VMEM((whole, 2 * D), bf16), pltpu.VMEM((whole, D), bf16), pltpu.VMEM((2 * D, D), bf16)]
    else:
        kernel = last_backward_kernel
        specs += [SMEM, per_seq(D), per_seq(NP, CH), fixed((CH, D))] + [fixed((8, D))] * 4 + [fixed((1, FF))] * 2
        scratch += [pltpu.VMEM((8, D), f32), pltpu.VMEM((ROWS, D), f32)]
        outs, out_specs = [], []
    return order(
        functools.partial(kernel, layer_id),
        [place, dmid, x, normed, qkv, lse, att, vec, wa, *more],
        specs,
        [shape_of(pieces, bf16), shape_of(pieces, bf16)] + outs,
        [fixed(pieces), fixed(pieces)] + out_specs,
        scratch,
        grid=(n_seqs,),
        name="attention_backward_%d" % layer_id,
    )


def device_id(x, c, z, y):
    return (x * 2 + c) * 8 + z * 2 + y


def pairs(move):
    every = [(x, c, z, y) for x in range(2) for c in range(2) for z in range(4) for y in range(2)]
    return [(device_id(*at), device_id(*move(*at))) for at in every]


TO_CORE = pairs(lambda x, c, z, y: (x, 1 - c, z, y))
TO_X = pairs(lambda x, c, z, y: (1 - x, c, z, y))
TO_Y = pairs(lambda x, c, z, y: (x, c, z, 1 - y))
TO_Z = [pairs(lambda x, c, z, y, k=k: (x, c, (z + k) % 4, y)) for k in range(4)]
PIECE_ROWS = {"a": 64, "m": 128, "s": 32, "t": 16}


def send(value, to):
    return lax.ppermute(value, ALL, to)


def rows_in(kinds):
    return sum(PIECE_ROWS[kind[0]] for kind in kinds)


def pack_kernel(kinds, c_ref, mats_ref, down_ref, skip_ref, tab_ref, vec_ref, weight_ref, u_ref, wide_s, narrow_s, sem):
    x, c, _, _ = coords(c_ref)
    copies, casts = [], []
    wide = narrow = row = 0
    for kind in kinds:
        l = int(kind[1:] or 0)
        if kind[0] in "am":
            for t in range(2):
                start = (2048 if kind[0] == "m" else 0) + 256 * (4 * c + 2 * t + x)
                copies.append((mats_ref.at[l, :, pl.ds(pl.multiple_of(start, 256), 256)], wide_s.at[wide]))
                casts.append((t, row, wide_s.at[wide], None))
                wide += 1
            row += 64
        if kind[0] in "ms":
            size = 32 if kind[0] == "m" else 16
            ref = down_ref.at[l] if kind[0] == "m" else skip_ref
            for t in range(2):
                start = pl.multiple_of(size * (4 * c + 2 * t + x), size)
                copies.append((ref.at[pl.ds(start, size)], narrow_s.at[narrow, :size]))
                for half in range(2):
                    cols = slice(256 * half, 256 * half + 256)
                    casts.append((t, row + size * half, narrow_s.at[narrow, :size], cols))
                narrow += 1
            row += 2 * size
        if kind[0] == "t":
            own_weight = weight_ref[0]
            for i in range(1, weight_ref.shape[0]):
                own_weight += weight_ref[i]
            turned = vec_ref[...].T
            first, last = CH + CLASSES, CH + CLASSES + SEQ_LEN
            corner = (lax.broadcasted_iota(jnp.int32, (16, 256), 0) == 8) & (
                lax.broadcasted_iota(jnp.int32, (16, 256), 1) == 255
            )
            for t in range(2):
                j = 4 * c + 2 * t + x
                table = tab_ref[pl.ds(pl.multiple_of(8 * j, 8), 8)]
                vecs = turned[0:8]
                for i in range(1, 8):
                    vecs = jnp.where(j == i, turned[8 * i : 8 * i + 8], vecs)
                rest = [
                    table[:, first : first + 2],
                    jnp.zeros((8, TAIL - 2), f32),
                    table[:, :first],
                    table[:, last:],
                    vecs,
                    jnp.zeros((8, ROWS - ROW_VEC - N_VEC), f32),
                ]
                piece = jnp.concatenate([table[:, first + 2 : last], jnp.concatenate(rest, 1)], 0)
                if t == 0:
                    piece = jnp.where(corner, own_weight.astype(f32), piece)
                u_ref[t, row : row + 16] = piece.astype(bf16)
            row += 16
    copies = [pltpu.make_async_copy(a, b, sem) for a, b in copies]
    for copy in copies:
        copy.start()
    yield
    for copy in copies:
        copy.wait()
    for t, at, ref, cols in casts:
        value = ref[...] if cols is None else ref[:, cols]
        u_ref[t, at : at + value.shape[0]] = value.astype(bf16)


def join_ring_kernel(u0, u1, u2, u3, b_ref, c_ref):
    for k, ref in enumerate((u0, u1, u2, u3)):
        b_ref[k] = ref[0]
        c_ref[k] = ref[1]


def join_pair_kernel(b0, b1, c0, c1, b_ref, c_ref):
    for i, (b, c) in enumerate(((b0, c0), (b1, c1))):
        b_ref[i] = b[...]
        c_ref[i] = c[...]


def join_own_kernel(b, c, both_ref):
    both_ref[0] = b[...]
    both_ref[1] = c[...]


def assemble_kernel(kinds, c_ref, *refs):
    x, c, z, y = coords(c_ref)
    sources, dests = refs[:6], refs[6:]
    for h in range(2):
        if h == 0:
            own_b, x_b, own_c, y_c = sources[:4]
        else:
            own_b, own_c, x_b, y_c = (sources[4 + i].at[k] for i in range(2) for k in range(2))
        for t in range(2):
            for g in range(2):
                j = 4 * (c ^ h) + 2 * t + (g ^ x)
                cols = pl.ds(pl.multiple_of(256 * j, 256), 256)
                for f in range(2):
                    src = ((own_b, x_b)[g].at[f]) if t == 0 else ((own_c, y_c)[f].at[g])
                    for k in range(4):
                        s = 2 * ((z - k) & 3) + (y ^ f)
                        row = 0
                        at = 0
                        for kind in kinds:
                            if kind[0] in "am":
                                rows = pl.ds(pl.multiple_of(64 * s, 64), 64)
                                dests[at][rows, cols] = src[k, row : row + 64]
                                row, at = row + 64, at + 1
                            if kind[0] in "ms":
                                size = 32 if kind[0] == "m" else 16
                                rows = pl.ds(pl.multiple_of(size * (8 * s + j), size), size)
                                for half in range(2):
                                    dests[at][half, rows] = src[k, row : row + size]
                                    row += size
                                at += 1
                            if kind[0] == "t":
                                both = src[k, row : row + 16].astype(f32)
                                rows = pl.ds(pl.multiple_of(64 * s + 8 * j, 8), 8)
                                dests[-1][rows, :256] = both[:8]
                                dests[-1][rows, 256:] = both[8:]
    if "t" in kinds:
        table_ref, vec_ref, total_ref, turned_s = dests[-4:]
        table = turned_s[...].T
        table_ref[...] = table.astype(bf16)
        vec_ref[...] = table[ROW_VEC : ROW_VEC + N_VEC]
        total_ref[0, 0] = jnp.sum(table[ROW_WEIGHT : ROW_WEIGHT + 1])


def assemble_all_kernel(kinds, source, *dests):
    for x in range(2):
        for c in range(2):
            for s in range(8):
                for t in range(2):
                    j = 4 * c + 2 * t + x
                    src = source.at[8 * (2 * x + c) + s, t]
                    row = at = 0
                    for kind in kinds:
                        if kind[0] in "am":
                            dests[at][64 * s : 64 * s + 64, 256 * j : 256 * j + 256] = src[row : row + 64]
                            row, at = row + 64, at + 1
                        if kind[0] in "ms":
                            size = 32 if kind[0] == "m" else 16
                            for half in range(2):
                                start = size * (8 * s + j)
                                dests[at][half, start : start + size] = src[row : row + size]
                                row += size
                            at += 1


class Gather:
    def __init__(self, place, kinds, sources):
        self.place, self.kinds, self.sources = place, kinds, sources
        self.rows = rows_in(kinds)

    def pack(self):
        return Part(
            functools.partial(pack_kernel, self.kinds),
            (self.place, *self.sources),
            [SMEM, ANY, ANY, ANY] + ([WHOLE, WHOLE, SMEM] if "t" in self.kinds else [ANY] * 3),
            [shape_of((2, self.rows, 256), bf16)],
            [WHOLE],
            [pltpu.VMEM((4, 64, 256), f32), pltpu.VMEM((4, 32, D), f32), pltpu.SemaphoreType.DMA],
        )

    def packed_for_all(self, results):
        self.every = lax.all_gather(results[0], ALL)

    def assemble_all(self):
        shapes = self.shapes()
        return Part(
            functools.partial(assemble_all_kernel, self.kinds), [self.every], [WHOLE], shapes, [WHOLE] * len(shapes)
        )

    def packed(self, results):
        (own,) = results
        self.ring = [own] + [send(own, TO_Z[k]) for k in range(1, 4)]

    def join_ring(self):
        half = shape_of((4, self.rows, 256), bf16)
        return Part(join_ring_kernel, self.ring, [WHOLE] * 4, [half] * 2, [WHOLE] * 2)

    def ring_joined(self, results):
        b, c = results
        self.halves = (b, send(b, TO_Y), c, send(c, TO_X))

    def join_pair(self):
        whole = shape_of((2, 4, self.rows, 256), bf16)
        return Part(join_pair_kernel, self.halves, [WHOLE] * 4, [whole, whole], [WHOLE] * 2)

    def pair_joined(self, results):
        b, c = results
        self.mine = [b, send(b, TO_X), c, send(c, TO_Y)]

    def join_own(self):
        both = shape_of((2, 2, 4, self.rows, 256), bf16)
        return Part(join_own_kernel, (self.mine[0], self.mine[2]), [WHOLE] * 2, [both], [WHOLE])

    def own_joined(self, results):
        self.other = [send(results[0], TO_CORE)]

    def join_rest(self):
        both = shape_of((2, 2, 4, self.rows, 256), bf16)
        return Part(join_own_kernel, (self.mine[1], self.mine[3]), [WHOLE] * 2, [both], [WHOLE])

    def rest_joined(self, results):
        self.other.append(send(results[0], TO_CORE))

    def shapes(self):
        shapes = []
        for kind in self.kinds:
            if kind[0] in "am":
                shapes.append(shape_of((D, 2048), bf16))
            if kind[0] == "m":
                shapes.append(shape_of((2, FF, 256), bf16))
            if kind[0] == "s":
                shapes.append(shape_of((2, 2 * D, 256), bf16))
            if kind[0] == "t":
                shapes += [shape_of((ROWS, D), bf16), shape_of((N_VEC, D)), shape_of((1, 1))]
        return shapes

    def assemble(self):
        shapes = self.shapes()
        scratch = [pltpu.VMEM((D, ROWS), f32)] if "t" in self.kinds else []
        return Part(
            functools.partial(assemble_kernel, self.kinds),
            (self.place, *self.mine, *self.other),
            [SMEM] + [WHOLE] * 6,
            shapes,
            [SMEM if shape.shape == (1, 1) else WHOLE for shape in shapes],
            scratch,
        )


def added(*values):
    total = values[0].astype(f32)
    for value in values[1:]:
        total += value.astype(f32)
    return total.astype(bf16)


def add_core_kernel(n, *refs):
    keeps, gots, (b0_ref, b1_ref, c0_ref, c1_ref) = refs[:n], refs[n : 2 * n], refs[2 * n :]
    row = 0
    for keep, got in zip(keeps, gots):
        rows = slice(row, row + keep.shape[4])
        row = rows.stop
        for i in range(2):
            for dest, at in ((b0_ref, (0, 0, i)), (b1_ref, (0, 1, i)), (c0_ref, (1, i, 0)), (c1_ref, (1, i, 1))):
                dest[i, :, rows] = added(keep[at], got[at])


def add_both_kernel(b0_ref, gb_ref, c0_ref, gc_ref, b_ref, sb_ref, c_ref, sc_ref):
    for keep, got, dests in ((b0_ref, gb_ref, (b_ref, sb_ref)), (c0_ref, gc_ref, (c_ref, sc_ref))):
        for i, dest in enumerate(dests):
            dest[...] = added(keep[i], got[i])


def add_ring_kernel(b_ref, gb_ref, c_ref, gc_ref, *dests):
    for t, (keep, got) in enumerate(((b_ref, gb_ref), (c_ref, gc_ref))):
        for k, dest in enumerate(dests):
            dest[t] = added(keep[k], got[k])


def add_last_kernel(*refs):
    row = 0
    for i in range(0, len(refs) - 1, 4):
        rows = slice(row, row + refs[i].shape[1])
        row = rows.stop
        refs[-1][:, rows] = added(*(ref[...] for ref in refs[i : i + 4]))


class Reduce:
    def __init__(self, kinds):
        self.kinds = kinds
        self.rows = rows_in(kinds)
        self.keep, self.got = [], []

    def start(self, keep, give):
        self.keep.append(keep)
        self.got.append(send(give, TO_CORE))

    def core(self):
        def six(rows):
            return pl.BlockSpec((2, 2, 2, 1, rows, 256), lambda k: (0, 0, 0, k, 0, 0))

        four = pl.BlockSpec((2, 1, self.rows, 256), lambda k: (0, k, 0, 0))
        parts = self.keep + self.got
        return Part(
            functools.partial(add_core_kernel, len(self.keep)),
            parts,
            [six(part.shape[4]) for part in parts],
            [shape_of((2, 4, self.rows, 256), bf16)] * 4,
            [four] * 4,
        )

    def core_added(self, results):
        b0, b1, c0, c1 = results
        self.parts = (b0, send(b1, TO_X), c0, send(c1, TO_Y))

    def both(self):
        four = pl.BlockSpec((2, 1, self.rows, 256), lambda k: (0, k, 0, 0))
        three = pl.BlockSpec((1, self.rows, 256), lambda k: (k, 0, 0))
        return Part(
            add_both_kernel, self.parts, [four] * 4, [shape_of((4, self.rows, 256), bf16)] * 4, [three] * 4
        )

    def both_added(self, results):
        b, sb, c, sc = results
        self.parts = (b, send(sb, TO_Y), c, send(sc, TO_X))

    def ring(self):
        small = shape_of((2, self.rows, 256), bf16)
        return Part(add_ring_kernel, self.parts, [WHOLE] * 4, [small] * 4, [WHOLE] * 4)

    def ring_added(self, results):
        self.parts = [results[0]] + [send(results[k], TO_Z[k]) for k in range(1, 4)]


class Owned:
    def __init__(self, *chunks):
        self.chunks = chunks
        self.kinds = [kind for chunk in chunks for kind in chunk.kinds]

    def last(self):
        parts = [part for chunk in self.chunks for part in chunk.parts]
        out = shape_of((2, rows_in(self.kinds), 256), bf16)
        return Part(add_last_kernel, parts, [WHOLE] * len(parts), [out], [WHOLE])

    def last_added(self, results):
        (mine,) = results
        near = send(mine, TO_X)
        self.parts = (mine, near, send(mine, TO_CORE), send(near, TO_CORE))

    def adam(self, order, place, states, bufs, name):
        inputs, in_specs, outs, out_specs, aliases = [place, *self.parts], [SMEM] + [WHOLE] * 4, [], [], {}
        targets = []
        for kind in self.kinds:
            l = int(kind[1:] or 0)
            if kind[0] == "a":
                targets.append(("mats", "a", pl.BlockSpec((1, 64, 4096), lambda i, l=l: (l, 0, 0))))
            if kind[0] == "m":
                targets.append(("down", "d", pl.BlockSpec((1, 256, D), lambda i, l=l: (l, 0, 0))))
            if kind[0] == "s":
                targets.append(("skip", "s", fixed((128, D))))
            if kind[0] == "t":
                targets.append(("tables", "t", fixed((64, SEQ_LEN + 3 * CH))))
                targets.append(("vectors", "v", fixed((N_VEC, 64))))
        held = []
        for name, _, spec in targets:
            inputs += list(states[name])
            in_specs += [spec] * 3
            weight = states[name][0]
            if bufs.get(name) is not None:
                held += [(len(outs) + i, buf) for i, buf in enumerate(bufs[name])]
            outs += [shape_of(weight.shape)] * 3 + [shape_of(weight.shape, bf16)]
            out_specs += [spec] * 4
        n_read = len(inputs)
        for at, buf in held:
            aliases[len(inputs)] = at
            inputs.append(buf)
            in_specs.append(ANY)
        scratch = []
        if any(t[1] == "d" for t in targets):
            scratch.append(pltpu.VMEM((D, 256), f32))
        if any(t[1] == "t" for t in targets):
            scratch.append(pltpu.VMEM((64, ROWS), f32))
            outs.append(shape_of((1, 1)))
            out_specs.append(SMEM)
        result = order(
            functools.partial(adam_kernel, self.kinds, [t[1] for t in targets], n_read, len(inputs)),
            inputs,
            in_specs,
            outs,
            out_specs,
            scratch,
            name=name,
            aliases=aliases,
        )
        for i, (name, _, _) in enumerate(targets):
            bufs[name] = result[4 * i : 4 * i + 4]
        return result[4 * len(targets) :]


def adam_kernel(kinds, targets, n_read, n_in, c_ref, *refs):
    x, c, _, _ = coords(c_ref)
    parts, ins, outs = refs[:4], refs[4 : n_read - 1], refs[n_in - 1 :]
    scratch = list(outs[4 * len(targets) :])
    loss_ref = scratch.pop(0) if "t" in targets else None
    offsets, row = {}, 0
    for kind in kinds:
        offsets[kind[0]] = row
        row += PIECE_ROWS[kind[0]]
    pieces = []
    for h in range(2):
        for g in range(2):
            for t in range(2):
                pieces.append((4 * (c ^ h) + 2 * t + (g ^ x), parts[2 * h + g].at[t]))
    for i, kind in enumerate(targets):
        state, dests = ins[3 * i : 3 * i + 3], outs[4 * i : 4 * i + 4]
        row = offsets[{"d": "m", "v": "t"}.get(kind, kind)]

        def update(at, grad, rate, state=state, dests=dests):
            weight, first, second = (ref[at] for ref in state)
            values = adam_update(weight, grad, first, second, rate)
            for dest, value in zip(dests, values):
                dest[at] = value

        if kind == "a":
            for at_row, start in ((row, 0), (offsets["m"], 2048)):
                for j, piece in pieces:
                    at = (0, slice(None), pl.ds(pl.multiple_of(start + 256 * j, 256), 256))
                    update(at, piece[at_row : at_row + 64], step_rates[0])
        if kind == "d":
            held = scratch[0]
            for j, piece in pieces:
                held[pl.ds(pl.multiple_of(64 * j, 64), 64)] = piece[row + 64 : row + 128].astype(f32)
            update((0,), held[...].T, step_rates[1])
        if kind == "s":
            for j, piece in pieces:
                for half in range(2):
                    at = (pl.ds(pl.multiple_of(16 * j, 16), 16), slice(256 * half, 256 * half + 256))
                    update(at, piece[row + 16 * half : row + 16 * half + 16], step_rates[2])
        if kind == "t":
            held = scratch[-1]
            for j, piece in pieces:
                both = piece[row : row + 16].astype(f32)
                rows = pl.ds(pl.multiple_of(8 * j, 8), 8)
                held[rows, :256] = both[:8]
                held[rows, 256:] = both[8:]
            grad = held[...]
            parts_of = [grad[:, ROW_PATCH:ROW_HEAD], grad[:, NP : NP + 2], grad[:, :NP], grad[:, ROW_HEAD:ROW_VEC]]
            update(slice(None), jnp.concatenate(parts_of, 1), step_rates[3])
            loss_ref[0, 0] = jnp.sum(grad[0:3, ROW_LOSS : ROW_LOSS + 32])
        if kind == "v":
            grad = scratch[-1][:, ROW_VEC : ROW_VEC + N_VEC].T
            update(slice(None), grad, step_rates[4])


def gather_any(mats, down, skip, tables, vectors):
    first, last = CH + CLASSES, CH + CLASSES + SEQ_LEN
    width = tables.shape[1]
    tab = jnp.concatenate(
        [
            tables[first + 2 : last],
            tables[first : first + 2],
            jnp.zeros((TAIL - 2, width), f32),
            tables[:first],
            tables[last:],
            vectors,
            jnp.zeros((ROWS - ROW_VEC - N_VEC, width), f32),
        ]
    )
    every = lax.all_gather(mats.astype(bf16), "shard", axis=1, tiled=True)
    downs = lax.all_gather(down.astype(bf16), "shard", axis=1, tiled=True)
    skips = lax.all_gather(skip.astype(bf16), "shard", axis=0, tiled=True)
    table = lax.all_gather(tab.astype(bf16), "shard", axis=1, tiled=True)

    def halves(m):
        return jnp.stack([m[:, : D // 2], m[:, D // 2 :]])

    mats_of = [(every[l, :, :2048], every[l, :, 2048:]) for l in range(LAYERS)]
    return (mats_of, [halves(downs[l]) for l in range(LAYERS)], halves(skips), table)


def reduce_any(grads):
    def ordered(kind):
        both = jnp.stack(grads[kind])
        return both.transpose(0, 1, 2, 4, 3, 5, 6).reshape((8, 8) + both.shape[5:])

    def shard_sum(value, axis):
        owned = lax.psum_scatter(value.astype(f32), "shard", scatter_dimension=axis, tiled=True)
        return lax.psum(owned.astype(bf16), "rep")

    mats, down = [], []
    for l in range(LAYERS):
        attn, mlp = ordered("a%d" % l), ordered("m%d" % l)
        both = [part[:, :, :64].transpose(1, 2, 0, 3).reshape(D, 2048) for part in (attn, mlp)]
        mats.append(jnp.concatenate(both, 1))
        down.append(mlp[:, :, 64:].transpose(0, 2, 1, 3).reshape(D, FF).T)
    skip = ordered("a1")[:, :, 64:].reshape(8, 8, 2, 16, 256).transpose(1, 0, 3, 2, 4).reshape(2 * D, D)
    turned = ordered("a0")[:, :, 64:].reshape(8, 8, 2, 8, 256).transpose(1, 0, 3, 2, 4).reshape(D, ROWS)
    return (shard_sum(jnp.stack(mats), 1), shard_sum(jnp.stack(down), 1), shard_sum(skip, 0), shard_sum(turned, 0))


def time_token(timesteps):
    half_width = D // 2
    freqs_row = jnp.exp(-math.log(10000.0) * jnp.arange(half_width, dtype=f32) / half_width)
    angles = timesteps.astype(f32)[:, None] * freqs_row[None, :]
    return jnp.concatenate([jnp.cos(angles), jnp.sin(angles)], -1)


def adam_update(weight, grad, moment_one, moment_two, step_rate):
    grad = grad.astype(f32)
    moment_one = beta_one * moment_one + (1.0 - beta_one) * grad
    moment_two = beta_two * moment_two + (1.0 - beta_two) * grad * grad
    first_hat = moment_one / (1.0 - beta_one**STEP)
    second_hat = moment_two / (1.0 - beta_two**STEP)
    weight = weight - step_rate * (first_hat / (jnp.sqrt(second_hat) + epsilon) + weight_decay * weight)
    return (moment_one, moment_two, weight, weight.astype(bf16))


def local(
    fast,
    latents,
    target_noise,
    labels,
    timesteps,
    loss_weight,
    layer_mats,
    layer_mats_first,
    layer_mats_second,
    down_mats,
    down_first,
    down_second,
    skip_mat,
    skip_first,
    skip_second,
    tables,
    tables_first,
    tables_second,
    vectors,
    vectors_first,
    vectors_second,
):
    n_seqs = latents.shape[0]
    if fast:
        rep, shard = lax.axis_index("rep"), lax.axis_index("shard")
        place = jnp.stack([rep // 2, rep % 2, shard // 2, shard % 2]).astype(jnp.int32)
    else:
        place = jnp.zeros((4,), jnp.int32)
    order = Order()
    time_rows = jnp.pad(time_token(timesteps)[:, None], ((0, 0), (0, TAIL - 1), (0, 0)))
    mats, downs = [None, None], [None, None]
    forward = {}

    def attention(l):
        if l == 0:
            inputs = (labels, latents, time_rows, table, vec, mats[0][0])
        else:
            inputs = (forward["x1"], forward["x0"], ws, vec, mats[1][0])
        forward["a%d" % l] = call_attention(order, l == 0, n_seqs, inputs)
        if l == 0:
            forward["x0"] = forward["a0"][0]

    def mlp():
        out = call_mlp(order, 0, n_seqs, forward["a0"][5], vec, mats[0][1], downs[0])
        forward["m0"] = out
        forward["x1"] = out[3]

    if fast:
        args = (layer_mats, down_mats, skip_mat, tables.T, vectors, loss_weight)
        one, two, three = (Gather(place, kinds, args) for kinds in GATHER_CHUNKS)
        one.packed(*order.fuse([one.pack()], "pack_0"))
        joined, packed = order.fuse([one.join_ring(), two.pack()], "join_ring_0")
        one.ring_joined(joined)
        two.packed(packed)
        one.pair_joined(*order.fuse([one.join_pair()], "join_pair_0"))
        joined, own = order.fuse([two.join_ring(), one.join_own()], "join_ring_1")
        two.ring_joined(joined)
        one.own_joined(own)
        one.rest_joined(*order.fuse([one.join_rest()], "join_rest_0"))
        (wa0, table, vec, weight_total), packed = order.fuse([one.assemble(), three.pack()], "assemble_0")
        mats[0] = (wa0, None)
        three.packed(packed)
        two.pair_joined(*order.fuse([two.join_pair()], "join_pair_1"))
        attention(0)
        joined, own = order.fuse([three.join_ring(), two.join_own()], "join_ring_2")
        three.ring_joined(joined)
        two.own_joined(own)
        two.rest_joined(*order.fuse([two.join_rest()], "join_rest_1"))
        ((w10, downs[0]),) = order.fuse([two.assemble()], "assemble_1")
        mats[0] = (wa0, w10)
        three.pair_joined(*order.fuse([three.join_pair()], "join_pair_2"))
        mlp()
        three.own_joined(*order.fuse([three.join_own()], "join_own_2"))
        three.rest_joined(*order.fuse([three.join_rest()], "join_rest_2"))
        ((wa1, ws, w11, downs[1]),) = order.fuse([three.assemble()], "assemble_2")
        mats[1] = (wa1, w11)
        attention(1)
    else:
        mats, downs, ws, table = gather_any(layer_mats, down_mats, skip_mat, tables, vectors)
        vec = table[ROW_VEC : ROW_VEC + N_VEC].astype(f32)
        weight_total = lax.psum(jnp.sum(loss_weight.astype(f32)), ALL).reshape(1, 1)
        attention(0)
        mlp()
        attention(1)

    grads, small = {}, {}

    def mlp_turn():
        mid = forward["a1"][5]
        out = call_mlp_turn(
            order, n_seqs, weight_total, loss_weight, place, mid, vec, mats[1][1], downs[1], target_noise, table
        )
        grads["m1"], small["m1"], small["f1"] = out[1:3], out[3], out[4]
        return out[0], out[5], out[6]

    def mlp_back(dout):
        normed, act, slope = forward["m0"][:3]
        out = call_mlp_backward(
            order, 0, n_seqs, place, dout, act, slope, normed, forward["a0"][5], vec, mats[0][1], downs[0]
        )
        grads["m0"], small["m0"], small["f0"] = out[1:3], out[3], out[4]
        return out[0]

    def attention_back(l, dmid, more):
        x, normed, qkv, lse, att, _ = forward["a%d" % l]
        out = call_attention_backward(order, l, n_seqs, place, dmid, x, normed, qkv, lse, att, vec, mats[l][0], more)
        grads["a%d" % l] = out[:2]
        return out[2:]

    bufs = {}
    if fast:
        first, second, third = (Reduce(kinds) for kinds in REDUCE_CHUNKS)
        states = {
            "mats": (layer_mats, layer_mats_first, layer_mats_second),
            "down": (down_mats, down_first, down_second),
            "skip": (skip_mat, skip_first, skip_second),
            "tables": (tables.T, tables_first.T, tables_second.T),
            "vectors": (vectors, vectors_first, vectors_second),
        }
    dmid, dhead, small_head = mlp_turn()
    if fast:
        first.start(*grads["m1"])
    dx, d0, small["a1"] = attention_back(1, dmid, (forward["x1"], forward["x0"], ws))
    if fast:
        first.start(*grads["a1"])
        first.core_added(*order.fuse([first.core()], "add_core_1", grid=(4,)))
    dmid = mlp_back(dx)
    if fast:
        second.start(*grads["m0"])
        first.both_added(*order.fuse([first.both()], "add_both_1", grid=(4,)))
        second.core_added(*order.fuse([second.core()], "add_core_2", grid=(4,)))
    last = (labels, d0, latents, dhead, small["m0"], small["m1"], small["a1"], small_head, small["f0"], small["f1"])
    attention_back(0, dmid, last)
    if fast:
        upper, lower = Owned(first), Owned(second, third)
        third.start(*grads["a0"])
        first.ring_added(*order.fuse([first.ring()], "add_ring_1"))
        second.both_added(*order.fuse([second.both()], "add_both_2", grid=(4,)))
        third.core_added(*order.fuse([third.core()], "add_core_3", grid=(4,)))
        second.ring_added(*order.fuse([second.ring()], "add_ring_2"))
        upper.last_added(*order.fuse([upper.last()], "add_last_1"))
        third.both_added(*order.fuse([third.both()], "add_both_3", grid=(4,)))
        third.ring_added(*order.fuse([third.ring()], "add_ring_3"))
        upper.adam(order, place, states, bufs, "adam_1")
        lower.last_added(*order.fuse([lower.last()], "add_last_0"))
        (loss,) = lower.adam(order, place, states, bufs, "adam_0")
        loss_sum = loss[0, 0]
        results = [bufs[name] for name in ("mats", "down", "skip", "tables", "vectors")]
        results[3] = [part.T for part in results[3]]
    else:
        loss_sum = lax.psum(small_head[2, 0], ALL)
        g_mats, g_down, g_skip, g_turned = reduce_any(grads)
        g_rows = g_turned.T
        g_tables = jnp.concatenate(
            [g_rows[ROW_PATCH:ROW_HEAD], g_rows[NP : NP + 2], g_rows[:NP], g_rows[ROW_HEAD:ROW_VEC]]
        )
        g_vectors = g_rows[ROW_VEC : ROW_VEC + N_VEC]
        results = [
            adam_update(layer_mats, g_mats, layer_mats_first, layer_mats_second, step_rates[0]),
            adam_update(down_mats, g_down, down_first, down_second, step_rates[1]),
            adam_update(skip_mat, g_skip, skip_first, skip_second, step_rates[2]),
            adam_update(tables, g_tables, tables_first, tables_second, step_rates[3]),
            adam_update(vectors, g_vectors, vectors_first, vectors_second, step_rates[4]),
        ]
    return (loss_sum, weight_total[0, 0], *(part for result in results for part in result))


GATHER_CHUNKS = (("a0", "t"), ("m0",), ("a1", "s", "m1"))
REDUCE_CHUNKS = (("m1", "a1", "s"), ("m0",), ("a0", "t"))


def solution(mesh):
    one, two, rows = P(None, "shard", None), P("shard", None), P(None, "shard")
    every = P(ALL, None, None)
    placed = (every, every, P(ALL), P(ALL), P(ALL), *[one] * 6, *[two] * 3, *[rows] * 6)
    fast = mesh.shape["rep"] == 4 and mesh.shape["shard"] == 8
    return jax.shard_map(
        functools.partial(local, fast),
        mesh=mesh,
        in_specs=placed,
        out_specs=(P(), P(), *[one] * 8, *[two] * 4, *[rows] * 8),
        check_vma=False,
    )
```

```python
import functools
import math

import jax
import jax.numpy as jnp
from jax import lax
from jax.experimental import pallas as pl
from jax.experimental.pallas import tpu as pltpu
from jax.sharding import PartitionSpec as P

D = 512
HEADS = 8
HD = 64
FF = 2048
CH = 16
NP = 256
CLASSES = 16
LAYERS = 2
STEP = 10
SEQ_LEN = 258

beta_one = 0.5
beta_two = 0.75
epsilon = 1e-08
weight_decay = 0.05
step_rates = (0.05, 0.03, 0.03, 0.05, 0.3)

TAIL = 16
T = NP + TAIL
ROW_PATCH = T
ROW_CLASS = ROW_PATCH + CH
ROW_HEAD = ROW_CLASS + CLASSES
ROW_VEC = ROW_HEAD + CH
N_VEC = LAYERS * (6 + FF // D) + 4
ROWS = D
ROW_WEIGHT = ROWS - 1
ROW_LOSS = 384
bf16 = jnp.bfloat16
f32 = jnp.float32
ALL = ("rep", "shard")
MIB = 1024 * 1024
MARGIN = 10 * MIB
WIDE = ("pack_0",)
ANY = pl.BlockSpec(memory_space=pl.ANY)
SMEM = pl.BlockSpec(memory_space=pltpu.SMEM)
WHOLE = pl.BlockSpec(memory_space=pltpu.VMEM)


def room(shape, dtype):
    size = jnp.dtype(dtype).itemsize
    rows, columns = ((1,) + tuple(shape))[-2:]
    rows, columns = -(-rows * size // 32) * 32 // size, -(-columns // 128) * 128
    return math.prod(shape[:-2]) * rows * columns * size


class Part:
    def __init__(self, body, inputs, in_specs, outs, out_specs, scratch=()):
        self.body, self.inputs, self.in_specs = body, list(inputs), list(in_specs)
        self.outs, self.out_specs, self.scratch = list(outs), list(out_specs), list(scratch)


class Order:
    def __init__(self):
        self.last = None

    def __call__(self, kernel, inputs, in_specs, outs, out_specs, scratch=(), grid=(1,), name=None, aliases=None):
        part = Part(kernel, inputs, in_specs, outs, out_specs, scratch)
        return self.fuse([part], name, grid=grid, aliases=aliases)[0]

    def fuse(self, parts, name, after=(), grid=(1,), aliases=None):
        extra = list(after) + ([] if self.last is None else [self.last])
        inputs = [value for part in parts for value in part.inputs]
        counts = [(len(p.inputs), len(p.outs), len(p.scratch)) for p in parts]
        ends = [sum(c[i] for c in counts) for i in range(3)]
        skip = len(extra)

        def body(*refs):
            groups = (refs[: ends[0]], refs[ends[0] + skip : ends[0] + skip + ends[1]], refs[ends[0] + skip + ends[1] :])
            at = [0, 0, 0]
            rest = []
            for part, count in zip(parts, counts):
                own = [r for i in range(3) for r in groups[i][at[i] : at[i] + count[i]]]
                at = [i + n for i, n in zip(at, count)]
                more = part.body(*own)
                if more is not None:
                    next(more)
                    rest.append(more)
            for more in rest:
                next(more, None)

        need = 0
        for part in parts:
            for spec, value in (*zip(part.in_specs, part.inputs), *zip(part.out_specs, part.outs)):
                if spec is not ANY and spec is not SMEM:
                    need += 2 * room(spec.block_shape or value.shape, value.dtype)
            need += sum(room(item.shape, item.dtype) for item in part.scratch if hasattr(item, "inner_aval") or hasattr(item, "shape"))
        result = pl.pallas_call(
            body,
            grid=grid,
            in_specs=[spec for part in parts for spec in part.in_specs] + [ANY] * skip,
            out_specs=[spec for part in parts for spec in part.out_specs],
            out_shape=[out for part in parts for out in part.outs],
            scratch_shapes=[item for part in parts for item in part.scratch],
            input_output_aliases=aliases or {},
            cost_estimate=pl.CostEstimate(flops=50_000_000_000, bytes_accessed=100_000_000, transcendentals=0),
            compiler_params=pltpu.CompilerParams(vmem_limit_bytes=56 * MIB if name in WIDE else min(need + MARGIN, 56 * MIB)),
            name=name,
        )(*inputs, *extra)
        self.last = result[0]
        split, at = [], 0
        for part in parts:
            split.append(result[at : at + len(part.outs)])
            at += len(part.outs)
        return split


def dot(left, right):
    return jnp.dot(left, right, preferred_element_type=f32)


def dot_t(left, right):
    return lax.dot_general(left, right, (((1,), (1,)), ((), ())), preferred_element_type=f32)


def t_dot(left, right):
    return lax.dot_general(left, right, (((0,), (0,)), ((), ())), preferred_element_type=f32)


def norm_hat(stream):
    center = jnp.mean(stream, -1, keepdims=True)
    offset = stream - center
    spread = jnp.mean(offset * offset, -1, keepdims=True)
    inverse = lax.rsqrt(spread + 1e-05)
    return (offset * inverse, inverse)


def norm_back(hat, inverse, gain, grad):
    scaled = grad * gain
    first = jnp.mean(scaled, -1, keepdims=True)
    second = jnp.mean(scaled * hat, -1, keepdims=True)
    return inverse * (scaled - first - hat * second)


def rows_sum(values):
    return jnp.sum(values, 0, keepdims=True)


LSE = 16


def apart(rows, scale):
    lane = lax.broadcasted_iota(jnp.int32, (1, 2 * HD), 1)
    return jnp.concatenate([rows * jnp.where(lane // HD == e, scale, 0.0).astype(bf16) for e in range(2)], 0)


def block_mask():
    row = lax.broadcasted_iota(jnp.int32, (TAIL, D), 0)
    lane = lax.broadcasted_iota(jnp.int32, (TAIL, D), 1)
    return (row // 2 == lane // HD, row % 2 == 0)


def spread_tail(rows, scale):
    own, first = block_mask()
    wide = rows.astype(f32)
    both = jnp.where(first, wide[0:1], wide[1:2]) * scale
    return jnp.where(own, both, 0.0).astype(bf16)


def gather_tail(values):
    own, first = block_mask()
    kept = jnp.where(own, values, 0.0)
    zero = rows_sum(jnp.where(first, kept, 0.0))
    one = rows_sum(jnp.where(first, 0.0, kept))
    row = lax.broadcasted_iota(jnp.int32, (TAIL, D), 0)
    return jnp.where(row == 0, zero, jnp.where(row == 1, one, 0.0))


def mask_keys(scores):
    tail = scores[NP:]
    row = lax.broadcasted_iota(jnp.int32, tail.shape, 0)
    return jnp.concatenate([scores[:NP], jnp.where(row < SEQ_LEN - NP, tail, -1e30)], 0)


def softmax_rows(scores):
    top = jnp.max(scores, 0, keepdims=True)
    expon = jnp.exp(scores - top)
    total = jnp.sum(expon, 0, keepdims=True)
    return (expon * (1.0 / total)).astype(bf16), top + jnp.log(total)


def pipelined(count, *stages):
    held = {}
    for step in range(count + len(stages) - 1):
        for i, stage in enumerate(stages):
            if 0 <= step - i < count:
                held[step - i] = stage(step - i, held.get(step - i))


def attention_forward(stream, layer_id, vec_ref, wa_ref, h_ref, qkv_ref, lse_ref, o_ref, mid_ref):
    base = layer_id * (6 + FF // D)
    hat, _ = norm_hat(stream)
    normed = (hat * vec_ref[base : base + 1] + vec_ref[base + 1 : base + 2]).astype(bf16)
    h_ref[0] = normed
    qkv_ref[0] = dot(normed, wa_ref[:, : 3 * D]).astype(bf16)
    scale = HD**-0.5

    def cut(part, pair):
        return qkv_ref[0, :, part * D + 128 * pair : part * D + 128 * pair + 128]

    def score(pair, _):
        return dot_t(cut(1, pair), apart(cut(0, pair)[:NP], scale))

    def weigh(pair, scores):
        weights, log_total = softmax_rows(mask_keys(scores))
        lse_ref[0, 2 * pair : 2 * pair + 1] = log_total[:, :NP]
        lse_ref[0, 2 * pair + 1 : 2 * pair + 2] = log_total[:, NP:]
        return weights

    def mix(pair, weights):
        values = apart(cut(2, pair), 1.0)
        out = t_dot(weights[:, :NP], values[:T]) + t_dot(weights[:, NP:], values[T:])
        o_ref[0, :NP, 128 * pair : 128 * pair + 128] = out.astype(bf16)

    tails = spread_tail(qkv_ref[0, NP:, :D], scale)
    weights, log_total = softmax_rows(mask_keys(dot_t(qkv_ref[0, :, D : 2 * D], tails)))
    lse_ref[0, HEADS : HEADS + 1, :TAIL] = log_total
    o_ref[0, NP:] = gather_tail(t_dot(weights, qkv_ref[0, :, 2 * D :])).astype(bf16)
    pipelined(HEADS // 2, score, weigh, mix)
    mid_ref[0] = stream + dot(o_ref[0], wa_ref[:, 3 * D :]) + vec_ref[base + 4 : base + 5]


def embed_attention_kernel(
    label_ref, latent_ref, time_ref, tab_ref, vec_ref, wa_ref, x_ref, h_ref, qkv_ref, lse_ref, o_ref, mid_ref
):
    b = pl.program_id(0)
    patch_rows = t_dot(latent_ref[0], tab_ref[ROW_PATCH:ROW_CLASS]) + vec_ref[N_VEC - 1 : N_VEC]
    row = lax.broadcasted_iota(jnp.int32, (TAIL, CLASSES), 0)
    column = lax.broadcasted_iota(jnp.int32, (TAIL, CLASSES), 1)
    choose = jnp.where((row == 1) & (column == label_ref[b]), 1.0, 0.0).astype(bf16)
    tail_rows = time_ref[0] + dot(choose, tab_ref[ROW_CLASS:ROW_HEAD])
    stream = jnp.concatenate([patch_rows, tail_rows], 0) + tab_ref[:T].astype(f32)
    x_ref[0] = stream
    attention_forward(stream, 0, vec_ref, wa_ref, h_ref, qkv_ref, lse_ref, o_ref, mid_ref)


def skip_attention_kernel(x1_ref, x0_ref, ws_ref, vec_ref, wa_ref, x_ref, h_ref, qkv_ref, lse_ref, o_ref, mid_ref):
    one = x1_ref[0].astype(bf16)
    zero = x0_ref[0].astype(bf16)
    halves = [dot(one, ws_ref[i, :D]) + dot(zero, ws_ref[i, D:]) for i in range(2)]
    stream = jnp.concatenate(halves, 1) + vec_ref[N_VEC - 2 : N_VEC - 1]
    x_ref[0] = stream
    attention_forward(stream, 1, vec_ref, wa_ref, h_ref, qkv_ref, lse_ref, o_ref, mid_ref)


def mlp_forward(layer_id, mid_ref, vec_ref, w1_ref, w2_ref, h_ref, act_ref, slope_ref):
    base = layer_id * (6 + FF // D)
    hat, _ = norm_hat(mid_ref[...])
    normed = (hat * vec_ref[base + 2 : base + 3] + vec_ref[base + 3 : base + 4]).astype(bf16)
    h_ref[...] = normed
    const = math.sqrt(2.0 / math.pi)

    for j in range(FF // D):
        cols = slice(D * j, D * j + D)
        pre = dot(normed, w1_ref[:, cols]) + vec_ref[base + 6 + j : base + 7 + j]
        square = pre * pre
        half = 0.5 + 0.5 * jnp.tanh(pre * (const + (const * 0.044715) * square))
        act = pre * half
        act_ref[:, cols] = act.astype(bf16)
        slope = half + act * (1.0 - half) * (2.0 * const + (6.0 * const * 0.044715) * square)
        slope_ref[:, cols] = slope.astype(bf16)
    total = jnp.concatenate([dot(act_ref[...], w2_ref[i]) for i in range(2)], 1)
    return mid_ref[...] + total + vec_ref[base + 5 : base + 6]


def mlp_kernel(layer_id, mid_ref, vec_ref, w1_ref, w2_ref, h_ref, act_ref, slope_ref, out_ref):
    out_ref[...] = mlp_forward(layer_id, mid_ref, vec_ref, w1_ref, w2_ref, h_ref, act_ref, slope_ref)


def head_backward(b, total_ref, weight_ref, out, noise_ref, tab_ref, vec_ref, dhead_ref, small_ref):
    hat, inverse = norm_hat(out[:NP])
    gain = vec_ref[N_VEC - 4 : N_VEC - 3]
    final = (hat * gain + vec_ref[N_VEC - 3 : N_VEC - 2]).astype(bf16)
    head = tab_ref[ROW_HEAD:ROW_VEC]
    errors = dot_t(head, final) - noise_ref[0].astype(f32)
    per_seq = jnp.sum(errors * errors) * (1.0 / (CH * NP))
    weight = weight_ref[b].astype(f32)
    scale = (jnp.ones((1, 1), f32) / total_ref[0, 0]) * weight * (2.0 / (CH * NP))
    grad_pred = (scale * errors).astype(bf16)
    dhead_ref[...] += dot(grad_pred, final)
    grad = t_dot(grad_pred, head)
    small_ref[0:1] += rows_sum(grad * hat)
    small_ref[1:2] += rows_sum(grad)
    small_ref[2:3] += jnp.full((1, D), weight * per_seq, f32)
    return jnp.concatenate([norm_back(hat, inverse, gain, grad), jnp.zeros((TAIL, D), f32)], 0)


def rows_of(b):
    return pl.ds(pl.multiple_of(T * b, TAIL), T)


def coords(c_ref):
    return tuple(c_ref[i] for i in range(4))


def place_of(c_ref, shard):
    _, _, z, y = coords(c_ref)
    return ((shard % 2) ^ y, (shard // 2 - z) & 3)


def sub_of(c_ref, h, t, g):
    x, c, _, _ = coords(c_ref)
    return 4 * (c ^ h) + 2 * t + (g ^ x)


def scatter_pieces(c_ref, keep_ref, send_ref, at, piece):
    for h, dest in ((0, keep_ref), (1, send_ref)):
        for t in range(2):
            for g in range(2):
                j = sub_of(c_ref, h, t, g)
                for s in range(8):
                    f, k = place_of(c_ref, s)
                    value = piece(j, s)
                    dest[t, g, f, k, at : at + value.shape[0]] = value


def by_columns(ref):
    return lambda j, s: ref[64 * s : 64 * s + 64, pl.ds(pl.multiple_of(256 * j, 256), 256)]


def by_rows(ref):
    return lambda j, s: ref[pl.ds(pl.multiple_of(64 * j, 64), 64), 256 * s : 256 * s + 256]


def mlp_backward(
    layer_id, rows, dout, slope_ref, mid_ref, vec_ref, w1_ref, w2_ref, dmid_ref, small_ref, dfc1b_ref, right_s, grads_s
):
    base = layer_id * (6 + FF // D)
    low = dout.astype(bf16)
    right_s[rows] = low

    def enter(j, _):
        block = slice(D * j, D * j + D)
        return dot_t(low[:, :256], w2_ref[0, block]) + dot_t(low[:, 256:], w2_ref[1, block])

    def bend(j, grad_act):
        cols = slice(D * j, D * j + D)
        grad_pre = grad_act * slope_ref[:, cols].astype(f32)
        dfc1b_ref[:, cols] += rows_sum(grad_pre)
        grad = grad_pre.astype(bf16)
        grads_s[rows, cols] = grad
        return grad

    total = []

    def leave(j, grad):
        part = dot_t(grad, w1_ref[:, D * j : D * j + D])
        total.append(part if not total else total[-1] + part)

    pipelined(FF // D, enter, bend, leave)
    grad_normed = total[-1]
    hat, inverse = norm_hat(mid_ref[...])
    small_ref[0:1] += rows_sum(grad_normed * hat)
    small_ref[1:2] += rows_sum(grad_normed)
    small_ref[2:3] += rows_sum(dout)
    dmid_ref[...] = dout + norm_back(hat, inverse, vec_ref[base + 2 : base + 3], grad_normed)


def mlp_weights(c_ref, keep_ref, send_ref, left_s, right_s, grads_s, acts_s, tile_s):
    tile_s[...] = t_dot(left_s[...], grads_s[...]).astype(bf16)
    scatter_pieces(c_ref, keep_ref, send_ref, 0, by_columns(tile_s))
    tile_s[...] = t_dot(right_s[...], acts_s[...]).astype(bf16)
    scatter_pieces(c_ref, keep_ref, send_ref, 64, by_rows(tile_s))


def mlp_backward_kernel(
    layer_id,
    c_ref,
    dout_ref,
    act_ref,
    slope_ref,
    h_ref,
    mid_ref,
    vec_ref,
    w1_ref,
    w2_ref,
    dmid_ref,
    keep_ref,
    send_ref,
    small_ref,
    dfc1b_ref,
    left_s,
    right_s,
    grads_s,
    acts_s,
    tile_s,
):
    b = pl.program_id(0)

    @pl.when(b == 0)
    def _():
        small_ref[...] = jnp.zeros_like(small_ref)
        dfc1b_ref[...] = jnp.zeros_like(dfc1b_ref)

    rows = rows_of(b)
    left_s[rows] = h_ref[...]
    acts_s[rows] = act_ref[...]
    weights = (mid_ref, vec_ref, w1_ref, w2_ref)
    mlp_backward(layer_id, rows, dout_ref[...], slope_ref, *weights, dmid_ref, small_ref, dfc1b_ref, right_s, grads_s)

    @pl.when(b == pl.num_programs(0) - 1)
    def _():
        mlp_weights(c_ref, keep_ref, send_ref, left_s, right_s, grads_s, acts_s, tile_s)


def mlp_turn_kernel(
    total_ref,
    weight_ref,
    c_ref,
    mid_ref,
    vec_ref,
    w1_ref,
    w2_ref,
    noise_ref,
    tab_ref,
    dmid_ref,
    keep_ref,
    send_ref,
    small_ref,
    dfc1b_ref,
    dhead_ref,
    small_head_ref,
    left_s,
    right_s,
    grads_s,
    acts_s,
    tile_s,
    slope_s,
):
    b = pl.program_id(0)

    @pl.when(b == 0)
    def _():
        for ref in (small_ref, dfc1b_ref, dhead_ref, small_head_ref):
            ref[...] = jnp.zeros_like(ref)

    rows = rows_of(b)
    weights = (mid_ref, vec_ref, w1_ref, w2_ref)
    out = mlp_forward(1, *weights, left_s.at[rows], acts_s.at[rows], slope_s)
    dout = head_backward(b, total_ref, weight_ref, out, noise_ref, tab_ref, vec_ref, dhead_ref, small_head_ref)
    mlp_backward(1, rows, dout, slope_s, *weights, dmid_ref, small_ref, dfc1b_ref, right_s, grads_s)

    @pl.when(b == pl.num_programs(0) - 1)
    def _():
        mlp_weights(c_ref, keep_ref, send_ref, left_s, right_s, grads_s, acts_s, tile_s)


def last_backward_kernel(
    layer_id,
    c_ref,
    dmid_ref,
    x_ref,
    h_ref,
    qkv_ref,
    lse_ref,
    o_ref,
    vec_ref,
    wa_ref,
    label_ref,
    d0_ref,
    latent_ref,
    dhead_ref,
    small_m0,
    small_m1,
    small_a1,
    small_head,
    dfc1b0,
    dfc1b1,
    keep_ref,
    send_ref,
    left_s,
    outs_s,
    grads_s,
    lows_s,
    dqkv_s,
    tile_s,
    small_ref,
    table_s,
):
    b = pl.program_id(0)

    @pl.when(b == 0)
    def _():
        table_s[...] = jnp.zeros_like(table_s)

    refs = (dmid_ref, x_ref, h_ref, qkv_ref, lse_ref, o_ref, vec_ref, wa_ref, small_ref, left_s, outs_s, grads_s, lows_s, dqkv_s)
    embed_grads(b, label_ref, attention_backward(layer_id, *refs) + d0_ref[0], latent_ref, table_s)

    @pl.when(b == pl.num_programs(0) - 1)
    def _():
        attention_weights(c_ref, keep_ref, send_ref, left_s, outs_s, grads_s, lows_s, tile_s)
        table_s[ROW_HEAD:ROW_VEC] = dhead_ref[...]
        row = ROW_VEC
        for own, mlp, fc1b in ((small_ref, small_m0, dfc1b0), (small_a1, small_m1, dfc1b1)):
            table_s[row : row + 2] = own[0:2]
            table_s[row + 2 : row + 4] = mlp[0:2]
            table_s[row + 4 : row + 5] = own[2:3]
            table_s[row + 5 : row + 6] = mlp[2:3]
            for i in range(FF // D):
                table_s[row + 6 + i : row + 7 + i] = fc1b[:, D * i : D * i + D]
            row += 6 + FF // D
        table_s[row : row + 2] = small_head[0:2]
        table_s[row + 2 : row + 3] = small_a1[3:4]
        table_pieces(c_ref, small_head[2:3, 0:1], table_s[...], keep_ref, send_ref, 64)


def attention_backward(
    layer_id, dmid_ref, x_ref, h_ref, qkv_ref, lse_ref, o_ref, vec_ref, wa_ref, small_ref, left_s, outs_s, grads_s, lows_s, dqkv_s
):
    b = pl.program_id(0)
    rows = rows_of(b)
    base = layer_id * (6 + FF // D)

    @pl.when(b == 0)
    def _():
        small_ref[...] = jnp.zeros_like(small_ref)

    dmid = dmid_ref[0]
    low = dmid.astype(bf16)
    left_s[rows] = h_ref[0]
    outs_s[rows] = o_ref[0]
    lows_s[rows] = low
    grad_att = dot_t(low, wa_ref[:, 3 * D :]).astype(bf16)
    scale = HD**-0.5

    def cut(part, pair):
        return qkv_ref[0, :, part * D + 128 * pair : part * D + 128 * pair + 128]

    def put(part, pair, value):
        dqkv_s[: value.shape[0], part * D + 128 * pair : part * D + 128 * pair + 128] = value.astype(bf16)

    tails, tail_douts = spread_tail(qkv_ref[0, NP:, :D], scale), spread_tail(grad_att[NP:], 1.0)
    weights = jnp.exp(mask_keys(dot_t(qkv_ref[0, :, D : 2 * D], tails)) - lse_ref[0, HEADS : HEADS + 1, :TAIL])
    grad_w = dot_t(qkv_ref[0, :, 2 * D :], tail_douts)
    grad_s = (weights * (grad_w - rows_sum(weights * grad_w))).astype(bf16)
    tail_dk = dot(grad_s, tails)
    tail_dv = dot(weights.astype(bf16), tail_douts)
    dqkv_s[NP:, :D] = (gather_tail(t_dot(grad_s, qkv_ref[0, :, D : 2 * D])) * scale).astype(bf16)

    def score(pair, _):
        queries = apart(cut(0, pair)[:NP], scale)
        douts = apart(grad_att[:NP, 128 * pair : 128 * pair + 128], 1.0)
        return dot_t(cut(1, pair), queries), dot_t(cut(2, pair), douts), queries, douts

    def weigh(pair, held):
        scores, grad_w, queries, douts = held
        log_total = jnp.concatenate([lse_ref[0, 2 * pair + e : 2 * pair + e + 1] for e in range(2)], 1)
        weights = jnp.exp(mask_keys(scores) - log_total)
        grad_s = weights * (grad_w - rows_sum(weights * grad_w))
        return weights.astype(bf16), grad_s.astype(bf16), queries, douts

    def mix(pair, held):
        weights, grad_s, queries, douts = held
        cols = slice(128 * pair, 128 * pair + 128)
        keys = apart(cut(1, pair), scale)
        put(0, pair, t_dot(grad_s[:, :NP], keys[:T]) + t_dot(grad_s[:, NP:], keys[T:]))
        put(1, pair, dot(grad_s, queries) + tail_dk[:, cols])
        put(2, pair, dot(weights, douts) + tail_dv[:, cols])

    pipelined(HEADS // 2, score, weigh, mix)
    grads_s[rows] = dqkv_s[...]
    grad_normed = dot_t(dqkv_s[...], wa_ref[:, : 3 * D])
    hat, inverse = norm_hat(x_ref[0])
    small_ref[0:1] += rows_sum(grad_normed * hat)
    small_ref[1:2] += rows_sum(grad_normed)
    small_ref[2:3] += rows_sum(dmid)
    return dmid + norm_back(hat, inverse, vec_ref[base : base + 1], grad_normed)


def attention_weights(c_ref, keep_ref, send_ref, left_s, outs_s, grads_s, lows_s, tile_s):
    tile_s[:, : 3 * D] = t_dot(left_s[...], grads_s[...]).astype(bf16)
    tile_s[:, 3 * D :] = t_dot(outs_s[...], lows_s[...]).astype(bf16)
    scatter_pieces(c_ref, keep_ref, send_ref, 0, by_columns(tile_s))


def middle_backward_kernel(
    layer_id,
    c_ref,
    dmid_ref,
    x_ref,
    h_ref,
    qkv_ref,
    lse_ref,
    o_ref,
    vec_ref,
    wa_ref,
    x1_ref,
    x0_ref,
    ws_ref,
    keep_ref,
    send_ref,
    d1_ref,
    d0_ref,
    small_ref,
    left_s,
    outs_s,
    grads_s,
    lows_s,
    dqkv_s,
    tile_s,
    both_s,
    skip_s,
    skip_tile_s,
):
    b = pl.program_id(0)
    refs = (dmid_ref, x_ref, h_ref, qkv_ref, lse_ref, o_ref, vec_ref, wa_ref, small_ref)
    grad = attention_backward(layer_id, *refs, left_s, outs_s, grads_s, lows_s, dqkv_s)
    low = grad.astype(bf16)
    small_ref[3:4] += rows_sum(grad)
    rows = rows_of(b)
    both_s[rows, :D] = x1_ref[0].astype(bf16)
    both_s[rows, D:] = x0_ref[0].astype(bf16)
    skip_s[rows] = low
    for u, dest in ((0, d1_ref), (1, d0_ref)):
        cols = slice(D * u, D * u + D)
        dest[0] = dot_t(low[:, :256], ws_ref[0, cols]) + dot_t(low[:, 256:], ws_ref[1, cols])

    @pl.when(b == pl.num_programs(0) - 1)
    def _():
        attention_weights(c_ref, keep_ref, send_ref, left_s, outs_s, grads_s, lows_s, tile_s)
        skip_tile_s[...] = t_dot(both_s[...], skip_s[...]).astype(bf16)
        for half in range(2):

            def piece(j, s, half=half):
                rows = pl.ds(pl.multiple_of(128 * s + 16 * j, 16), 16)
                return skip_tile_s[rows, 256 * half : 256 * half + 256]

            scatter_pieces(c_ref, keep_ref, send_ref, 64 + 16 * half, piece)


def embed_grads(b, label_ref, grad, latent_ref, table_s):
    table_s[:T] += grad
    patch = grad[:NP]
    last = ROW_VEC + N_VEC - 1
    table_s[last : last + 1] += rows_sum(patch)
    table_s[ROW_PATCH:ROW_CLASS] += dot(latent_ref[0], patch.astype(bf16))
    row = lax.broadcasted_iota(jnp.int32, (CLASSES, D), 0)
    table_s[ROW_CLASS:ROW_HEAD] += jnp.where(row == label_ref[b], grad[NP + 1 : NP + 2], 0.0)


def table_pieces(c_ref, loss, table, keep_ref, send_ref, at):
    x, c, z, y = coords(c_ref)
    me = (x * 2 + c) * 8 + z * 2 + y
    high = loss.astype(bf16).astype(f32)
    middle = (loss - high).astype(bf16).astype(f32)
    small = loss - high - middle
    row = lax.broadcasted_iota(jnp.int32, (ROWS, D), 0)
    kind = lax.broadcasted_iota(jnp.int32, (ROWS, D), 1) % 8
    slots = jnp.where(kind == 0, high, jnp.where(kind == 1, middle, jnp.where(kind == 2, small, 0.0)))
    turned = jnp.where(row == ROW_LOSS + me, slots, table).T
    for s in range(8):
        f, k = place_of(c_ref, s)
        for j in range(8):
            rows = slice(64 * s + 8 * j, 64 * s + 8 * j + 8)
            piece = jnp.concatenate([turned[rows, :256], turned[rows, 256:]], 0).astype(bf16)
            h, t, g = (j // 4) ^ c, j // 2 % 2, (j % 2) ^ x

            @pl.when(h == 0)
            def _(piece=piece, t=t, g=g, f=f, k=k):
                keep_ref[t, g, f, k, at : at + 16] = piece

            @pl.when(h == 1)
            def _(piece=piece, t=t, g=g, f=f, k=k):
                send_ref[t, g, f, k, at : at + 16] = piece


def per_seq(width, rows=T):
    return pl.BlockSpec((1, rows, width), lambda b: (b, 0, 0))


def fixed(shape):
    return pl.BlockSpec(shape, lambda b: (0,) * len(shape))


def shape_of(shape, dtype=f32):
    return jax.ShapeDtypeStruct(shape, dtype)


def pieces_shape(rows):
    return (2, 2, 2, 4, rows, 256)


def call_attention(order, first, n_seqs, inputs):
    shapes = [(T, D, f32), (T, D, bf16), (T, 3 * D, bf16), (LSE, NP, f32), (T, D, bf16), (T, D, f32)]
    vec_spec, wa_spec = fixed((N_VEC, D)), fixed((D, 4 * D))
    if first:
        in_specs = [SMEM, per_seq(NP, CH), per_seq(D, TAIL), fixed((ROWS, D)), vec_spec, wa_spec]
    else:
        in_specs = [per_seq(D), per_seq(D), fixed((2, 2 * D, D // 2)), vec_spec, wa_spec]
    return order(
        embed_attention_kernel if first else skip_attention_kernel,
        inputs,
        in_specs,
        [shape_of((n_seqs, r, w), d) for r, w, d in shapes],
        [per_seq(w, r) for r, w, _ in shapes],
        grid=(n_seqs,),
        name="attention_forward_%d" % (0 if first else 1),
    )


def flat(width):
    return pl.BlockSpec((T, width), lambda b: (b, 0))


def call_mlp(order, layer_id, n_seqs, mid, vec, w1, w2):
    shapes = [(D, bf16), (FF, bf16), (FF, bf16), (D, f32)]
    whole = n_seqs * T
    out = order(
        functools.partial(mlp_kernel, layer_id),
        [mid.reshape(whole, D), vec, w1, w2],
        [flat(D), fixed((N_VEC, D)), fixed((D, FF)), fixed((2, FF, D // 2))],
        [shape_of((whole, w), d) for w, d in shapes],
        [flat(w) for w, _ in shapes],
        grid=(n_seqs,),
        name="mlp_forward_%d" % layer_id,
    )
    return [*out[:3], out[3].reshape(n_seqs, T, D)]


def mlp_backward_outs(n_seqs):
    whole = n_seqs * T
    pieces = pieces_shape(128)
    outs = [shape_of((whole, D)), shape_of(pieces, bf16), shape_of(pieces, bf16), shape_of((8, D)), shape_of((1, FF))]
    out_specs = [flat(D), fixed(pieces), fixed(pieces), fixed((8, D)), fixed((1, FF))]
    scratch = [
        pltpu.VMEM((whole, D), bf16),
        pltpu.VMEM((whole, D), bf16),
        pltpu.VMEM((whole, FF), bf16),
        pltpu.VMEM((whole, FF), bf16),
        pltpu.VMEM((D, FF), bf16),
    ]
    return outs, out_specs, scratch


def call_mlp_backward(order, layer_id, n_seqs, place, dout, act, slope, normed, mid, vec, w1, w2):
    whole = n_seqs * T
    outs, out_specs, scratch = mlp_backward_outs(n_seqs)
    out = order(
        functools.partial(mlp_backward_kernel, layer_id),
        (place, dout.reshape(whole, D), act, slope, normed, mid.reshape(whole, D), vec, w1, w2),
        [SMEM, flat(D), flat(FF), flat(FF), flat(D), flat(D)]
        + [fixed((N_VEC, D)), fixed((D, FF)), fixed((2, FF, D // 2))],
        outs,
        out_specs,
        scratch,
        grid=(n_seqs,),
        name="mlp_backward_%d" % layer_id,
    )
    return [out[0].reshape(n_seqs, T, D), *out[1:]]


def call_mlp_turn(order, n_seqs, total, weights, place, mid, vec, w1, w2, noise, tab):
    whole = n_seqs * T
    outs, out_specs, scratch = mlp_backward_outs(n_seqs)
    out = order(
        mlp_turn_kernel,
        (total, weights, place, mid.reshape(whole, D), vec, w1, w2, noise, tab),
        [SMEM, SMEM, SMEM, flat(D), fixed((N_VEC, D)), fixed((D, FF)), fixed((2, FF, D // 2))]
        + [per_seq(NP, CH), fixed((ROWS, D))],
        outs + [shape_of((CH, D)), shape_of((8, D))],
        out_specs + [fixed((CH, D)), fixed((8, D))],
        scratch + [pltpu.VMEM((T, FF), bf16)],
        grid=(n_seqs,),
        name="mlp_turn",
    )
    return [out[0].reshape(n_seqs, T, D), *out[1:]]


def call_attention_backward(order, layer_id, n_seqs, place, dmid, x, normed, qkv, lse, att, vec, wa, more):
    whole = n_seqs * T
    pieces = pieces_shape(80 if layer_id == 0 else 96)
    specs = [SMEM, per_seq(D), per_seq(D), per_seq(D), per_seq(3 * D), per_seq(NP, LSE), per_seq(D)]
    specs += [fixed((N_VEC, D)), fixed((D, 4 * D))]
    scratch = [
        pltpu.VMEM((whole, D), bf16),
        pltpu.VMEM((whole, D), bf16),
        pltpu.VMEM((whole, 3 * D), bf16),
        pltpu.VMEM((whole, D), bf16),
        pltpu.VMEM((T, 3 * D), bf16),
        pltpu.VMEM((D, 4 * D), bf16),
    ]
    if layer_id == 1:
        kernel = middle_backward_kernel
        specs += [per_seq(D), per_seq(D), fixed((2, 2 * D, D // 2))]
        outs = [shape_of((n_seqs, T, D)), shape_of((n_seqs, T, D)), shape_of((8, D))]
        out_specs = [per_seq(D), per_seq(D), fixed((8, D))]
        scratch += [pltpu.VMEM((whole, 2 * D), bf16), pltpu.VMEM((whole, D), bf16), pltpu.VMEM((2 * D, D), bf16)]
    else:
        kernel = last_backward_kernel
        specs += [SMEM, per_seq(D), per_seq(NP, CH), fixed((CH, D))] + [fixed((8, D))] * 4 + [fixed((1, FF))] * 2
        scratch += [pltpu.VMEM((8, D), f32), pltpu.VMEM((ROWS, D), f32)]
        outs, out_specs = [], []
    return order(
        functools.partial(kernel, layer_id),
        [place, dmid, x, normed, qkv, lse, att, vec, wa, *more],
        specs,
        [shape_of(pieces, bf16), shape_of(pieces, bf16)] + outs,
        [fixed(pieces), fixed(pieces)] + out_specs,
        scratch,
        grid=(n_seqs,),
        name="attention_backward_%d" % layer_id,
    )


def device_id(x, c, z, y):
    return (x * 2 + c) * 8 + z * 2 + y


def pairs(move):
    every = [(x, c, z, y) for x in range(2) for c in range(2) for z in range(4) for y in range(2)]
    return [(device_id(*at), device_id(*move(*at))) for at in every]


TO_CORE = pairs(lambda x, c, z, y: (x, 1 - c, z, y))
TO_X = pairs(lambda x, c, z, y: (1 - x, c, z, y))
TO_Y = pairs(lambda x, c, z, y: (x, c, z, 1 - y))
TO_Z = [pairs(lambda x, c, z, y, k=k: (x, c, (z + k) % 4, y)) for k in range(4)]
PIECE_ROWS = {"a": 64, "m": 128, "s": 32, "t": 16}


def send(value, to):
    return lax.ppermute(value, ALL, to)


def rows_in(kinds):
    return sum(PIECE_ROWS[kind[0]] for kind in kinds)


def pack_kernel(kinds, c_ref, mats_ref, down_ref, skip_ref, tab_ref, vec_ref, weight_ref, u_ref, wide_s, narrow_s, sem):
    x, c, _, _ = coords(c_ref)
    copies, casts = [], []
    wide = narrow = row = 0
    for kind in kinds:
        l = int(kind[1:] or 0)
        if kind[0] in "am":
            for t in range(2):
                start = (2048 if kind[0] == "m" else 0) + 256 * (4 * c + 2 * t + x)
                copies.append((mats_ref.at[l, :, pl.ds(pl.multiple_of(start, 256), 256)], wide_s.at[wide]))
                casts.append((t, row, wide_s.at[wide], None))
                wide += 1
            row += 64
        if kind[0] in "ms":
            size = 32 if kind[0] == "m" else 16
            ref = down_ref.at[l] if kind[0] == "m" else skip_ref
            for t in range(2):
                start = pl.multiple_of(size * (4 * c + 2 * t + x), size)
                copies.append((ref.at[pl.ds(start, size)], narrow_s.at[narrow, :size]))
                for half in range(2):
                    cols = slice(256 * half, 256 * half + 256)
                    casts.append((t, row + size * half, narrow_s.at[narrow, :size], cols))
                narrow += 1
            row += 2 * size
        if kind[0] == "t":
            own_weight = weight_ref[0]
            for i in range(1, weight_ref.shape[0]):
                own_weight += weight_ref[i]
            turned = vec_ref[...].T
            first, last = CH + CLASSES, CH + CLASSES + SEQ_LEN
            corner = (lax.broadcasted_iota(jnp.int32, (16, 256), 0) == 8) & (
                lax.broadcasted_iota(jnp.int32, (16, 256), 1) == 255
            )
            for t in range(2):
                j = 4 * c + 2 * t + x
                table = tab_ref[pl.ds(pl.multiple_of(8 * j, 8), 8)]
                vecs = turned[0:8]
                for i in range(1, 8):
                    vecs = jnp.where(j == i, turned[8 * i : 8 * i + 8], vecs)
                rest = [
                    table[:, first : first + 2],
                    jnp.zeros((8, TAIL - 2), f32),
                    table[:, :first],
                    table[:, last:],
                    vecs,
                    jnp.zeros((8, ROWS - ROW_VEC - N_VEC), f32),
                ]
                piece = jnp.concatenate([table[:, first + 2 : last], jnp.concatenate(rest, 1)], 0)
                if t == 0:
                    piece = jnp.where(corner, own_weight.astype(f32), piece)
                u_ref[t, row : row + 16] = piece.astype(bf16)
            row += 16
    copies = [pltpu.make_async_copy(a, b, sem) for a, b in copies]
    for copy in copies:
        copy.start()
    yield
    for copy in copies:
        copy.wait()
    for t, at, ref, cols in casts:
        value = ref[...] if cols is None else ref[:, cols]
        u_ref[t, at : at + value.shape[0]] = value.astype(bf16)


def join_ring_kernel(u0, u1, u2, u3, b_ref, c_ref):
    for k, ref in enumerate((u0, u1, u2, u3)):
        b_ref[k] = ref[0]
        c_ref[k] = ref[1]


def join_pair_kernel(b0, b1, c0, c1, b_ref, c_ref):
    for i, (b, c) in enumerate(((b0, c0), (b1, c1))):
        b_ref[i] = b[...]
        c_ref[i] = c[...]


def join_own_kernel(b, c, both_ref):
    both_ref[0] = b[...]
    both_ref[1] = c[...]


def assemble_kernel(kinds, c_ref, *refs):
    x, c, z, y = coords(c_ref)
    sources, dests = refs[:6], refs[6:]
    for h in range(2):
        if h == 0:
            own_b, x_b, own_c, y_c = sources[:4]
        else:
            own_b, own_c, x_b, y_c = (sources[4 + i].at[k] for i in range(2) for k in range(2))
        for t in range(2):
            for g in range(2):
                j = 4 * (c ^ h) + 2 * t + (g ^ x)
                cols = pl.ds(pl.multiple_of(256 * j, 256), 256)
                for f in range(2):
                    src = ((own_b, x_b)[g].at[f]) if t == 0 else ((own_c, y_c)[f].at[g])
                    for k in range(4):
                        s = 2 * ((z - k) & 3) + (y ^ f)
                        row = 0
                        at = 0
                        for kind in kinds:
                            if kind[0] in "am":
                                rows = pl.ds(pl.multiple_of(64 * s, 64), 64)
                                dests[at][rows, cols] = src[k, row : row + 64]
                                row, at = row + 64, at + 1
                            if kind[0] in "ms":
                                size = 32 if kind[0] == "m" else 16
                                rows = pl.ds(pl.multiple_of(size * (8 * s + j), size), size)
                                for half in range(2):
                                    dests[at][half, rows] = src[k, row : row + size]
                                    row += size
                                at += 1
                            if kind[0] == "t":
                                both = src[k, row : row + 16].astype(f32)
                                rows = pl.ds(pl.multiple_of(64 * s + 8 * j, 8), 8)
                                dests[-1][rows, :256] = both[:8]
                                dests[-1][rows, 256:] = both[8:]
    if "t" in kinds:
        table_ref, vec_ref, total_ref, turned_s = dests[-4:]
        table = turned_s[...].T
        table_ref[...] = table.astype(bf16)
        vec_ref[...] = table[ROW_VEC : ROW_VEC + N_VEC]
        total_ref[0, 0] = jnp.sum(table[ROW_WEIGHT : ROW_WEIGHT + 1])


def assemble_all_kernel(kinds, source, *dests):
    for x in range(2):
        for c in range(2):
            for s in range(8):
                for t in range(2):
                    j = 4 * c + 2 * t + x
                    src = source.at[8 * (2 * x + c) + s, t]
                    row = at = 0
                    for kind in kinds:
                        if kind[0] in "am":
                            dests[at][64 * s : 64 * s + 64, 256 * j : 256 * j + 256] = src[row : row + 64]
                            row, at = row + 64, at + 1
                        if kind[0] in "ms":
                            size = 32 if kind[0] == "m" else 16
                            for half in range(2):
                                start = size * (8 * s + j)
                                dests[at][half, start : start + size] = src[row : row + size]
                                row += size
                            at += 1


class Gather:
    def __init__(self, place, kinds, sources):
        self.place, self.kinds, self.sources = place, kinds, sources
        self.rows = rows_in(kinds)

    def pack(self):
        return Part(
            functools.partial(pack_kernel, self.kinds),
            (self.place, *self.sources),
            [SMEM, ANY, ANY, ANY] + ([WHOLE, WHOLE, SMEM] if "t" in self.kinds else [ANY] * 3),
            [shape_of((2, self.rows, 256), bf16)],
            [WHOLE],
            [pltpu.VMEM((4, 64, 256), f32), pltpu.VMEM((4, 32, D), f32), pltpu.SemaphoreType.DMA],
        )

    def packed_for_all(self, results):
        self.every = lax.all_gather(results[0], ALL)

    def assemble_all(self):
        shapes = self.shapes()
        return Part(
            functools.partial(assemble_all_kernel, self.kinds), [self.every], [WHOLE], shapes, [WHOLE] * len(shapes)
        )

    def packed(self, results):
        (own,) = results
        self.ring = [own] + [send(own, TO_Z[k]) for k in range(1, 4)]

    def join_ring(self):
        half = shape_of((4, self.rows, 256), bf16)
        return Part(join_ring_kernel, self.ring, [WHOLE] * 4, [half] * 2, [WHOLE] * 2)

    def ring_joined(self, results):
        b, c = results
        self.halves = (b, send(b, TO_Y), c, send(c, TO_X))

    def join_pair(self):
        whole = shape_of((2, 4, self.rows, 256), bf16)
        return Part(join_pair_kernel, self.halves, [WHOLE] * 4, [whole, whole], [WHOLE] * 2)

    def pair_joined(self, results):
        b, c = results
        self.mine = [b, send(b, TO_X), c, send(c, TO_Y)]

    def join_own(self):
        both = shape_of((2, 2, 4, self.rows, 256), bf16)
        return Part(join_own_kernel, (self.mine[0], self.mine[2]), [WHOLE] * 2, [both], [WHOLE])

    def own_joined(self, results):
        self.other = [send(results[0], TO_CORE)]

    def join_rest(self):
        both = shape_of((2, 2, 4, self.rows, 256), bf16)
        return Part(join_own_kernel, (self.mine[1], self.mine[3]), [WHOLE] * 2, [both], [WHOLE])

    def rest_joined(self, results):
        self.other.append(send(results[0], TO_CORE))

    def shapes(self):
        shapes = []
        for kind in self.kinds:
            if kind[0] in "am":
                shapes.append(shape_of((D, 2048), bf16))
            if kind[0] == "m":
                shapes.append(shape_of((2, FF, 256), bf16))
            if kind[0] == "s":
                shapes.append(shape_of((2, 2 * D, 256), bf16))
            if kind[0] == "t":
                shapes += [shape_of((ROWS, D), bf16), shape_of((N_VEC, D)), shape_of((1, 1))]
        return shapes

    def assemble(self):
        shapes = self.shapes()
        scratch = [pltpu.VMEM((D, ROWS), f32)] if "t" in self.kinds else []
        return Part(
            functools.partial(assemble_kernel, self.kinds),
            (self.place, *self.mine, *self.other),
            [SMEM] + [WHOLE] * 6,
            shapes,
            [SMEM if shape.shape == (1, 1) else WHOLE for shape in shapes],
            scratch,
        )


def added(*values):
    total = values[0].astype(f32)
    for value in values[1:]:
        total += value.astype(f32)
    return total.astype(bf16)


def add_core_kernel(n, *refs):
    keeps, gots, (b0_ref, b1_ref, c0_ref, c1_ref) = refs[:n], refs[n : 2 * n], refs[2 * n :]
    row = 0
    for keep, got in zip(keeps, gots):
        rows = slice(row, row + keep.shape[4])
        row = rows.stop
        for i in range(2):
            for dest, at in ((b0_ref, (0, 0, i)), (b1_ref, (0, 1, i)), (c0_ref, (1, i, 0)), (c1_ref, (1, i, 1))):
                dest[i, :, rows] = added(keep[at], got[at])


def add_both_kernel(b0_ref, gb_ref, c0_ref, gc_ref, b_ref, sb_ref, c_ref, sc_ref):
    for keep, got, dests in ((b0_ref, gb_ref, (b_ref, sb_ref)), (c0_ref, gc_ref, (c_ref, sc_ref))):
        for i, dest in enumerate(dests):
            dest[...] = added(keep[i], got[i])


def add_ring_kernel(b_ref, gb_ref, c_ref, gc_ref, *dests):
    for t, (keep, got) in enumerate(((b_ref, gb_ref), (c_ref, gc_ref))):
        for k, dest in enumerate(dests):
            dest[t] = added(keep[k], got[k])


def add_last_kernel(*refs):
    row = 0
    for i in range(0, len(refs) - 1, 4):
        rows = slice(row, row + refs[i].shape[1])
        row = rows.stop
        refs[-1][:, rows] = added(*(ref[...] for ref in refs[i : i + 4]))


class Reduce:
    def __init__(self, kinds):
        self.kinds = kinds
        self.rows = rows_in(kinds)
        self.keep, self.got = [], []

    def start(self, keep, give):
        self.keep.append(keep)
        self.got.append(send(give, TO_CORE))

    def core(self):
        def six(rows):
            return pl.BlockSpec((2, 2, 2, 1, rows, 256), lambda k: (0, 0, 0, k, 0, 0))

        four = pl.BlockSpec((2, 1, self.rows, 256), lambda k: (0, k, 0, 0))
        parts = self.keep + self.got
        return Part(
            functools.partial(add_core_kernel, len(self.keep)),
            parts,
            [six(part.shape[4]) for part in parts],
            [shape_of((2, 4, self.rows, 256), bf16)] * 4,
            [four] * 4,
        )

    def core_added(self, results):
        b0, b1, c0, c1 = results
        self.parts = (b0, send(b1, TO_X), c0, send(c1, TO_Y))

    def both(self):
        four = pl.BlockSpec((2, 1, self.rows, 256), lambda k: (0, k, 0, 0))
        three = pl.BlockSpec((1, self.rows, 256), lambda k: (k, 0, 0))
        return Part(
            add_both_kernel, self.parts, [four] * 4, [shape_of((4, self.rows, 256), bf16)] * 4, [three] * 4
        )

    def both_added(self, results):
        b, sb, c, sc = results
        self.parts = (b, send(sb, TO_Y), c, send(sc, TO_X))

    def ring(self):
        small = shape_of((2, self.rows, 256), bf16)
        return Part(add_ring_kernel, self.parts, [WHOLE] * 4, [small] * 4, [WHOLE] * 4)

    def ring_added(self, results):
        self.parts = [results[0]] + [send(results[k], TO_Z[k]) for k in range(1, 4)]


class Owned:
    def __init__(self, *chunks):
        self.chunks = chunks
        self.kinds = [kind for chunk in chunks for kind in chunk.kinds]

    def last(self):
        parts = [part for chunk in self.chunks for part in chunk.parts]
        out = shape_of((2, rows_in(self.kinds), 256), bf16)
        return Part(add_last_kernel, parts, [WHOLE] * len(parts), [out], [WHOLE])

    def last_added(self, results):
        (mine,) = results
        near = send(mine, TO_X)
        self.parts = (mine, near, send(mine, TO_CORE), send(near, TO_CORE))

    def adam(self, order, place, states, bufs, name):
        inputs, in_specs, outs, out_specs, aliases = [place, *self.parts], [SMEM] + [WHOLE] * 4, [], [], {}
        targets = []
        for kind in self.kinds:
            l = int(kind[1:] or 0)
            if kind[0] == "a":
                targets.append(("mats", "a", pl.BlockSpec((1, 64, 4096), lambda i, l=l: (l, 0, 0))))
            if kind[0] == "m":
                targets.append(("down", "d", pl.BlockSpec((1, 256, D), lambda i, l=l: (l, 0, 0))))
            if kind[0] == "s":
                targets.append(("skip", "s", fixed((128, D))))
            if kind[0] == "t":
                targets.append(("tables", "t", fixed((64, SEQ_LEN + 3 * CH))))
                targets.append(("vectors", "v", fixed((N_VEC, 64))))
        held = []
        for name, _, spec in targets:
            inputs += list(states[name])
            in_specs += [spec] * 3
            weight = states[name][0]
            if bufs.get(name) is not None:
                held += [(len(outs) + i, buf) for i, buf in enumerate(bufs[name])]
            outs += [shape_of(weight.shape)] * 3 + [shape_of(weight.shape, bf16)]
            out_specs += [spec] * 4
        n_read = len(inputs)
        for at, buf in held:
            aliases[len(inputs)] = at
            inputs.append(buf)
            in_specs.append(ANY)
        scratch = []
        if any(t[1] == "d" for t in targets):
            scratch.append(pltpu.VMEM((D, 256), f32))
        if any(t[1] == "t" for t in targets):
            scratch.append(pltpu.VMEM((64, ROWS), f32))
            outs.append(shape_of((1, 1)))
            out_specs.append(SMEM)
        result = order(
            functools.partial(adam_kernel, self.kinds, [t[1] for t in targets], n_read, len(inputs)),
            inputs,
            in_specs,
            outs,
            out_specs,
            scratch,
            name=name,
            aliases=aliases,
        )
        for i, (name, _, _) in enumerate(targets):
            bufs[name] = result[4 * i : 4 * i + 4]
        return result[4 * len(targets) :]


def adam_kernel(kinds, targets, n_read, n_in, c_ref, *refs):
    x, c, _, _ = coords(c_ref)
    parts, ins, outs = refs[:4], refs[4 : n_read - 1], refs[n_in - 1 :]
    scratch = list(outs[4 * len(targets) :])
    loss_ref = scratch.pop(0) if "t" in targets else None
    offsets, row = {}, 0
    for kind in kinds:
        offsets[kind[0]] = row
        row += PIECE_ROWS[kind[0]]
    pieces = []
    for h in range(2):
        for g in range(2):
            for t in range(2):
                pieces.append((4 * (c ^ h) + 2 * t + (g ^ x), parts[2 * h + g].at[t]))
    for i, kind in enumerate(targets):
        state, dests = ins[3 * i : 3 * i + 3], outs[4 * i : 4 * i + 4]
        row = offsets[{"d": "m", "v": "t"}.get(kind, kind)]

        def update(at, grad, rate, state=state, dests=dests):
            weight, first, second = (ref[at] for ref in state)
            values = adam_update(weight, grad, first, second, rate)
            for dest, value in zip(dests, values):
                dest[at] = value

        if kind == "a":
            for at_row, start in ((row, 0), (offsets["m"], 2048)):
                for j, piece in pieces:
                    at = (0, slice(None), pl.ds(pl.multiple_of(start + 256 * j, 256), 256))
                    update(at, piece[at_row : at_row + 64], step_rates[0])
        if kind == "d":
            held = scratch[0]
            for j, piece in pieces:
                held[pl.ds(pl.multiple_of(64 * j, 64), 64)] = piece[row + 64 : row + 128].astype(f32)
            update((0,), held[...].T, step_rates[1])
        if kind == "s":
            for j, piece in pieces:
                for half in range(2):
                    at = (pl.ds(pl.multiple_of(16 * j, 16), 16), slice(256 * half, 256 * half + 256))
                    update(at, piece[row + 16 * half : row + 16 * half + 16], step_rates[2])
        if kind == "t":
            held = scratch[-1]
            for j, piece in pieces:
                both = piece[row : row + 16].astype(f32)
                rows = pl.ds(pl.multiple_of(8 * j, 8), 8)
                held[rows, :256] = both[:8]
                held[rows, 256:] = both[8:]
            grad = held[...]
            parts_of = [grad[:, ROW_PATCH:ROW_HEAD], grad[:, NP : NP + 2], grad[:, :NP], grad[:, ROW_HEAD:ROW_VEC]]
            update(slice(None), jnp.concatenate(parts_of, 1), step_rates[3])
            loss_ref[0, 0] = jnp.sum(grad[0:3, ROW_LOSS : ROW_LOSS + 32])
        if kind == "v":
            grad = scratch[-1][:, ROW_VEC : ROW_VEC + N_VEC].T
            update(slice(None), grad, step_rates[4])


def gather_any(mats, down, skip, tables, vectors):
    first, last = CH + CLASSES, CH + CLASSES + SEQ_LEN
    width = tables.shape[1]
    tab = jnp.concatenate(
        [
            tables[first + 2 : last],
            tables[first : first + 2],
            jnp.zeros((TAIL - 2, width), f32),
            tables[:first],
            tables[last:],
            vectors,
            jnp.zeros((ROWS - ROW_VEC - N_VEC, width), f32),
        ]
    )
    every = lax.all_gather(mats.astype(bf16), "shard", axis=1, tiled=True)
    downs = lax.all_gather(down.astype(bf16), "shard", axis=1, tiled=True)
    skips = lax.all_gather(skip.astype(bf16), "shard", axis=0, tiled=True)
    table = lax.all_gather(tab.astype(bf16), "shard", axis=1, tiled=True)

    def halves(m):
        return jnp.stack([m[:, : D // 2], m[:, D // 2 :]])

    mats_of = [(every[l, :, :2048], every[l, :, 2048:]) for l in range(LAYERS)]
    return (mats_of, [halves(downs[l]) for l in range(LAYERS)], halves(skips), table)


def reduce_any(grads):
    def ordered(kind):
        both = jnp.stack(grads[kind])
        return both.transpose(0, 1, 2, 4, 3, 5, 6).reshape((8, 8) + both.shape[5:])

    def shard_sum(value, axis):
        owned = lax.psum_scatter(value.astype(f32), "shard", scatter_dimension=axis, tiled=True)
        return lax.psum(owned.astype(bf16), "rep")

    mats, down = [], []
    for l in range(LAYERS):
        attn, mlp = ordered("a%d" % l), ordered("m%d" % l)
        both = [part[:, :, :64].transpose(1, 2, 0, 3).reshape(D, 2048) for part in (attn, mlp)]
        mats.append(jnp.concatenate(both, 1))
        down.append(mlp[:, :, 64:].transpose(0, 2, 1, 3).reshape(D, FF).T)
    skip = ordered("a1")[:, :, 64:].reshape(8, 8, 2, 16, 256).transpose(1, 0, 3, 2, 4).reshape(2 * D, D)
    turned = ordered("a0")[:, :, 64:].reshape(8, 8, 2, 8, 256).transpose(1, 0, 3, 2, 4).reshape(D, ROWS)
    return (shard_sum(jnp.stack(mats), 1), shard_sum(jnp.stack(down), 1), shard_sum(skip, 0), shard_sum(turned, 0))


def time_token(timesteps):
    half_width = D // 2
    freqs_row = jnp.exp(-math.log(10000.0) * jnp.arange(half_width, dtype=f32) / half_width)
    angles = timesteps.astype(f32)[:, None] * freqs_row[None, :]
    return jnp.concatenate([jnp.cos(angles), jnp.sin(angles)], -1)


def adam_update(weight, grad, moment_one, moment_two, step_rate):
    grad = grad.astype(f32)
    moment_one = beta_one * moment_one + (1.0 - beta_one) * grad
    moment_two = beta_two * moment_two + (1.0 - beta_two) * grad * grad
    first_hat = moment_one / (1.0 - beta_one**STEP)
    second_hat = moment_two / (1.0 - beta_two**STEP)
    weight = weight - step_rate * (first_hat / (jnp.sqrt(second_hat) + epsilon) + weight_decay * weight)
    return (moment_one, moment_two, weight, weight.astype(bf16))


def local(
    fast,
    latents,
    target_noise,
    labels,
    timesteps,
    loss_weight,
    layer_mats,
    layer_mats_first,
    layer_mats_second,
    down_mats,
    down_first,
    down_second,
    skip_mat,
    skip_first,
    skip_second,
    tables,
    tables_first,
    tables_second,
    vectors,
    vectors_first,
    vectors_second,
):
    n_seqs = latents.shape[0]
    if fast:
        rep, shard = lax.axis_index("rep"), lax.axis_index("shard")
        place = jnp.stack([rep // 2, rep % 2, shard // 2, shard % 2]).astype(jnp.int32)
    else:
        place = jnp.zeros((4,), jnp.int32)
    order = Order()
    time_rows = jnp.pad(time_token(timesteps)[:, None], ((0, 0), (0, TAIL - 1), (0, 0)))
    mats, downs = [None, None], [None, None]
    forward = {}

    def attention(l):
        if l == 0:
            inputs = (labels, latents, time_rows, table, vec, mats[0][0])
        else:
            inputs = (forward["x1"], forward["x0"], ws, vec, mats[1][0])
        forward["a%d" % l] = call_attention(order, l == 0, n_seqs, inputs)
        if l == 0:
            forward["x0"] = forward["a0"][0]

    def mlp():
        out = call_mlp(order, 0, n_seqs, forward["a0"][5], vec, mats[0][1], downs[0])
        forward["m0"] = out
        forward["x1"] = out[3]

    if fast:
        args = (layer_mats, down_mats, skip_mat, tables.T, vectors, loss_weight)
        one, two, three = (Gather(place, kinds, args) for kinds in GATHER_CHUNKS)
        one.packed(*order.fuse([one.pack()], "pack_0"))
        joined, packed = order.fuse([one.join_ring(), two.pack()], "join_ring_0")
        one.ring_joined(joined)
        two.packed(packed)
        one.pair_joined(*order.fuse([one.join_pair()], "join_pair_0"))
        joined, own = order.fuse([two.join_ring(), one.join_own()], "join_ring_1")
        two.ring_joined(joined)
        one.own_joined(own)
        one.rest_joined(*order.fuse([one.join_rest()], "join_rest_0"))
        (wa0, table, vec, weight_total), packed = order.fuse([one.assemble(), three.pack()], "assemble_0")
        mats[0] = (wa0, None)
        three.packed(packed)
        two.pair_joined(*order.fuse([two.join_pair()], "join_pair_1"))
        attention(0)
        joined, own = order.fuse([three.join_ring(), two.join_own()], "join_ring_2")
        three.ring_joined(joined)
        two.own_joined(own)
        two.rest_joined(*order.fuse([two.join_rest()], "join_rest_1"))
        ((w10, downs[0], ws),) = order.fuse([two.assemble()], "assemble_1")
        mats[0] = (wa0, w10)
        three.pair_joined(*order.fuse([three.join_pair()], "join_pair_2"))
        mlp()
        three.own_joined(*order.fuse([three.join_own()], "join_own_2"))
        three.rest_joined(*order.fuse([three.join_rest()], "join_rest_2"))
        ((wa1, w11, downs[1]),) = order.fuse([three.assemble()], "assemble_2")
        mats[1] = (wa1, w11)
        attention(1)
    else:
        mats, downs, ws, table = gather_any(layer_mats, down_mats, skip_mat, tables, vectors)
        vec = table[ROW_VEC : ROW_VEC + N_VEC].astype(f32)
        weight_total = lax.psum(jnp.sum(loss_weight.astype(f32)), ALL).reshape(1, 1)
        attention(0)
        mlp()
        attention(1)

    grads, small = {}, {}

    def mlp_turn():
        mid = forward["a1"][5]
        out = call_mlp_turn(
            order, n_seqs, weight_total, loss_weight, place, mid, vec, mats[1][1], downs[1], target_noise, table
        )
        grads["m1"], small["m1"], small["f1"] = out[1:3], out[3], out[4]
        return out[0], out[5], out[6]

    def mlp_back(dout):
        normed, act, slope = forward["m0"][:3]
        out = call_mlp_backward(
            order, 0, n_seqs, place, dout, act, slope, normed, forward["a0"][5], vec, mats[0][1], downs[0]
        )
        grads["m0"], small["m0"], small["f0"] = out[1:3], out[3], out[4]
        return out[0]

    def attention_back(l, dmid, more):
        x, normed, qkv, lse, att, _ = forward["a%d" % l]
        out = call_attention_backward(order, l, n_seqs, place, dmid, x, normed, qkv, lse, att, vec, mats[l][0], more)
        grads["a%d" % l] = out[:2]
        return out[2:]

    bufs = {}
    if fast:
        first, second, third = (Reduce(kinds) for kinds in REDUCE_CHUNKS)
        states = {
            "mats": (layer_mats, layer_mats_first, layer_mats_second),
            "down": (down_mats, down_first, down_second),
            "skip": (skip_mat, skip_first, skip_second),
            "tables": (tables.T, tables_first.T, tables_second.T),
            "vectors": (vectors, vectors_first, vectors_second),
        }
    dmid, dhead, small_head = mlp_turn()
    if fast:
        first.start(*grads["m1"])
    dx, d0, small["a1"] = attention_back(1, dmid, (forward["x1"], forward["x0"], ws))
    if fast:
        first.start(*grads["a1"])
        first.core_added(*order.fuse([first.core()], "add_core_1", grid=(4,)))
    dmid = mlp_back(dx)
    if fast:
        second.start(*grads["m0"])
        first.both_added(*order.fuse([first.both()], "add_both_1", grid=(4,)))
        second.core_added(*order.fuse([second.core()], "add_core_2", grid=(4,)))
    last = (labels, d0, latents, dhead, small["m0"], small["m1"], small["a1"], small_head, small["f0"], small["f1"])
    attention_back(0, dmid, last)
    if fast:
        upper, lower = Owned(first), Owned(second, third)
        third.start(*grads["a0"])
        first.ring_added(*order.fuse([first.ring()], "add_ring_1"))
        second.both_added(*order.fuse([second.both()], "add_both_2", grid=(4,)))
        third.core_added(*order.fuse([third.core()], "add_core_3", grid=(4,)))
        second.ring_added(*order.fuse([second.ring()], "add_ring_2"))
        upper.last_added(*order.fuse([upper.last()], "add_last_1"))
        third.both_added(*order.fuse([third.both()], "add_both_3", grid=(4,)))
        third.ring_added(*order.fuse([third.ring()], "add_ring_3"))
        upper.adam(order, place, states, bufs, "adam_1")
        lower.last_added(*order.fuse([lower.last()], "add_last_0"))
        (loss,) = lower.adam(order, place, states, bufs, "adam_0")
        loss_sum = loss[0, 0]
        results = [bufs[name] for name in ("mats", "down", "skip", "tables", "vectors")]
        results[3] = [part.T for part in results[3]]
    else:
        loss_sum = lax.psum(small_head[2, 0], ALL)
        g_mats, g_down, g_skip, g_turned = reduce_any(grads)
        g_rows = g_turned.T
        g_tables = jnp.concatenate(
            [g_rows[ROW_PATCH:ROW_HEAD], g_rows[NP : NP + 2], g_rows[:NP], g_rows[ROW_HEAD:ROW_VEC]]
        )
        g_vectors = g_rows[ROW_VEC : ROW_VEC + N_VEC]
        results = [
            adam_update(layer_mats, g_mats, layer_mats_first, layer_mats_second, step_rates[0]),
            adam_update(down_mats, g_down, down_first, down_second, step_rates[1]),
            adam_update(skip_mat, g_skip, skip_first, skip_second, step_rates[2]),
            adam_update(tables, g_tables, tables_first, tables_second, step_rates[3]),
            adam_update(vectors, g_vectors, vectors_first, vectors_second, step_rates[4]),
        ]
    return (loss_sum, weight_total[0, 0], *(part for result in results for part in result))


GATHER_CHUNKS = (("a0", "t"), ("m0", "s"), ("a1", "m1"))
REDUCE_CHUNKS = (("m1", "a1", "s"), ("m0",), ("a0", "t"))


def solution(mesh):
    one, two, rows = P(None, "shard", None), P("shard", None), P(None, "shard")
    every = P(ALL, None, None)
    placed = (every, every, P(ALL), P(ALL), P(ALL), *[one] * 6, *[two] * 3, *[rows] * 6)
    fast = mesh.shape["rep"] == 4 and mesh.shape["shard"] == 8
    return jax.shard_map(
        functools.partial(local, fast),
        mesh=mesh,
        in_specs=placed,
        out_specs=(P(), P(), *[one] * 8, *[two] * 4, *[rows] * 8),
        check_vma=False,
    )
```

```python
import functools
import math

import jax
import jax.numpy as jnp
from jax import lax
from jax.experimental import pallas as pl
from jax.experimental.pallas import tpu as pltpu
from jax.sharding import PartitionSpec as P

D = 512
HEADS = 8
HD = 64
FF = 2048
CH = 16
NP = 256
CLASSES = 16
LAYERS = 2
STEP = 10
SEQ_LEN = 258

beta_one = 0.5
beta_two = 0.75
epsilon = 1e-08
weight_decay = 0.05
step_rates = (0.05, 0.03, 0.03, 0.05, 0.3)

TAIL = 16
T = NP + TAIL
ROW_PATCH = T
ROW_CLASS = ROW_PATCH + CH
ROW_HEAD = ROW_CLASS + CLASSES
ROW_VEC = ROW_HEAD + CH
N_VEC = LAYERS * (6 + FF // D) + 4
ROWS = D
ROW_WEIGHT = ROWS - 1
ROW_LOSS = 384
bf16 = jnp.bfloat16
f32 = jnp.float32
ALL = ("rep", "shard")
MIB = 1024 * 1024
MARGIN = 10 * MIB
WIDE = ("pack_0",)
ANY = pl.BlockSpec(memory_space=pl.ANY)
SMEM = pl.BlockSpec(memory_space=pltpu.SMEM)
WHOLE = pl.BlockSpec(memory_space=pltpu.VMEM)


def room(shape, dtype):
    size = jnp.dtype(dtype).itemsize
    rows, columns = ((1,) + tuple(shape))[-2:]
    rows, columns = -(-rows * size // 32) * 32 // size, -(-columns // 128) * 128
    return math.prod(shape[:-2]) * rows * columns * size


class Part:
    def __init__(self, body, inputs, in_specs, outs, out_specs, scratch=()):
        self.body, self.inputs, self.in_specs = body, list(inputs), list(in_specs)
        self.outs, self.out_specs, self.scratch = list(outs), list(out_specs), list(scratch)


class Order:
    def __init__(self):
        self.last = None

    def __call__(self, kernel, inputs, in_specs, outs, out_specs, scratch=(), grid=(1,), name=None, aliases=None):
        part = Part(kernel, inputs, in_specs, outs, out_specs, scratch)
        return self.fuse([part], name, grid=grid, aliases=aliases)[0]

    def fuse(self, parts, name, after=(), grid=(1,), aliases=None):
        extra = list(after) + ([] if self.last is None else [self.last])
        inputs = [value for part in parts for value in part.inputs]
        counts = [(len(p.inputs), len(p.outs), len(p.scratch)) for p in parts]
        ends = [sum(c[i] for c in counts) for i in range(3)]
        skip = len(extra)

        def body(*refs):
            groups = (refs[: ends[0]], refs[ends[0] + skip : ends[0] + skip + ends[1]], refs[ends[0] + skip + ends[1] :])
            at = [0, 0, 0]
            rest = []
            for part, count in zip(parts, counts):
                own = [r for i in range(3) for r in groups[i][at[i] : at[i] + count[i]]]
                at = [i + n for i, n in zip(at, count)]
                more = part.body(*own)
                if more is not None:
                    next(more)
                    rest.append(more)
            for more in rest:
                next(more, None)

        need = 0
        for part in parts:
            for spec, value in (*zip(part.in_specs, part.inputs), *zip(part.out_specs, part.outs)):
                if spec is not ANY and spec is not SMEM:
                    need += 2 * room(spec.block_shape or value.shape, value.dtype)
            need += sum(room(item.shape, item.dtype) for item in part.scratch if hasattr(item, "inner_aval") or hasattr(item, "shape"))
        result = pl.pallas_call(
            body,
            grid=grid,
            in_specs=[spec for part in parts for spec in part.in_specs] + [ANY] * skip,
            out_specs=[spec for part in parts for spec in part.out_specs],
            out_shape=[out for part in parts for out in part.outs],
            scratch_shapes=[item for part in parts for item in part.scratch],
            input_output_aliases=aliases or {},
            cost_estimate=pl.CostEstimate(flops=50_000_000_000, bytes_accessed=100_000_000, transcendentals=0),
            compiler_params=pltpu.CompilerParams(vmem_limit_bytes=56 * MIB if name in WIDE else min(need + MARGIN, 56 * MIB)),
            name=name,
        )(*inputs, *extra)
        self.last = result[0]
        split, at = [], 0
        for part in parts:
            split.append(result[at : at + len(part.outs)])
            at += len(part.outs)
        return split


def dot(left, right):
    return jnp.dot(left, right, preferred_element_type=f32)


def dot_t(left, right):
    return lax.dot_general(left, right, (((1,), (1,)), ((), ())), preferred_element_type=f32)


def t_dot(left, right):
    return lax.dot_general(left, right, (((0,), (0,)), ((), ())), preferred_element_type=f32)


def norm_hat(stream):
    center = jnp.mean(stream, -1, keepdims=True)
    offset = stream - center
    spread = jnp.mean(offset * offset, -1, keepdims=True)
    inverse = lax.rsqrt(spread + 1e-05)
    return (offset * inverse, inverse)


def norm_back(hat, inverse, gain, grad):
    scaled = grad * gain
    first = jnp.mean(scaled, -1, keepdims=True)
    second = jnp.mean(scaled * hat, -1, keepdims=True)
    return inverse * (scaled - first - hat * second)


def rows_sum(values):
    return jnp.sum(values, 0, keepdims=True)


LSE = 16


def apart(rows, scale):
    lane = lax.broadcasted_iota(jnp.int32, (1, 2 * HD), 1)
    return jnp.concatenate([rows * jnp.where(lane // HD == e, scale, 0.0).astype(bf16) for e in range(2)], 0)


def block_mask():
    row = lax.broadcasted_iota(jnp.int32, (TAIL, D), 0)
    lane = lax.broadcasted_iota(jnp.int32, (TAIL, D), 1)
    return (row // 2 == lane // HD, row % 2 == 0)


def spread_tail(rows, scale):
    own, first = block_mask()
    wide = rows.astype(f32)
    both = jnp.where(first, wide[0:1], wide[1:2]) * scale
    return jnp.where(own, both, 0.0).astype(bf16)


def gather_tail(values):
    own, first = block_mask()
    kept = jnp.where(own, values, 0.0)
    zero = rows_sum(jnp.where(first, kept, 0.0))
    one = rows_sum(jnp.where(first, 0.0, kept))
    row = lax.broadcasted_iota(jnp.int32, (TAIL, D), 0)
    return jnp.where(row == 0, zero, jnp.where(row == 1, one, 0.0))


def mask_keys(scores):
    tail = scores[NP:]
    row = lax.broadcasted_iota(jnp.int32, tail.shape, 0)
    return jnp.concatenate([scores[:NP], jnp.where(row < SEQ_LEN - NP, tail, -1e30)], 0)


def softmax_rows(scores):
    top = jnp.max(scores, 0, keepdims=True)
    expon = jnp.exp(scores - top)
    total = jnp.sum(expon, 0, keepdims=True)
    return (expon * (1.0 / total)).astype(bf16), top + jnp.log(total)


def pipelined(count, *stages):
    held = {}
    for step in range(count + len(stages) - 1):
        for i, stage in enumerate(stages):
            if 0 <= step - i < count:
                held[step - i] = stage(step - i, held.get(step - i))


def attention_forward(stream, layer_id, vec_ref, wa_ref, h_ref, qkv_ref, lse_ref, o_ref, mid_ref):
    base = layer_id * (6 + FF // D)
    hat, _ = norm_hat(stream)
    normed = (hat * vec_ref[base : base + 1] + vec_ref[base + 1 : base + 2]).astype(bf16)
    h_ref[0] = normed
    qkv_ref[0] = dot(normed, wa_ref[:, : 3 * D]).astype(bf16)
    scale = HD**-0.5

    def cut(part, pair):
        return qkv_ref[0, :, part * D + 128 * pair : part * D + 128 * pair + 128]

    def score(pair, _):
        return dot_t(cut(1, pair), apart(cut(0, pair)[:NP], scale))

    def weigh(pair, scores):
        weights, log_total = softmax_rows(mask_keys(scores))
        lse_ref[0, 2 * pair : 2 * pair + 1] = log_total[:, :NP]
        lse_ref[0, 2 * pair + 1 : 2 * pair + 2] = log_total[:, NP:]
        return weights

    def mix(pair, weights):
        values = apart(cut(2, pair), 1.0)
        out = t_dot(weights[:, :NP], values[:T]) + t_dot(weights[:, NP:], values[T:])
        o_ref[0, :NP, 128 * pair : 128 * pair + 128] = out.astype(bf16)

    tails = spread_tail(qkv_ref[0, NP:, :D], scale)
    weights, log_total = softmax_rows(mask_keys(dot_t(qkv_ref[0, :, D : 2 * D], tails)))
    lse_ref[0, HEADS : HEADS + 1, :TAIL] = log_total
    o_ref[0, NP:] = gather_tail(t_dot(weights, qkv_ref[0, :, 2 * D :])).astype(bf16)
    pipelined(HEADS // 2, score, weigh, mix)
    mid_ref[0] = stream + dot(o_ref[0], wa_ref[:, 3 * D :]) + vec_ref[base + 4 : base + 5]


def embed_attention_kernel(
    label_ref, latent_ref, time_ref, tab_ref, vec_ref, wa_ref, x_ref, h_ref, qkv_ref, lse_ref, o_ref, mid_ref
):
    b = pl.program_id(0)
    patch_rows = t_dot(latent_ref[0], tab_ref[ROW_PATCH:ROW_CLASS]) + vec_ref[N_VEC - 1 : N_VEC]
    row = lax.broadcasted_iota(jnp.int32, (TAIL, CLASSES), 0)
    column = lax.broadcasted_iota(jnp.int32, (TAIL, CLASSES), 1)
    choose = jnp.where((row == 1) & (column == label_ref[b]), 1.0, 0.0).astype(bf16)
    tail_rows = time_ref[0] + dot(choose, tab_ref[ROW_CLASS:ROW_HEAD])
    stream = jnp.concatenate([patch_rows, tail_rows], 0) + tab_ref[:T].astype(f32)
    x_ref[0] = stream
    attention_forward(stream, 0, vec_ref, wa_ref, h_ref, qkv_ref, lse_ref, o_ref, mid_ref)


def skip_attention_kernel(x1_ref, x0_ref, ws_ref, vec_ref, wa_ref, x_ref, h_ref, qkv_ref, lse_ref, o_ref, mid_ref):
    one = x1_ref[0].astype(bf16)
    zero = x0_ref[0].astype(bf16)
    halves = [dot(one, ws_ref[i, :D]) + dot(zero, ws_ref[i, D:]) for i in range(2)]
    stream = jnp.concatenate(halves, 1) + vec_ref[N_VEC - 2 : N_VEC - 1]
    x_ref[0] = stream
    attention_forward(stream, 1, vec_ref, wa_ref, h_ref, qkv_ref, lse_ref, o_ref, mid_ref)


def mlp_forward(layer_id, mid_ref, vec_ref, w1_ref, w2_ref, h_ref, act_ref, slope_ref):
    base = layer_id * (6 + FF // D)
    hat, _ = norm_hat(mid_ref[...])
    normed = (hat * vec_ref[base + 2 : base + 3] + vec_ref[base + 3 : base + 4]).astype(bf16)
    h_ref[...] = normed
    const = math.sqrt(2.0 / math.pi)

    for j in range(FF // D):
        cols = slice(D * j, D * j + D)
        pre = dot(normed, w1_ref[:, cols]) + vec_ref[base + 6 + j : base + 7 + j]
        square = pre * pre
        half = 0.5 + 0.5 * jnp.tanh(pre * (const + (const * 0.044715) * square))
        act = pre * half
        act_ref[:, cols] = act.astype(bf16)
        slope = half + act * (1.0 - half) * (2.0 * const + (6.0 * const * 0.044715) * square)
        slope_ref[:, cols] = slope.astype(bf16)
    total = jnp.concatenate([dot(act_ref[...], w2_ref[i]) for i in range(2)], 1)
    return mid_ref[...] + total + vec_ref[base + 5 : base + 6]


def mlp_kernel(layer_id, mid_ref, vec_ref, w1_ref, w2_ref, h_ref, act_ref, slope_ref, out_ref):
    out_ref[...] = mlp_forward(layer_id, mid_ref, vec_ref, w1_ref, w2_ref, h_ref, act_ref, slope_ref)


def head_backward(b, total_ref, weight_ref, out, noise_ref, tab_ref, vec_ref, dhead_ref, small_ref):
    hat, inverse = norm_hat(out[:NP])
    gain = vec_ref[N_VEC - 4 : N_VEC - 3]
    final = (hat * gain + vec_ref[N_VEC - 3 : N_VEC - 2]).astype(bf16)
    head = tab_ref[ROW_HEAD:ROW_VEC]
    errors = dot_t(head, final) - noise_ref[0].astype(f32)
    per_seq = jnp.sum(errors * errors) * (1.0 / (CH * NP))
    weight = weight_ref[b].astype(f32)
    scale = (jnp.ones((1, 1), f32) / total_ref[0, 0]) * weight * (2.0 / (CH * NP))
    grad_pred = (scale * errors).astype(bf16)
    dhead_ref[...] += dot(grad_pred, final)
    grad = t_dot(grad_pred, head)
    small_ref[0:1] += rows_sum(grad * hat)
    small_ref[1:2] += rows_sum(grad)
    small_ref[2:3] += jnp.full((1, D), weight * per_seq, f32)
    return jnp.concatenate([norm_back(hat, inverse, gain, grad), jnp.zeros((TAIL, D), f32)], 0)


def rows_of(b):
    return pl.ds(pl.multiple_of(T * b, TAIL), T)


def coords(c_ref):
    return tuple(c_ref[i] for i in range(4))


def place_of(c_ref, shard):
    _, _, z, y = coords(c_ref)
    return ((shard % 2) ^ y, (shard // 2 - z) & 3)


def sub_of(c_ref, h, t, g):
    x, c, _, _ = coords(c_ref)
    return 4 * (c ^ h) + 2 * t + (g ^ x)


def scatter_pieces(c_ref, keep_ref, send_ref, at, piece):
    for h, dest in ((0, keep_ref), (1, send_ref)):
        for t in range(2):
            for g in range(2):
                j = sub_of(c_ref, h, t, g)
                for s in range(8):
                    f, k = place_of(c_ref, s)
                    value = piece(j, s)
                    dest[t, g, f, k, at : at + value.shape[0]] = value


def by_columns(ref):
    return lambda j, s: ref[64 * s : 64 * s + 64, pl.ds(pl.multiple_of(256 * j, 256), 256)]


def by_rows(ref):
    return lambda j, s: ref[pl.ds(pl.multiple_of(64 * j, 64), 64), 256 * s : 256 * s + 256]


def mlp_backward(
    layer_id, rows, dout, slope_ref, mid_ref, vec_ref, w1_ref, w2_ref, dmid_ref, small_ref, dfc1b_ref, right_s, grads_s
):
    base = layer_id * (6 + FF // D)
    low = dout.astype(bf16)
    right_s[rows] = low

    def enter(j, _):
        block = slice(D * j, D * j + D)
        return dot_t(low[:, :256], w2_ref[0, block]) + dot_t(low[:, 256:], w2_ref[1, block])

    def bend(j, grad_act):
        cols = slice(D * j, D * j + D)
        grad_pre = grad_act * slope_ref[:, cols].astype(f32)
        dfc1b_ref[:, cols] += rows_sum(grad_pre)
        grad = grad_pre.astype(bf16)
        grads_s[rows, cols] = grad
        return grad

    total = []

    def leave(j, grad):
        part = dot_t(grad, w1_ref[:, D * j : D * j + D])
        total.append(part if not total else total[-1] + part)

    pipelined(FF // D, enter, bend, leave)
    grad_normed = total[-1]
    hat, inverse = norm_hat(mid_ref[...])
    small_ref[0:1] += rows_sum(grad_normed * hat)
    small_ref[1:2] += rows_sum(grad_normed)
    small_ref[2:3] += rows_sum(dout)
    dmid_ref[...] = dout + norm_back(hat, inverse, vec_ref[base + 2 : base + 3], grad_normed)


def mlp_weights(c_ref, keep_ref, send_ref, left_s, right_s, grads_s, acts_s, tile_s):
    tile_s[...] = t_dot(left_s[...], grads_s[...]).astype(bf16)
    scatter_pieces(c_ref, keep_ref, send_ref, 0, by_columns(tile_s))
    tile_s[...] = t_dot(right_s[...], acts_s[...]).astype(bf16)
    scatter_pieces(c_ref, keep_ref, send_ref, 64, by_rows(tile_s))


def mlp_backward_kernel(
    layer_id,
    c_ref,
    dout_ref,
    act_ref,
    slope_ref,
    h_ref,
    mid_ref,
    vec_ref,
    w1_ref,
    w2_ref,
    dmid_ref,
    keep_ref,
    send_ref,
    small_ref,
    dfc1b_ref,
    left_s,
    right_s,
    grads_s,
    acts_s,
    tile_s,
):
    b = pl.program_id(0)

    @pl.when(b == 0)
    def _():
        small_ref[...] = jnp.zeros_like(small_ref)
        dfc1b_ref[...] = jnp.zeros_like(dfc1b_ref)

    rows = rows_of(b)
    left_s[rows] = h_ref[...]
    acts_s[rows] = act_ref[...]
    weights = (mid_ref, vec_ref, w1_ref, w2_ref)
    mlp_backward(layer_id, rows, dout_ref[...], slope_ref, *weights, dmid_ref, small_ref, dfc1b_ref, right_s, grads_s)

    @pl.when(b == pl.num_programs(0) - 1)
    def _():
        mlp_weights(c_ref, keep_ref, send_ref, left_s, right_s, grads_s, acts_s, tile_s)


def mlp_turn_kernel(
    total_ref,
    weight_ref,
    c_ref,
    mid_ref,
    vec_ref,
    w1_ref,
    w2_ref,
    noise_ref,
    tab_ref,
    dmid_ref,
    keep_ref,
    send_ref,
    small_ref,
    dfc1b_ref,
    dhead_ref,
    small_head_ref,
    left_s,
    right_s,
    grads_s,
    acts_s,
    tile_s,
    slope_s,
):
    b = pl.program_id(0)

    @pl.when(b == 0)
    def _():
        for ref in (small_ref, dfc1b_ref, dhead_ref, small_head_ref):
            ref[...] = jnp.zeros_like(ref)

    rows = rows_of(b)
    weights = (mid_ref, vec_ref, w1_ref, w2_ref)
    out = mlp_forward(1, *weights, left_s.at[rows], acts_s.at[rows], slope_s)
    dout = head_backward(b, total_ref, weight_ref, out, noise_ref, tab_ref, vec_ref, dhead_ref, small_head_ref)
    mlp_backward(1, rows, dout, slope_s, *weights, dmid_ref, small_ref, dfc1b_ref, right_s, grads_s)

    @pl.when(b == pl.num_programs(0) - 1)
    def _():
        mlp_weights(c_ref, keep_ref, send_ref, left_s, right_s, grads_s, acts_s, tile_s)


def last_backward_kernel(
    layer_id,
    c_ref,
    dmid_ref,
    x_ref,
    h_ref,
    qkv_ref,
    lse_ref,
    o_ref,
    vec_ref,
    wa_ref,
    label_ref,
    d0_ref,
    latent_ref,
    dhead_ref,
    small_m0,
    small_m1,
    small_a1,
    small_head,
    dfc1b0,
    dfc1b1,
    keep_ref,
    send_ref,
    left_s,
    outs_s,
    grads_s,
    lows_s,
    dqkv_s,
    tile_s,
    small_ref,
    table_s,
):
    b = pl.program_id(0)

    @pl.when(b == 0)
    def _():
        table_s[...] = jnp.zeros_like(table_s)

    refs = (dmid_ref, x_ref, h_ref, qkv_ref, lse_ref, o_ref, vec_ref, wa_ref, small_ref, left_s, outs_s, grads_s, lows_s, dqkv_s)
    embed_grads(b, label_ref, attention_backward(layer_id, *refs) + d0_ref[0], latent_ref, table_s)

    @pl.when(b == pl.num_programs(0) - 1)
    def _():
        attention_weights(c_ref, keep_ref, send_ref, left_s, outs_s, grads_s, lows_s, tile_s)
        table_s[ROW_HEAD:ROW_VEC] = dhead_ref[...]
        row = ROW_VEC
        for own, mlp, fc1b in ((small_ref, small_m0, dfc1b0), (small_a1, small_m1, dfc1b1)):
            table_s[row : row + 2] = own[0:2]
            table_s[row + 2 : row + 4] = mlp[0:2]
            table_s[row + 4 : row + 5] = own[2:3]
            table_s[row + 5 : row + 6] = mlp[2:3]
            for i in range(FF // D):
                table_s[row + 6 + i : row + 7 + i] = fc1b[:, D * i : D * i + D]
            row += 6 + FF // D
        table_s[row : row + 2] = small_head[0:2]
        table_s[row + 2 : row + 3] = small_a1[3:4]
        table_pieces(c_ref, small_head[2:3, 0:1], table_s[...], keep_ref, send_ref, 64)


def attention_backward(
    layer_id, dmid_ref, x_ref, h_ref, qkv_ref, lse_ref, o_ref, vec_ref, wa_ref, small_ref, left_s, outs_s, grads_s, lows_s, dqkv_s
):
    b = pl.program_id(0)
    rows = rows_of(b)
    base = layer_id * (6 + FF // D)

    @pl.when(b == 0)
    def _():
        small_ref[...] = jnp.zeros_like(small_ref)

    dmid = dmid_ref[0]
    low = dmid.astype(bf16)
    left_s[rows] = h_ref[0]
    outs_s[rows] = o_ref[0]
    lows_s[rows] = low
    grad_att = dot_t(low, wa_ref[:, 3 * D :]).astype(bf16)
    scale = HD**-0.5

    def cut(part, pair):
        return qkv_ref[0, :, part * D + 128 * pair : part * D + 128 * pair + 128]

    def put(part, pair, value):
        dqkv_s[: value.shape[0], part * D + 128 * pair : part * D + 128 * pair + 128] = value.astype(bf16)

    tails, tail_douts = spread_tail(qkv_ref[0, NP:, :D], scale), spread_tail(grad_att[NP:], 1.0)
    weights = jnp.exp(mask_keys(dot_t(qkv_ref[0, :, D : 2 * D], tails)) - lse_ref[0, HEADS : HEADS + 1, :TAIL])
    grad_w = dot_t(qkv_ref[0, :, 2 * D :], tail_douts)
    grad_s = (weights * (grad_w - rows_sum(weights * grad_w))).astype(bf16)
    tail_dk = dot(grad_s, tails)
    tail_dv = dot(weights.astype(bf16), tail_douts)
    dqkv_s[NP:, :D] = (gather_tail(t_dot(grad_s, qkv_ref[0, :, D : 2 * D])) * scale).astype(bf16)

    def score(pair, _):
        queries = apart(cut(0, pair)[:NP], scale)
        douts = apart(grad_att[:NP, 128 * pair : 128 * pair + 128], 1.0)
        return dot_t(cut(1, pair), queries), dot_t(cut(2, pair), douts), queries, douts

    def weigh(pair, held):
        scores, grad_w, queries, douts = held
        log_total = jnp.concatenate([lse_ref[0, 2 * pair + e : 2 * pair + e + 1] for e in range(2)], 1)
        weights = jnp.exp(mask_keys(scores) - log_total)
        grad_s = weights * (grad_w - rows_sum(weights * grad_w))
        return weights.astype(bf16), grad_s.astype(bf16), queries, douts

    def mix(pair, held):
        weights, grad_s, queries, douts = held
        cols = slice(128 * pair, 128 * pair + 128)
        keys = apart(cut(1, pair), scale)
        put(0, pair, t_dot(grad_s[:, :NP], keys[:T]) + t_dot(grad_s[:, NP:], keys[T:]))
        put(1, pair, dot(grad_s, queries) + tail_dk[:, cols])
        put(2, pair, dot(weights, douts) + tail_dv[:, cols])

    pipelined(HEADS // 2, score, weigh, mix)
    grads_s[rows] = dqkv_s[...]
    grad_normed = dot_t(dqkv_s[...], wa_ref[:, : 3 * D])
    hat, inverse = norm_hat(x_ref[0])
    small_ref[0:1] += rows_sum(grad_normed * hat)
    small_ref[1:2] += rows_sum(grad_normed)
    small_ref[2:3] += rows_sum(dmid)
    return dmid + norm_back(hat, inverse, vec_ref[base : base + 1], grad_normed)


def attention_weights(c_ref, keep_ref, send_ref, left_s, outs_s, grads_s, lows_s, tile_s):
    tile_s[:, : 3 * D] = t_dot(left_s[...], grads_s[...]).astype(bf16)
    tile_s[:, 3 * D :] = t_dot(outs_s[...], lows_s[...]).astype(bf16)
    scatter_pieces(c_ref, keep_ref, send_ref, 0, by_columns(tile_s))


def middle_backward_kernel(
    layer_id,
    c_ref,
    dmid_ref,
    x_ref,
    h_ref,
    qkv_ref,
    lse_ref,
    o_ref,
    vec_ref,
    wa_ref,
    x1_ref,
    x0_ref,
    ws_ref,
    keep_ref,
    send_ref,
    d1_ref,
    d0_ref,
    small_ref,
    left_s,
    outs_s,
    grads_s,
    lows_s,
    dqkv_s,
    tile_s,
    both_s,
    skip_s,
    skip_tile_s,
):
    b = pl.program_id(0)
    refs = (dmid_ref, x_ref, h_ref, qkv_ref, lse_ref, o_ref, vec_ref, wa_ref, small_ref)
    grad = attention_backward(layer_id, *refs, left_s, outs_s, grads_s, lows_s, dqkv_s)
    low = grad.astype(bf16)
    small_ref[3:4] += rows_sum(grad)
    rows = rows_of(b)
    both_s[rows, :D] = x1_ref[0].astype(bf16)
    both_s[rows, D:] = x0_ref[0].astype(bf16)
    skip_s[rows] = low
    for u, dest in ((0, d1_ref), (1, d0_ref)):
        cols = slice(D * u, D * u + D)
        dest[0] = dot_t(low[:, :256], ws_ref[0, cols]) + dot_t(low[:, 256:], ws_ref[1, cols])

    @pl.when(b == pl.num_programs(0) - 1)
    def _():
        attention_weights(c_ref, keep_ref, send_ref, left_s, outs_s, grads_s, lows_s, tile_s)
        skip_tile_s[...] = t_dot(both_s[...], skip_s[...]).astype(bf16)
        for half in range(2):

            def piece(j, s, half=half):
                rows = pl.ds(pl.multiple_of(128 * s + 16 * j, 16), 16)
                return skip_tile_s[rows, 256 * half : 256 * half + 256]

            scatter_pieces(c_ref, keep_ref, send_ref, 64 + 16 * half, piece)


def embed_grads(b, label_ref, grad, latent_ref, table_s):
    table_s[:T] += grad
    patch = grad[:NP]
    last = ROW_VEC + N_VEC - 1
    table_s[last : last + 1] += rows_sum(patch)
    table_s[ROW_PATCH:ROW_CLASS] += dot(latent_ref[0], patch.astype(bf16))
    row = lax.broadcasted_iota(jnp.int32, (CLASSES, D), 0)
    table_s[ROW_CLASS:ROW_HEAD] += jnp.where(row == label_ref[b], grad[NP + 1 : NP + 2], 0.0)


def table_pieces(c_ref, loss, table, keep_ref, send_ref, at):
    x, c, z, y = coords(c_ref)
    me = (x * 2 + c) * 8 + z * 2 + y
    high = loss.astype(bf16).astype(f32)
    middle = (loss - high).astype(bf16).astype(f32)
    small = loss - high - middle
    row = lax.broadcasted_iota(jnp.int32, (ROWS, D), 0)
    kind = lax.broadcasted_iota(jnp.int32, (ROWS, D), 1) % 8
    slots = jnp.where(kind == 0, high, jnp.where(kind == 1, middle, jnp.where(kind == 2, small, 0.0)))
    turned = jnp.where(row == ROW_LOSS + me, slots, table).T
    for s in range(8):
        f, k = place_of(c_ref, s)
        for j in range(8):
            rows = slice(64 * s + 8 * j, 64 * s + 8 * j + 8)
            piece = jnp.concatenate([turned[rows, :256], turned[rows, 256:]], 0).astype(bf16)
            h, t, g = (j // 4) ^ c, j // 2 % 2, (j % 2) ^ x

            @pl.when(h == 0)
            def _(piece=piece, t=t, g=g, f=f, k=k):
                keep_ref[t, g, f, k, at : at + 16] = piece

            @pl.when(h == 1)
            def _(piece=piece, t=t, g=g, f=f, k=k):
                send_ref[t, g, f, k, at : at + 16] = piece


def per_seq(width, rows=T):
    return pl.BlockSpec((1, rows, width), lambda b: (b, 0, 0))


def fixed(shape):
    return pl.BlockSpec(shape, lambda b: (0,) * len(shape))


def shape_of(shape, dtype=f32):
    return jax.ShapeDtypeStruct(shape, dtype)


def pieces_shape(rows):
    return (2, 2, 2, 4, rows, 256)


def call_attention(order, first, n_seqs, inputs):
    shapes = [(T, D, f32), (T, D, bf16), (T, 3 * D, bf16), (LSE, NP, f32), (T, D, bf16), (T, D, f32)]
    vec_spec, wa_spec = fixed((N_VEC, D)), fixed((D, 4 * D))
    if first:
        in_specs = [SMEM, per_seq(NP, CH), per_seq(D, TAIL), fixed((ROWS, D)), vec_spec, wa_spec]
    else:
        in_specs = [per_seq(D), per_seq(D), fixed((2, 2 * D, D // 2)), vec_spec, wa_spec]
    return order(
        embed_attention_kernel if first else skip_attention_kernel,
        inputs,
        in_specs,
        [shape_of((n_seqs, r, w), d) for r, w, d in shapes],
        [per_seq(w, r) for r, w, _ in shapes],
        grid=(n_seqs,),
        name="attention_forward_%d" % (0 if first else 1),
    )


def flat(width):
    return pl.BlockSpec((T, width), lambda b: (b, 0))


def call_mlp(order, layer_id, n_seqs, mid, vec, w1, w2):
    shapes = [(D, bf16), (FF, bf16), (FF, bf16), (D, f32)]
    whole = n_seqs * T
    out = order(
        functools.partial(mlp_kernel, layer_id),
        [mid.reshape(whole, D), vec, w1, w2],
        [flat(D), fixed((N_VEC, D)), fixed((D, FF)), fixed((2, FF, D // 2))],
        [shape_of((whole, w), d) for w, d in shapes],
        [flat(w) for w, _ in shapes],
        grid=(n_seqs,),
        name="mlp_forward_%d" % layer_id,
    )
    return [*out[:3], out[3].reshape(n_seqs, T, D)]


def mlp_backward_outs(n_seqs):
    whole = n_seqs * T
    pieces = pieces_shape(128)
    outs = [shape_of((whole, D)), shape_of(pieces, bf16), shape_of(pieces, bf16), shape_of((8, D)), shape_of((1, FF))]
    out_specs = [flat(D), fixed(pieces), fixed(pieces), fixed((8, D)), fixed((1, FF))]
    scratch = [
        pltpu.VMEM((whole, D), bf16),
        pltpu.VMEM((whole, D), bf16),
        pltpu.VMEM((whole, FF), bf16),
        pltpu.VMEM((whole, FF), bf16),
        pltpu.VMEM((D, FF), bf16),
    ]
    return outs, out_specs, scratch


def call_mlp_backward(order, layer_id, n_seqs, place, dout, act, slope, normed, mid, vec, w1, w2):
    whole = n_seqs * T
    outs, out_specs, scratch = mlp_backward_outs(n_seqs)
    out = order(
        functools.partial(mlp_backward_kernel, layer_id),
        (place, dout.reshape(whole, D), act, slope, normed, mid.reshape(whole, D), vec, w1, w2),
        [SMEM, flat(D), flat(FF), flat(FF), flat(D), flat(D)]
        + [fixed((N_VEC, D)), fixed((D, FF)), fixed((2, FF, D // 2))],
        outs,
        out_specs,
        scratch,
        grid=(n_seqs,),
        name="mlp_backward_%d" % layer_id,
    )
    return [out[0].reshape(n_seqs, T, D), *out[1:]]


def call_mlp_turn(order, n_seqs, total, weights, place, mid, vec, w1, w2, noise, tab):
    whole = n_seqs * T
    outs, out_specs, scratch = mlp_backward_outs(n_seqs)
    out = order(
        mlp_turn_kernel,
        (total, weights, place, mid.reshape(whole, D), vec, w1, w2, noise, tab),
        [SMEM, SMEM, SMEM, flat(D), fixed((N_VEC, D)), fixed((D, FF)), fixed((2, FF, D // 2))]
        + [per_seq(NP, CH), fixed((ROWS, D))],
        outs + [shape_of((CH, D)), shape_of((8, D))],
        out_specs + [fixed((CH, D)), fixed((8, D))],
        scratch + [pltpu.VMEM((T, FF), bf16)],
        grid=(n_seqs,),
        name="mlp_turn",
    )
    return [out[0].reshape(n_seqs, T, D), *out[1:]]


def call_attention_backward(order, layer_id, n_seqs, place, dmid, x, normed, qkv, lse, att, vec, wa, more):
    whole = n_seqs * T
    pieces = pieces_shape(80 if layer_id == 0 else 96)
    specs = [SMEM, per_seq(D), per_seq(D), per_seq(D), per_seq(3 * D), per_seq(NP, LSE), per_seq(D)]
    specs += [fixed((N_VEC, D)), fixed((D, 4 * D))]
    scratch = [
        pltpu.VMEM((whole, D), bf16),
        pltpu.VMEM((whole, D), bf16),
        pltpu.VMEM((whole, 3 * D), bf16),
        pltpu.VMEM((whole, D), bf16),
        pltpu.VMEM((T, 3 * D), bf16),
        pltpu.VMEM((D, 4 * D), bf16),
    ]
    if layer_id == 1:
        kernel = middle_backward_kernel
        specs += [per_seq(D), per_seq(D), fixed((2, 2 * D, D // 2))]
        outs = [shape_of((n_seqs, T, D)), shape_of((n_seqs, T, D)), shape_of((8, D))]
        out_specs = [per_seq(D), per_seq(D), fixed((8, D))]
        scratch += [pltpu.VMEM((whole, 2 * D), bf16), pltpu.VMEM((whole, D), bf16), pltpu.VMEM((2 * D, D), bf16)]
    else:
        kernel = last_backward_kernel
        specs += [SMEM, per_seq(D), per_seq(NP, CH), fixed((CH, D))] + [fixed((8, D))] * 4 + [fixed((1, FF))] * 2
        scratch += [pltpu.VMEM((8, D), f32), pltpu.VMEM((ROWS, D), f32)]
        outs, out_specs = [], []
    return order(
        functools.partial(kernel, layer_id),
        [place, dmid, x, normed, qkv, lse, att, vec, wa, *more],
        specs,
        [shape_of(pieces, bf16), shape_of(pieces, bf16)] + outs,
        [fixed(pieces), fixed(pieces)] + out_specs,
        scratch,
        grid=(n_seqs,),
        name="attention_backward_%d" % layer_id,
    )


def device_id(x, c, z, y):
    return (x * 2 + c) * 8 + z * 2 + y


def pairs(move):
    every = [(x, c, z, y) for x in range(2) for c in range(2) for z in range(4) for y in range(2)]
    return [(device_id(*at), device_id(*move(*at))) for at in every]


TO_CORE = pairs(lambda x, c, z, y: (x, 1 - c, z, y))
TO_X = pairs(lambda x, c, z, y: (1 - x, c, z, y))
TO_Y = pairs(lambda x, c, z, y: (x, c, z, 1 - y))
TO_Z = [pairs(lambda x, c, z, y, k=k: (x, c, (z + k) % 4, y)) for k in range(4)]
PIECE_ROWS = {"a": 64, "m": 128, "s": 32, "t": 16}


def send(value, to):
    return lax.ppermute(value, ALL, to)


def rows_in(kinds):
    return sum(PIECE_ROWS[kind[0]] for kind in kinds)


def pack_kernel(kinds, c_ref, mats_ref, down_ref, skip_ref, tab_ref, vec_ref, weight_ref, u_ref, wide_s, narrow_s, sem):
    x, c, _, _ = coords(c_ref)
    copies, casts = [], []
    wide = narrow = row = 0
    for kind in kinds:
        l = int(kind[1:] or 0)
        if kind[0] in "am":
            for t in range(2):
                start = (2048 if kind[0] == "m" else 0) + 256 * (4 * c + 2 * t + x)
                copies.append((mats_ref.at[l, :, pl.ds(pl.multiple_of(start, 256), 256)], wide_s.at[wide]))
                casts.append((t, row, wide_s.at[wide], None))
                wide += 1
            row += 64
        if kind[0] in "ms":
            size = 32 if kind[0] == "m" else 16
            ref = down_ref.at[l] if kind[0] == "m" else skip_ref
            for t in range(2):
                start = pl.multiple_of(size * (4 * c + 2 * t + x), size)
                copies.append((ref.at[pl.ds(start, size)], narrow_s.at[narrow, :size]))
                for half in range(2):
                    cols = slice(256 * half, 256 * half + 256)
                    casts.append((t, row + size * half, narrow_s.at[narrow, :size], cols))
                narrow += 1
            row += 2 * size
        if kind[0] == "t":
            own_weight = weight_ref[0]
            for i in range(1, weight_ref.shape[0]):
                own_weight += weight_ref[i]
            turned = vec_ref[...].T
            first, last = CH + CLASSES, CH + CLASSES + SEQ_LEN
            corner = (lax.broadcasted_iota(jnp.int32, (16, 256), 0) == 8) & (
                lax.broadcasted_iota(jnp.int32, (16, 256), 1) == 255
            )
            for t in range(2):
                j = 4 * c + 2 * t + x
                table = tab_ref[pl.ds(pl.multiple_of(8 * j, 8), 8)]
                vecs = turned[0:8]
                for i in range(1, 8):
                    vecs = jnp.where(j == i, turned[8 * i : 8 * i + 8], vecs)
                rest = [
                    table[:, first : first + 2],
                    jnp.zeros((8, TAIL - 2), f32),
                    table[:, :first],
                    table[:, last:],
                    vecs,
                    jnp.zeros((8, ROWS - ROW_VEC - N_VEC), f32),
                ]
                piece = jnp.concatenate([table[:, first + 2 : last], jnp.concatenate(rest, 1)], 0)
                if t == 0:
                    piece = jnp.where(corner, own_weight.astype(f32), piece)
                u_ref[t, row : row + 16] = piece.astype(bf16)
            row += 16
    copies = [pltpu.make_async_copy(a, b, sem) for a, b in copies]
    for copy in copies:
        copy.start()
    yield
    for copy in copies:
        copy.wait()
    for t, at, ref, cols in casts:
        value = ref[...] if cols is None else ref[:, cols]
        u_ref[t, at : at + value.shape[0]] = value.astype(bf16)


def join_ring_kernel(u0, u1, u2, u3, b_ref, c_ref):
    for k, ref in enumerate((u0, u1, u2, u3)):
        b_ref[k] = ref[0]
        c_ref[k] = ref[1]


def join_pair_kernel(b0, b1, c0, c1, b_ref, c_ref):
    for i, (b, c) in enumerate(((b0, c0), (b1, c1))):
        b_ref[i] = b[...]
        c_ref[i] = c[...]


def join_own_kernel(b, c, both_ref):
    both_ref[0] = b[...]
    both_ref[1] = c[...]


def assemble_kernel(kinds, c_ref, *refs):
    x, c, z, y = coords(c_ref)
    sources, dests = refs[:6], refs[6:]
    for h in range(2):
        if h == 0:
            own_b, x_b, own_c, y_c = sources[:4]
        else:
            own_b, own_c, x_b, y_c = (sources[4 + i].at[k] for i in range(2) for k in range(2))
        for t in range(2):
            for g in range(2):
                j = 4 * (c ^ h) + 2 * t + (g ^ x)
                cols = pl.ds(pl.multiple_of(256 * j, 256), 256)
                for f in range(2):
                    src = ((own_b, x_b)[g].at[f]) if t == 0 else ((own_c, y_c)[f].at[g])
                    for k in range(4):
                        s = 2 * ((z - k) & 3) + (y ^ f)
                        row = 0
                        at = 0
                        for kind in kinds:
                            if kind[0] in "am":
                                rows = pl.ds(pl.multiple_of(64 * s, 64), 64)
                                dests[at][rows, cols] = src[k, row : row + 64]
                                row, at = row + 64, at + 1
                            if kind[0] in "ms":
                                size = 32 if kind[0] == "m" else 16
                                rows = pl.ds(pl.multiple_of(size * (8 * s + j), size), size)
                                for half in range(2):
                                    dests[at][half, rows] = src[k, row : row + size]
                                    row += size
                                at += 1
                            if kind[0] == "t":
                                both = src[k, row : row + 16].astype(f32)
                                rows = pl.ds(pl.multiple_of(64 * s + 8 * j, 8), 8)
                                dests[-1][rows, :256] = both[:8]
                                dests[-1][rows, 256:] = both[8:]
    if "t" in kinds:
        table_ref, vec_ref, total_ref, turned_s = dests[-4:]
        table = turned_s[...].T
        table_ref[...] = table.astype(bf16)
        vec_ref[...] = table[ROW_VEC : ROW_VEC + N_VEC]
        total_ref[0, 0] = jnp.sum(table[ROW_WEIGHT : ROW_WEIGHT + 1])


def assemble_all_kernel(kinds, source, *dests):
    for x in range(2):
        for c in range(2):
            for s in range(8):
                for t in range(2):
                    j = 4 * c + 2 * t + x
                    src = source.at[8 * (2 * x + c) + s, t]
                    row = at = 0
                    for kind in kinds:
                        if kind[0] in "am":
                            dests[at][64 * s : 64 * s + 64, 256 * j : 256 * j + 256] = src[row : row + 64]
                            row, at = row + 64, at + 1
                        if kind[0] in "ms":
                            size = 32 if kind[0] == "m" else 16
                            for half in range(2):
                                start = size * (8 * s + j)
                                dests[at][half, start : start + size] = src[row : row + size]
                                row += size
                            at += 1


class Gather:
    def __init__(self, place, kinds, sources):
        self.place, self.kinds, self.sources = place, kinds, sources
        self.rows = rows_in(kinds)

    def pack(self):
        return Part(
            functools.partial(pack_kernel, self.kinds),
            (self.place, *self.sources),
            [SMEM, ANY, ANY, ANY] + ([WHOLE, WHOLE, SMEM] if "t" in self.kinds else [ANY] * 3),
            [shape_of((2, self.rows, 256), bf16)],
            [WHOLE],
            [pltpu.VMEM((4, 64, 256), f32), pltpu.VMEM((4, 32, D), f32), pltpu.SemaphoreType.DMA],
        )

    def packed_for_all(self, results):
        self.every = lax.all_gather(results[0], ALL)

    def assemble_all(self):
        shapes = self.shapes()
        return Part(
            functools.partial(assemble_all_kernel, self.kinds), [self.every], [WHOLE], shapes, [WHOLE] * len(shapes)
        )

    def packed(self, results):
        (own,) = results
        self.ring = [own] + [send(own, TO_Z[k]) for k in range(1, 4)]

    def join_ring(self):
        half = shape_of((4, self.rows, 256), bf16)
        return Part(join_ring_kernel, self.ring, [WHOLE] * 4, [half] * 2, [WHOLE] * 2)

    def ring_joined(self, results):
        b, c = results
        self.halves = (b, send(b, TO_Y), c, send(c, TO_X))

    def join_pair(self):
        whole = shape_of((2, 4, self.rows, 256), bf16)
        return Part(join_pair_kernel, self.halves, [WHOLE] * 4, [whole, whole], [WHOLE] * 2)

    def pair_joined(self, results):
        b, c = results
        self.mine = [b, send(b, TO_X), c, send(c, TO_Y)]

    def join_own(self):
        both = shape_of((2, 2, 4, self.rows, 256), bf16)
        return Part(join_own_kernel, (self.mine[0], self.mine[2]), [WHOLE] * 2, [both], [WHOLE])

    def own_joined(self, results):
        self.other = [send(results[0], TO_CORE)]

    def join_rest(self):
        both = shape_of((2, 2, 4, self.rows, 256), bf16)
        return Part(join_own_kernel, (self.mine[1], self.mine[3]), [WHOLE] * 2, [both], [WHOLE])

    def rest_joined(self, results):
        self.other.append(send(results[0], TO_CORE))

    def shapes(self):
        shapes = []
        for kind in self.kinds:
            if kind[0] in "am":
                shapes.append(shape_of((D, 2048), bf16))
            if kind[0] == "m":
                shapes.append(shape_of((2, FF, 256), bf16))
            if kind[0] == "s":
                shapes.append(shape_of((2, 2 * D, 256), bf16))
            if kind[0] == "t":
                shapes += [shape_of((ROWS, D), bf16), shape_of((N_VEC, D)), shape_of((1, 1))]
        return shapes

    def assemble(self):
        shapes = self.shapes()
        scratch = [pltpu.VMEM((D, ROWS), f32)] if "t" in self.kinds else []
        return Part(
            functools.partial(assemble_kernel, self.kinds),
            (self.place, *self.mine, *self.other),
            [SMEM] + [WHOLE] * 6,
            shapes,
            [SMEM if shape.shape == (1, 1) else WHOLE for shape in shapes],
            scratch,
        )


def added(*values):
    total = values[0].astype(f32)
    for value in values[1:]:
        total += value.astype(f32)
    return total.astype(bf16)


def add_core_kernel(n, *refs):
    keeps, gots, (b0_ref, b1_ref, c0_ref, c1_ref) = refs[:n], refs[n : 2 * n], refs[2 * n :]
    row = 0
    for keep, got in zip(keeps, gots):
        rows = slice(row, row + keep.shape[4])
        row = rows.stop
        for i in range(2):
            for dest, at in ((b0_ref, (0, 0, i)), (b1_ref, (0, 1, i)), (c0_ref, (1, i, 0)), (c1_ref, (1, i, 1))):
                dest[i, :, rows] = added(keep[at], got[at])


def add_both_kernel(b0_ref, gb_ref, c0_ref, gc_ref, b_ref, sb_ref, c_ref, sc_ref):
    for keep, got, dests in ((b0_ref, gb_ref, (b_ref, sb_ref)), (c0_ref, gc_ref, (c_ref, sc_ref))):
        for i, dest in enumerate(dests):
            dest[...] = added(keep[i], got[i])


def add_ring_kernel(b_ref, gb_ref, c_ref, gc_ref, *dests):
    for t, (keep, got) in enumerate(((b_ref, gb_ref), (c_ref, gc_ref))):
        for k, dest in enumerate(dests):
            dest[t] = added(keep[k], got[k])


def add_last_kernel(*refs):
    row = 0
    for i in range(0, len(refs) - 1, 4):
        rows = slice(row, row + refs[i].shape[1])
        row = rows.stop
        refs[-1][:, rows] = added(*(ref[...] for ref in refs[i : i + 4]))


class Reduce:
    def __init__(self, kinds):
        self.kinds = kinds
        self.rows = rows_in(kinds)
        self.keep, self.got = [], []

    def start(self, keep, give):
        self.keep.append(keep)
        self.got.append(send(give, TO_CORE))

    def core(self):
        def six(rows):
            return pl.BlockSpec((2, 2, 2, 1, rows, 256), lambda k: (0, 0, 0, k, 0, 0))

        four = pl.BlockSpec((2, 1, self.rows, 256), lambda k: (0, k, 0, 0))
        parts = self.keep + self.got
        return Part(
            functools.partial(add_core_kernel, len(self.keep)),
            parts,
            [six(part.shape[4]) for part in parts],
            [shape_of((2, 4, self.rows, 256), bf16)] * 4,
            [four] * 4,
        )

    def core_added(self, results):
        b0, b1, c0, c1 = results
        self.parts = (b0, send(b1, TO_X), c0, send(c1, TO_Y))

    def both(self):
        four = pl.BlockSpec((2, 1, self.rows, 256), lambda k: (0, k, 0, 0))
        three = pl.BlockSpec((1, self.rows, 256), lambda k: (k, 0, 0))
        return Part(
            add_both_kernel, self.parts, [four] * 4, [shape_of((4, self.rows, 256), bf16)] * 4, [three] * 4
        )

    def both_added(self, results):
        b, sb, c, sc = results
        self.parts = (b, send(sb, TO_Y), c, send(sc, TO_X))

    def ring(self):
        small = shape_of((2, self.rows, 256), bf16)
        return Part(add_ring_kernel, self.parts, [WHOLE] * 4, [small] * 4, [WHOLE] * 4)

    def ring_added(self, results):
        self.parts = [results[0]] + [send(results[k], TO_Z[k]) for k in range(1, 4)]


class Owned:
    def __init__(self, *chunks):
        self.chunks = chunks
        self.kinds = [kind for chunk in chunks for kind in chunk.kinds]

    def last(self):
        parts = [part for chunk in self.chunks for part in chunk.parts]
        out = shape_of((2, rows_in(self.kinds), 256), bf16)
        return Part(add_last_kernel, parts, [WHOLE] * len(parts), [out], [WHOLE])

    def last_added(self, results):
        (mine,) = results
        near = send(mine, TO_X)
        self.parts = (mine, near, send(mine, TO_CORE), send(near, TO_CORE))

    def adam(self, order, place, states, bufs, name):
        inputs, in_specs, outs, out_specs, aliases = [place, *self.parts], [SMEM] + [WHOLE] * 4, [], [], {}
        targets = []
        for kind in self.kinds:
            l = int(kind[1:] or 0)
            if kind[0] == "a":
                targets.append(("mats", "a", pl.BlockSpec((1, 64, 4096), lambda i, l=l: (l, 0, 0))))
            if kind[0] == "m":
                targets.append(("down", "d", pl.BlockSpec((1, 256, D), lambda i, l=l: (l, 0, 0))))
            if kind[0] == "s":
                targets.append(("skip", "s", fixed((128, D))))
            if kind[0] == "t":
                targets.append(("tables", "t", fixed((64, SEQ_LEN + 3 * CH))))
                targets.append(("vectors", "v", fixed((N_VEC, 64))))
        held = []
        for name, _, spec in targets:
            inputs += list(states[name])
            in_specs += [spec] * 3
            weight = states[name][0]
            if bufs.get(name) is not None:
                held += [(len(outs) + i, buf) for i, buf in enumerate(bufs[name])]
            outs += [shape_of(weight.shape)] * 3 + [shape_of(weight.shape, bf16)]
            out_specs += [spec] * 4
        n_read = len(inputs)
        for at, buf in held:
            aliases[len(inputs)] = at
            inputs.append(buf)
            in_specs.append(ANY)
        scratch = []
        if any(t[1] == "d" for t in targets):
            scratch.append(pltpu.VMEM((D, 256), f32))
        if any(t[1] == "t" for t in targets):
            scratch.append(pltpu.VMEM((64, ROWS), f32))
            outs.append(shape_of((1, 1)))
            out_specs.append(SMEM)
        result = order(
            functools.partial(adam_kernel, self.kinds, [t[1] for t in targets], n_read, len(inputs)),
            inputs,
            in_specs,
            outs,
            out_specs,
            scratch,
            name=name,
            aliases=aliases,
        )
        for i, (name, _, _) in enumerate(targets):
            bufs[name] = result[4 * i : 4 * i + 4]
        return result[4 * len(targets) :]


def adam_kernel(kinds, targets, n_read, n_in, c_ref, *refs):
    x, c, _, _ = coords(c_ref)
    parts, ins, outs = refs[:4], refs[4 : n_read - 1], refs[n_in - 1 :]
    scratch = list(outs[4 * len(targets) :])
    loss_ref = scratch.pop(0) if "t" in targets else None
    offsets, row = {}, 0
    for kind in kinds:
        offsets[kind[0]] = row
        row += PIECE_ROWS[kind[0]]
    pieces = []
    for h in range(2):
        for g in range(2):
            for t in range(2):
                pieces.append((4 * (c ^ h) + 2 * t + (g ^ x), parts[2 * h + g].at[t]))
    for i, kind in enumerate(targets):
        state, dests = ins[3 * i : 3 * i + 3], outs[4 * i : 4 * i + 4]
        row = offsets[{"d": "m", "v": "t"}.get(kind, kind)]

        def update(at, grad, rate, state=state, dests=dests):
            weight, first, second = (ref[at] for ref in state)
            values = adam_update(weight, grad, first, second, rate)
            for dest, value in zip(dests, values):
                dest[at] = value

        if kind == "a":
            for at_row, start in ((row, 0), (offsets["m"], 2048)):
                for j, piece in pieces:
                    at = (0, slice(None), pl.ds(pl.multiple_of(start + 256 * j, 256), 256))
                    update(at, piece[at_row : at_row + 64], step_rates[0])
        if kind == "d":
            held = scratch[0]
            for j, piece in pieces:
                held[pl.ds(pl.multiple_of(64 * j, 64), 64)] = piece[row + 64 : row + 128].astype(f32)
            update((0,), held[...].T, step_rates[1])
        if kind == "s":
            for j, piece in pieces:
                for half in range(2):
                    at = (pl.ds(pl.multiple_of(16 * j, 16), 16), slice(256 * half, 256 * half + 256))
                    update(at, piece[row + 16 * half : row + 16 * half + 16], step_rates[2])
        if kind == "t":
            held = scratch[-1]
            for j, piece in pieces:
                both = piece[row : row + 16].astype(f32)
                rows = pl.ds(pl.multiple_of(8 * j, 8), 8)
                held[rows, :256] = both[:8]
                held[rows, 256:] = both[8:]
            grad = held[...]
            parts_of = [grad[:, ROW_PATCH:ROW_HEAD], grad[:, NP : NP + 2], grad[:, :NP], grad[:, ROW_HEAD:ROW_VEC]]
            update(slice(None), jnp.concatenate(parts_of, 1), step_rates[3])
            loss_ref[0, 0] = jnp.sum(grad[0:3, ROW_LOSS : ROW_LOSS + 32])
        if kind == "v":
            grad = scratch[-1][:, ROW_VEC : ROW_VEC + N_VEC].T
            update(slice(None), grad, step_rates[4])


def gather_any(mats, down, skip, tables, vectors):
    first, last = CH + CLASSES, CH + CLASSES + SEQ_LEN
    width = tables.shape[1]
    tab = jnp.concatenate(
        [
            tables[first + 2 : last],
            tables[first : first + 2],
            jnp.zeros((TAIL - 2, width), f32),
            tables[:first],
            tables[last:],
            vectors,
            jnp.zeros((ROWS - ROW_VEC - N_VEC, width), f32),
        ]
    )
    every = lax.all_gather(mats.astype(bf16), "shard", axis=1, tiled=True)
    downs = lax.all_gather(down.astype(bf16), "shard", axis=1, tiled=True)
    skips = lax.all_gather(skip.astype(bf16), "shard", axis=0, tiled=True)
    table = lax.all_gather(tab.astype(bf16), "shard", axis=1, tiled=True)

    def halves(m):
        return jnp.stack([m[:, : D // 2], m[:, D // 2 :]])

    mats_of = [(every[l, :, :2048], every[l, :, 2048:]) for l in range(LAYERS)]
    return (mats_of, [halves(downs[l]) for l in range(LAYERS)], halves(skips), table)


def reduce_any(grads):
    def ordered(kind):
        both = jnp.stack(grads[kind])
        return both.transpose(0, 1, 2, 4, 3, 5, 6).reshape((8, 8) + both.shape[5:])

    def shard_sum(value, axis):
        owned = lax.psum_scatter(value.astype(f32), "shard", scatter_dimension=axis, tiled=True)
        return lax.psum(owned.astype(bf16), "rep")

    mats, down = [], []
    for l in range(LAYERS):
        attn, mlp = ordered("a%d" % l), ordered("m%d" % l)
        both = [part[:, :, :64].transpose(1, 2, 0, 3).reshape(D, 2048) for part in (attn, mlp)]
        mats.append(jnp.concatenate(both, 1))
        down.append(mlp[:, :, 64:].transpose(0, 2, 1, 3).reshape(D, FF).T)
    skip = ordered("a1")[:, :, 64:].reshape(8, 8, 2, 16, 256).transpose(1, 0, 3, 2, 4).reshape(2 * D, D)
    turned = ordered("a0")[:, :, 64:].reshape(8, 8, 2, 8, 256).transpose(1, 0, 3, 2, 4).reshape(D, ROWS)
    return (shard_sum(jnp.stack(mats), 1), shard_sum(jnp.stack(down), 1), shard_sum(skip, 0), shard_sum(turned, 0))


def time_token(timesteps):
    half_width = D // 2
    freqs_row = jnp.exp(-math.log(10000.0) * jnp.arange(half_width, dtype=f32) / half_width)
    angles = timesteps.astype(f32)[:, None] * freqs_row[None, :]
    return jnp.concatenate([jnp.cos(angles), jnp.sin(angles)], -1)


def adam_update(weight, grad, moment_one, moment_two, step_rate):
    grad = grad.astype(f32)
    moment_one = beta_one * moment_one + (1.0 - beta_one) * grad
    moment_two = beta_two * moment_two + (1.0 - beta_two) * grad * grad
    first_hat = moment_one / (1.0 - beta_one**STEP)
    second_hat = moment_two / (1.0 - beta_two**STEP)
    weight = weight - step_rate * (first_hat / (jnp.sqrt(second_hat) + epsilon) + weight_decay * weight)
    return (moment_one, moment_two, weight, weight.astype(bf16))


def local(
    fast,
    latents,
    target_noise,
    labels,
    timesteps,
    loss_weight,
    layer_mats,
    layer_mats_first,
    layer_mats_second,
    down_mats,
    down_first,
    down_second,
    skip_mat,
    skip_first,
    skip_second,
    tables,
    tables_first,
    tables_second,
    vectors,
    vectors_first,
    vectors_second,
):
    n_seqs = latents.shape[0]
    if fast:
        rep, shard = lax.axis_index("rep"), lax.axis_index("shard")
        place = jnp.stack([rep // 2, rep % 2, shard // 2, shard % 2]).astype(jnp.int32)
    else:
        place = jnp.zeros((4,), jnp.int32)
    order = Order()
    time_rows = jnp.pad(time_token(timesteps)[:, None], ((0, 0), (0, TAIL - 1), (0, 0)))
    mats, downs = [None, None], [None, None]
    forward = {}

    def attention(l):
        if l == 0:
            inputs = (labels, latents, time_rows, table, vec, mats[0][0])
        else:
            inputs = (forward["x1"], forward["x0"], ws, vec, mats[1][0])
        forward["a%d" % l] = call_attention(order, l == 0, n_seqs, inputs)
        if l == 0:
            forward["x0"] = forward["a0"][0]

    def mlp():
        out = call_mlp(order, 0, n_seqs, forward["a0"][5], vec, mats[0][1], downs[0])
        forward["m0"] = out
        forward["x1"] = out[3]

    if fast:
        args = (layer_mats, down_mats, skip_mat, tables.T, vectors, loss_weight)
        one, two, three = (Gather(place, kinds, args) for kinds in GATHER_CHUNKS)
        one.packed(*order.fuse([one.pack()], "pack_0"))
        joined, packed = order.fuse([one.join_ring(), two.pack()], "join_ring_0")
        one.ring_joined(joined)
        two.packed(packed)
        one.pair_joined(*order.fuse([one.join_pair()], "join_pair_0"))
        joined, own = order.fuse([two.join_ring(), one.join_own()], "join_ring_1")
        two.ring_joined(joined)
        one.own_joined(own)
        one.rest_joined(*order.fuse([one.join_rest()], "join_rest_0"))
        (wa0, table, vec, weight_total), packed = order.fuse([one.assemble(), three.pack()], "assemble_0")
        mats[0] = (wa0, None)
        three.packed(packed)
        two.pair_joined(*order.fuse([two.join_pair()], "join_pair_1"))
        attention(0)
        joined, own = order.fuse([three.join_ring(), two.join_own()], "join_ring_2")
        three.ring_joined(joined)
        two.own_joined(own)
        two.rest_joined(*order.fuse([two.join_rest()], "join_rest_1"))
        ((w10, downs[0], ws),) = order.fuse([two.assemble()], "assemble_1")
        mats[0] = (wa0, w10)
        three.pair_joined(*order.fuse([three.join_pair()], "join_pair_2"))
        mlp()
        three.own_joined(*order.fuse([three.join_own()], "join_own_2"))
        three.rest_joined(*order.fuse([three.join_rest()], "join_rest_2"))
        ((wa1, w11, downs[1]),) = order.fuse([three.assemble()], "assemble_2")
        mats[1] = (wa1, w11)
        attention(1)
    else:
        mats, downs, ws, table = gather_any(layer_mats, down_mats, skip_mat, tables, vectors)
        vec = table[ROW_VEC : ROW_VEC + N_VEC].astype(f32)
        weight_total = lax.psum(jnp.sum(loss_weight.astype(f32)), ALL).reshape(1, 1)
        attention(0)
        mlp()
        attention(1)

    grads, small = {}, {}

    def mlp_turn():
        mid = forward["a1"][5]
        out = call_mlp_turn(
            order, n_seqs, weight_total, loss_weight, place, mid, vec, mats[1][1], downs[1], target_noise, table
        )
        grads["m1"], small["m1"], small["f1"] = out[1:3], out[3], out[4]
        return out[0], out[5], out[6]

    def mlp_back(dout):
        normed, act, slope = forward["m0"][:3]
        out = call_mlp_backward(
            order, 0, n_seqs, place, dout, act, slope, normed, forward["a0"][5], vec, mats[0][1], downs[0]
        )
        grads["m0"], small["m0"], small["f0"] = out[1:3], out[3], out[4]
        return out[0]

    def attention_back(l, dmid, more):
        x, normed, qkv, lse, att, _ = forward["a%d" % l]
        out = call_attention_backward(order, l, n_seqs, place, dmid, x, normed, qkv, lse, att, vec, mats[l][0], more)
        grads["a%d" % l] = out[:2]
        return out[2:]

    bufs = {}
    if fast:
        first, second, third = (Reduce(kinds) for kinds in REDUCE_CHUNKS)
        states = {
            "mats": (layer_mats, layer_mats_first, layer_mats_second),
            "down": (down_mats, down_first, down_second),
            "skip": (skip_mat, skip_first, skip_second),
            "tables": (tables.T, tables_first.T, tables_second.T),
            "vectors": (vectors, vectors_first, vectors_second),
        }
    dmid, dhead, small_head = mlp_turn()
    if fast:
        first.start(*grads["m1"])
    dx, d0, small["a1"] = attention_back(1, dmid, (forward["x1"], forward["x0"], ws))
    if fast:
        first.start(*grads["a1"])
        first.core_added(*order.fuse([first.core()], "add_core_1", grid=(4,)))
    dmid = mlp_back(dx)
    if fast:
        second.start(*grads["m0"])
        both, core = order.fuse([first.both(), second.core()], "add_both_1", grid=(4,))
        first.both_added(both)
        second.core_added(core)
    last = (labels, d0, latents, dhead, small["m0"], small["m1"], small["a1"], small_head, small["f0"], small["f1"])
    attention_back(0, dmid, last)
    if fast:
        upper, lower = Owned(first), Owned(second, third)
        third.start(*grads["a0"])
        first.ring_added(*order.fuse([first.ring()], "add_ring_1"))
        both, core = order.fuse([second.both(), third.core()], "add_both_2", grid=(4,))
        second.both_added(both)
        third.core_added(core)
        second.ring_added(*order.fuse([second.ring()], "add_ring_2"))
        upper.last_added(*order.fuse([upper.last()], "add_last_1"))
        third.both_added(*order.fuse([third.both()], "add_both_3", grid=(4,)))
        third.ring_added(*order.fuse([third.ring()], "add_ring_3"))
        upper.adam(order, place, states, bufs, "adam_1")
        lower.last_added(*order.fuse([lower.last()], "add_last_0"))
        (loss,) = lower.adam(order, place, states, bufs, "adam_0")
        loss_sum = loss[0, 0]
        results = [bufs[name] for name in ("mats", "down", "skip", "tables", "vectors")]
        results[3] = [part.T for part in results[3]]
    else:
        loss_sum = lax.psum(small_head[2, 0], ALL)
        g_mats, g_down, g_skip, g_turned = reduce_any(grads)
        g_rows = g_turned.T
        g_tables = jnp.concatenate(
            [g_rows[ROW_PATCH:ROW_HEAD], g_rows[NP : NP + 2], g_rows[:NP], g_rows[ROW_HEAD:ROW_VEC]]
        )
        g_vectors = g_rows[ROW_VEC : ROW_VEC + N_VEC]
        results = [
            adam_update(layer_mats, g_mats, layer_mats_first, layer_mats_second, step_rates[0]),
            adam_update(down_mats, g_down, down_first, down_second, step_rates[1]),
            adam_update(skip_mat, g_skip, skip_first, skip_second, step_rates[2]),
            adam_update(tables, g_tables, tables_first, tables_second, step_rates[3]),
            adam_update(vectors, g_vectors, vectors_first, vectors_second, step_rates[4]),
        ]
    return (loss_sum, weight_total[0, 0], *(part for result in results for part in result))


GATHER_CHUNKS = (("a0", "t"), ("m0", "s"), ("a1", "m1"))
REDUCE_CHUNKS = (("m1", "a1", "s"), ("m0",), ("a0", "t"))


def solution(mesh):
    one, two, rows = P(None, "shard", None), P("shard", None), P(None, "shard")
    every = P(ALL, None, None)
    placed = (every, every, P(ALL), P(ALL), P(ALL), *[one] * 6, *[two] * 3, *[rows] * 6)
    fast = mesh.shape["rep"] == 4 and mesh.shape["shard"] == 8
    return jax.shard_map(
        functools.partial(local, fast),
        mesh=mesh,
        in_specs=placed,
        out_specs=(P(), P(), *[one] * 8, *[two] * 4, *[rows] * 8),
        check_vma=False,
    )
```
